256 devices in a mesh: band: 64 (over y, z, core), rep: 4 (over x).
Axes of the slice: x: 4, y: 4, z: 8, core: 2. Of those that a mesh axis runs over, the one named last changes fastest.
Arguments:
- embeddings: bfloat16 [128, 32768], P('rep', 'band'), may hold values from -6 to 6
- route: int32 [32768, 1], P('band'), may hold values from 0 to 63; in each aligned block of 512 rows (0 to 511, 512 to 1023, ...) at most 20 rows name the same one
- place: bfloat16 [2, 32768], P(None, 'band'), may hold values from 0 to 1
- scales: float32 [4], replicated, may hold values from 0.25 to 1
- first_weight: bfloat16 [512, 512], replicated, may hold values from -0.25 to 0.25
- first_bias: float32 [512], replicated, may hold values from -3 to 3
- second_weight: bfloat16 [512, 512], replicated, may hold values from -0.25 to 0.25
- out_cotangent: bfloat16 [512, 768, 256], P(None, ('band', 'rep')), may hold values from -6 to 6
Outputs:
- embed_gradient: float32 [128, 32768], P('rep', 'band')
- first_weight_gradient: float32 [512, 512], replicated
- first_bias_gradient: float32 [512], replicated
- second_weight_gradient: float32 [512, 512], replicated
The draws below stay inside these ranges and needn't reach their ends.
Inputs may be any that keep to these rules, and one draw needn't show every extreme that they name: `route`: within the 512 reports of one feed (aligned blocks of rows), at most 20 name the same band, and in some block exactly 20 do.
All inputs are finite; a program needn't handle non-finite values.
Results may differ from the reference program's by a relative error of at most 0.0063.
Values may be sent and summed in bfloat16 or wider, within the bound.
A program may use at most 128 MiB of HBM per device.

```python
import math
import jax
import jax.numpy as jnp
import numpy as np
from jax import lax

C = 128
L = 4
HID = 512
OUTC = 512
LAT_DEV = 12
NLON = 256
R_DEV = 512
F = 512
CAP = 20
REPORTS = 32768
NLAT = 768
N_BAND = 64


def block_scale(rng, dims, shards, low, largest):
    def one(dim, shards_of):
        draws = jax.random.uniform(jax.random.fold_in(jax.random.fold_in(rng, 6), dim), (shards_of,), jnp.float32, low / len(shards), largest / len(shards))
        return jnp.repeat(jnp.exp(draws), dims[dim] // shards_of).reshape((-1,) + (1,) * (len(dims) - dim - 1))

    gain = one(*shards[0])
    for cut in shards[1:]:
        gain = gain * one(*cut)
    return gain


def deal_out(stream_key, own, number, rows, count, top, limit, slope):
    ranking = jax.random.permutation(stream_key, count)
    crowded, ordinary = shares(count, rows * top, limit, slope, True), shares(count, rows * top, limit, slope, False)
    places = jnp.arange(count)

    def named(lengths, offset_by):
        used = int((lengths > 0).sum())
        fixed = max(1, used // 4)
        shifted = fixed + (places - fixed + offset_by * (used - fixed)) % max(1, count - fixed)
        return jnp.zeros((count,), jnp.int32).at[ranking[jnp.where(places < fixed, places, shifted)]].set(jnp.asarray(lengths, jnp.int32))

    lengths = jnp.where(number % 4 == 0, named(crowded, number // 4), named(ordinary, number - number // 4 - 1))
    mixed = jax.random.permutation(jax.random.fold_in(own, 3), count)
    donor, taker = mixed[0:count // 2 * 2:2], mixed[1:count // 2 * 2:2]
    margin = jnp.minimum(lengths[donor] - 1, limit - lengths[taker]) // 2
    margin = jnp.where((donor == ranking[0]) | (taker == ranking[0]) | (lengths[taker] == 0), 0, jnp.maximum(margin, 0))
    shifted = jax.random.randint(jax.random.fold_in(own, 4), (count // 2,), 0, 1 << 20) % (margin + 1)
    lengths = lengths.at[donor].add(-shifted).at[taker].add(shifted)
    items = jnp.searchsorted(jnp.cumsum(lengths), jnp.arange(rows * top), side="right").astype(jnp.int32)
    listing = items.reshape(top, rows).T
    listing = listing[jax.random.permutation(jax.random.fold_in(own, 1), rows)]
    offset_by = jax.random.randint(jax.random.fold_in(own, 2), (rows, 1), 0, top)
    return jnp.take_along_axis(listing, (jnp.arange(top)[None, :] + offset_by) % top, axis=1)


def shares(number_of, total, most, lean, full):
    portions = [(1 << 20) // math.isqrt(rank ** lean) + 1 for rank in range(1, number_of + 1)]
    largest = most if full else min(most, max(-(-total // number_of), total * portions[0] // sum(portions)))
    least = 1 if total - largest >= number_of - 1 else 0
    given, surplus = [largest] + [least] * (number_of - 1), total - largest - least * (number_of - 1)
    while surplus > 0:
        movable = [i for i in range(1, number_of) if given[i] < largest] or [i for i in range(1, number_of) if given[i] < most]
        pool, remaining = sum([portions[i] for i in movable]), surplus
        for i in movable:
            extra = min(most - given[i], max(1, remaining * portions[i] // pool), surplus)
            given[i] = given[i] + extra
            surplus = surplus - extra
    return np.array(given)


def gaussian(rng, extent, deviation, bound, cuts=(), kind=jnp.bfloat16):
    drawn = deviation * jax.random.normal(rng, extent, jnp.float32)
    if cuts:
        drawn = drawn * block_scale(rng, extent, cuts, -0.22, 0.18)
    return jnp.clip(drawn, -bound, bound).astype(kind)


def setup_inputs(seed: int = 0) -> dict:
    streams_of = jax.random.split(jax.random.key(seed), 9)
    embeddings = gaussian(streams_of[0], (C, REPORTS), 1.0, 6.0, ((0, 4), (1, 64)))
    route_keys = jax.random.split(jax.random.fold_in(streams_of[1], 1), REPORTS // R_DEV)
    route_turns = jax.random.permutation(jax.random.fold_in(streams_of[1], 3), REPORTS // R_DEV)
    route = jax.vmap(lambda own, number: deal_out(jax.random.fold_in(streams_of[1], 2), own, number, R_DEV, N_BAND, 1, CAP, 2))(route_keys, route_turns).reshape((REPORTS, 1))
    place = jnp.clip(1.0 * jax.random.uniform(streams_of[2], (2, REPORTS), jnp.float32) ** block_scale(streams_of[2], (2, REPORTS), ((1, 64),), -0.2, 0.2), 0.0, 1.0).astype(jnp.bfloat16)
    scales = jnp.clip(jnp.exp(jax.random.uniform(streams_of[3], (L,), jnp.float32, math.log(0.25), math.log(1.0))), 0.25, 1.0)
    first_weight = gaussian(streams_of[4], (F, HID), F ** -0.5, 0.25)
    first_bias = gaussian(streams_of[5], (HID,), 0.5, 3.0, (), jnp.float32)
    second_weight = gaussian(streams_of[6], (HID, OUTC), HID ** -0.5, 0.25)
    out_cotangent = gaussian(streams_of[7], (OUTC, NLAT, NLON), 1.0, 6.0, ((1, 256),))
    return {"embeddings": embeddings, "route": route, "place": place, "scales": scales, "first_weight": first_weight, "first_bias": first_bias, "second_weight": second_weight, "out_cotangent": out_cotangent}


root_two_pi = 0.7978845608028654
cubic = 0.044715


def gelu_value(value):
    inner = root_two_pi * (value + cubic * value * value * value)
    return 0.5 * value * (1.0 + jnp.tanh(inner))


def gelu_slope(value):
    tangent = jnp.tanh(root_two_pi * (value + cubic * value * value * value))
    return 0.5 * (1.0 + tangent) + 0.5 * value * (1.0 - tangent * tangent) * root_two_pi * (1.0 + 3.0 * cubic * value * value)


def kernel_factors(geometry, block, scales, lat_rows, columns):
    north_fraction = geometry[0]
    east_fraction = geometry[1]
    valid = geometry[2]
    centre_rows = jnp.arange(lat_rows, dtype=jnp.float32) + 0.5
    north_gap = ((1 - block).astype(jnp.float32) * lat_rows)[None, :] + centre_rows[:, None] - (north_fraction * lat_rows)[None, :]
    east_gap = (jnp.arange(columns, dtype=jnp.float32) + 0.5)[:, None] - (east_fraction * columns)[None, :]
    reach = scales * lat_rows
    inverse = 0.5 / (reach * reach)
    row_kernel = (jnp.exp(-(north_gap * north_gap)[None] * inverse[:, None, None]) * valid[None, None, :]).astype(jnp.bfloat16)
    column_kernel = jnp.exp(-(east_gap * east_gap)[None] * inverse[:, None, None]).astype(jnp.bfloat16)
    return row_kernel, column_kernel


def splat(embedded, row_kernel, column_kernel):
    channels = embedded.shape[0]
    levels, lat_rows, slots = row_kernel.shape
    columns = column_kernel.shape[1]
    sums = []
    weights = []
    for level in range(levels):
        weighted = (embedded[:, None, :] * row_kernel[level][None]).reshape(channels * lat_rows, slots)
        sums.append(lax.dot_general(weighted, column_kernel[level], (((1,), (1,)), ((), ())), preferred_element_type=jnp.float32))
        weights.append(lax.dot_general(row_kernel[level], column_kernel[level], (((1,), (1,)), ((), ())), preferred_element_type=jnp.float32))
    splatted = jnp.stack(sums).reshape(levels, channels, lat_rows * columns)
    density = jnp.stack(weights).reshape(levels, lat_rows * columns)
    features = (splatted / (density[:, None, :] + 1.0)).transpose(1, 0, 2).reshape(channels * levels, lat_rows * columns).astype(jnp.bfloat16)
    return features, density


def spread_back(gradient, row_kernel, column_kernel):
    levels, lat_rows, slots = row_kernel.shape
    columns = column_kernel.shape[1]
    channels = gradient.shape[0] // levels
    grid = gradient.reshape(channels, levels, lat_rows * columns)
    total = jnp.zeros((channels, slots), jnp.float32)
    for level in range(levels):
        slab = grid[:, level].reshape(channels * lat_rows, columns)
        along = jnp.dot(slab, column_kernel[level], preferred_element_type=jnp.float32).reshape(channels, lat_rows, slots)
        total = total + jnp.sum(along * row_kernel[level][None].astype(jnp.float32), axis=1)
    return total


def reference(embeddings, route, place, scales, first_weight, first_bias, second_weight, out_cotangent):
    channels, total = embeddings.shape
    bands = N_BAND
    capacity = CAP
    reports = R_DEV
    lat_rows = LAT_DEV
    columns = NLON
    levels = L
    cells = lat_rows * columns
    slots = bands * capacity
    owner = route[:, 0].reshape(bands, reports)
    onehot = (owner[:, :, None] == jnp.arange(bands, dtype=jnp.int32)[None, None, :]).astype(jnp.int32)
    running = jnp.cumsum(onehot, axis=1)
    rank = jnp.sum((running - 1) * onehot, axis=2)
    source = jnp.arange(bands, dtype=jnp.int32)[:, None] * jnp.ones((1, reports), jnp.int32)
    position = (owner * slots + source * capacity + rank).reshape(-1).astype(jnp.int32)
    table = jnp.full((bands * slots,), -1, jnp.int32).at[position].set(jnp.arange(total, dtype=jnp.int32))
    table = table.reshape(bands, slots)
    empty = jnp.full((1, slots), -1, jnp.int32)
    padded = jnp.concatenate([empty, table, empty], axis=0)
    block = (jnp.arange(3 * slots, dtype=jnp.int32) // slots).astype(jnp.int32)
    packed_all = jnp.concatenate([embeddings, place, jnp.ones((1, total), jnp.bfloat16)], axis=0)

    def one_band(carry, band):
        gradient_sum, first_sum, bias_sum, second_sum = carry
        members = lax.dynamic_slice_in_dim(padded, band, 3, 0).reshape(-1)
        valid = members >= 0
        safe = jnp.where(valid, members, 0).astype(jnp.int32)
        gathered = jnp.where(valid[None, :], packed_all[:, safe], jnp.zeros((), jnp.bfloat16))
        embedded = gathered[:channels]
        geometry = gathered[channels:].astype(jnp.float32)
        row_kernel, column_kernel = kernel_factors(geometry, block, scales, lat_rows, columns)
        features, density = splat(embedded, row_kernel, column_kernel)
        cotangent = lax.dynamic_slice_in_dim(out_cotangent, (band * lat_rows).astype(jnp.int32), lat_rows, 1).reshape(out_cotangent.shape[0], cells)
        preact = lax.dot_general(first_weight, features, (((0,), (0,)), ((), ())), preferred_element_type=jnp.float32) + first_bias[:, None]
        hidden = gelu_value(preact).astype(jnp.bfloat16)
        pre_gradient = (jnp.dot(second_weight, cotangent, preferred_element_type=jnp.float32) * gelu_slope(preact)).astype(jnp.bfloat16)
        first_sum = first_sum + lax.dot_general(features, pre_gradient, (((1,), (1,)), ((), ())), preferred_element_type=jnp.float32)
        second_sum = second_sum + lax.dot_general(hidden, cotangent, (((1,), (1,)), ((), ())), preferred_element_type=jnp.float32)
        bias_sum = bias_sum + jnp.sum(pre_gradient.astype(jnp.float32), axis=1)
        feature_gradient = jnp.dot(first_weight, pre_gradient, preferred_element_type=jnp.float32)
        splat_gradient = (feature_gradient.reshape(channels, levels, cells) / (density[None] + 1.0)).reshape(channels * levels, cells).astype(jnp.bfloat16)
        slot_gradient = spread_back(splat_gradient, row_kernel, column_kernel)
        gradient_sum = gradient_sum.at[:, safe].add(jnp.where(valid[None, :], slot_gradient, 0.0))
        return (gradient_sum, first_sum, bias_sum, second_sum), None

    start = (jnp.zeros((channels, total), jnp.float32),
             jnp.zeros(first_weight.shape, jnp.float32),
             jnp.zeros(first_bias.shape, jnp.float32),
             jnp.zeros(second_weight.shape, jnp.float32))
    final, _ = lax.scan(one_band, start, jnp.arange(bands, dtype=jnp.int32))
    return final[0], final[1], final[2], final[3]
```

```python
import jax
import jax.numpy as jnp
from jax import lax
from jax.experimental import pallas as pl
from jax.experimental.pallas import tpu as pltpu
from jax.sharding import PartitionSpec as P

MESH = pl.DeviceIdType.MESH
bf16 = jnp.bfloat16
f32 = jnp.float32

root_two_pi = 0.7978845608028654
cubic = 0.044715
half_log2e = 0.8493218002880191

BANDS = 64
REPS = 4
YS, ZS, CORES = 4, 8, 2
CAP = 20
TILE = 16
ROWS = BANDS * TILE
REPORTS = 512
LEVELS = 4
CH = 128
PART = 32
SUB = 3
NLON = 256
LAT = 12.0
CELLS = SUB * NLON
HID = 512
GROWS = 4096


def iota(shape, dim):
    return lax.broadcasted_iota(jnp.int32, shape, dim)


def one_where(cond):
    return jnp.where(cond, 1.0, 0.0).astype(bf16)


def dot(a, b):
    return lax.dot_general(a, b, (((1,), (0,)), ((), ())), preferred_element_type=f32)


def dot_nt(a, b):
    return lax.dot_general(a, b, (((1,), (1,)), ((), ())), preferred_element_type=f32)


def eye(n):
    return one_where(iota((n, n), 0) == iota((n, n), 1))


def row_keys(start, rows):
    row = iota((rows, 1), 0) + start
    band = row >> 4
    ok = row & 15
    key = jnp.where(ok == 15, -1000, (band - 1) * 5 + ok).astype(f32)
    place_band = jnp.where(ok == 15, band, -1000).astype(f32)
    return key, place_band


def report_ranks(route_ref):
    owner = jnp.zeros((1, REPORTS), f32)
    cols = []
    for part in range(4):
        col = route_ref[part * 128 : (part + 1) * 128, :].astype(f32)
        cols.append(col)
        same = iota((128, REPORTS), 0) + part * 128 == iota((128, REPORTS), 1)
        owner = owner + jnp.sum(jnp.where(same, col, 0.0), axis=0, keepdims=True)
    rank = jnp.zeros((1, REPORTS), f32)
    for part in range(4):
        before = iota((128, REPORTS), 0) + part * 128 < iota((128, REPORTS), 1)
        rank = rank + jnp.sum(
            jnp.where((cols[part] == owner) & before, 1.0, 0.0), axis=0, keepdims=True
        )
    return owner, rank


def greet(me, rep):
    barrier = pltpu.get_barrier_semaphore()

    def band_peer(d, carry):
        pl.semaphore_signal(
            barrier, inc=1, device_id=(lax.rem(me + d, BANDS), rep), device_id_type=MESH
        )
        return carry

    lax.fori_loop(1, BANDS, band_peer, 0)
    for d in range(1, REPS):
        pl.semaphore_signal(
            barrier, inc=1, device_id=(me, lax.rem(rep + d, REPS)), device_id_type=MESH
        )
    return barrier


def send_tiles(me, rep, table, landing, send_sem, recv_sem):
    def send(d, carry):
        peer = lax.rem(me + d, BANDS)
        pltpu.make_async_remote_copy(
            src_ref=table.at[pl.ds(pl.multiple_of(peer * TILE, TILE), TILE)],
            dst_ref=landing.at[pl.ds(pl.multiple_of(me * TILE, TILE), TILE)],
            send_sem=send_sem,
            recv_sem=recv_sem,
            device_id=(peer, rep),
            device_id_type=MESH,
        ).start()
        return carry

    lax.fori_loop(1, BANDS, send, 0)


def tiles_done(me, rep, table, landing, send_sem, recv_sem):
    return pltpu.make_async_remote_copy(
        src_ref=table.at[pl.ds(0, ROWS - TILE)],
        dst_ref=landing.at[pl.ds(0, ROWS - TILE)],
        send_sem=send_sem,
        recv_sem=recv_sem,
        device_id=(lax.rem(me + 1, BANDS), rep),
        device_id_type=MESH,
    )


def gather_kernel(emb_ref, route_ref, place_ref, rr_ref, keys_ref, table, ssem, rsem, xs, xr):
    me = lax.axis_index("band")
    rep = lax.axis_index("rep")
    barrier = greet(me, rep)
    owner, rank = report_ranks(route_ref)
    quad = jnp.floor(rank * 0.25)
    within = rank - 4.0 * quad
    key = owner * 5.0 + quad
    third = owner - 3.0 * jnp.floor((owner + 0.5) * (1.0 / 3.0))
    pad = jnp.zeros((6, REPORTS), f32)
    keys_ref[...] = jnp.concatenate([key, within, pad], axis=0)
    emb = emb_ref[...].astype(f32)
    emb_b = jnp.concatenate(
        [jnp.where(within == float(s), emb, 0.0) for s in range(4)], axis=0
    ).astype(bf16)
    lam = iota((128, REPORTS), 0).astype(f32)
    spot = third * 20.0 + rank
    north = place_ref[0:1, :].astype(f32)
    east = place_ref[1:2, :].astype(f32)
    place_b = (
        jnp.where(lam == spot, north, 0.0)
        + jnp.where(lam == spot + 64.0, east, 0.0)
        + jnp.where(lam == third + 60.0, 1.0, 0.0)
    ).astype(bf16)
    for part in range(8):
        row_key, place_band = row_keys(part * 128, 128)
        pick = one_where(row_key == key)
        near = one_where(jnp.abs(place_band - owner) <= 1.0)
        table[part * 128 : (part + 1) * 128, :] = (
            dot_nt(pick, emb_b) + dot_nt(near, place_b)
        ).astype(bf16)
    pl.semaphore_wait(barrier, BANDS - 1 + REPS - 1)
    landing = rr_ref.at[rep]
    send_tiles(me, rep, table, landing, ssem, rsem)
    own = pl.ds(pl.multiple_of(me * TILE, TILE), TILE)
    rr_ref[rep, own, :] = table[own, :]
    done = tiles_done(me, rep, table, landing, ssem, rsem)
    done.wait_recv()
    copies = []
    for d in range(1, REPS):
        copy = pltpu.make_async_remote_copy(
            src_ref=rr_ref.at[rep],
            dst_ref=rr_ref.at[rep],
            send_sem=xs.at[d],
            recv_sem=xr.at[d],
            device_id=(me, lax.rem(rep + d, REPS)),
            device_id_type=MESH,
        )
        copy.start()
        copies.append(copy)
    done.wait_send()
    for copy in copies:
        copy.wait()


def decode_places(t, rep, expand, base_ref, east_ref, valid_ref):
    lane = iota((1, ROWS), 1)
    ok = lane & 15
    o = (ok >= 5).astype(jnp.int32) + (ok >= 10).astype(jnp.int32) + (ok >= 15).astype(jnp.int32)
    k4 = (ok - 5 * o) * 4
    v = lax.rem(t + 2, 3) + o
    third = jnp.where(v >= 3, v - 3, v)
    code = third * 20 + k4
    lam = iota((64, ROWS), 0)
    low = expand[0:64, :]
    high = expand[64:128, :]
    count = jnp.sum(jnp.where(lam == third + 60, low, 0.0), axis=0, keepdims=True)
    offset = (1 - o).astype(f32) * LAT + (rep * SUB).astype(f32) + 0.5
    for s in range(4):
        hit = lam == code + s
        north = jnp.sum(jnp.where(hit, low, 0.0), axis=0, keepdims=True)
        east = jnp.sum(jnp.where(hit, high, 0.0), axis=0, keepdims=True)
        valid = jnp.where((ok < 15) & ((k4 + s).astype(f32) < count), 1.0, 0.0)
        base_ref[s] = jnp.broadcast_to(offset - north * LAT, (16, ROWS))
        valid_ref[s] = jnp.broadcast_to(valid, (16, ROWS))
        east_ref[s] = jnp.broadcast_to(east * float(NLON), (8, ROWS))


def local_kernel(
    rr_ref, scales_ref, w1_ref, b1_ref, w2_ref, cot_ref,
    d_ref, g_ref, bias_ref,
    emb_t, expand, base_ref, east_ref, valid_ref, col_ref, rowf_ref, w_ref, acc_ref,
    feat_ref, w1p_ref, w1t_ref, bcol_ref, hid_ref, pg_ref, sg_ref, tot_ref,
):
    t = lax.axis_index("band")
    rep = lax.axis_index("rep")
    ident = eye(128)
    group = one_where(
        ((iota((128, 128), 0) >> 4) == (iota((128, 128), 1) >> 4)) & ((iota((128, 128), 0) & 15) == 15)
    )
    for q in range(REPS):
        turned = dot_nt(ident, rr_ref[q]).astype(bf16)
        for s in range(4):
            emb_t[s, q * PART : (q + 1) * PART, :] = turned[s * PART : (s + 1) * PART, :]
        if q == 0:
            for b in range(8):
                expand[:, b * 128 : (b + 1) * 128] = dot(turned[:, b * 128 : (b + 1) * 128], group)
    decode_places(t, rep, expand, base_ref, east_ref, valid_ref)
    acc_ref[...] = jnp.zeros_like(acc_ref)

    def splat(it, carry):
        s = it >> 2
        level = it & 3
        reach = scales_ref[level] * LAT
        scale = half_log2e / jnp.full((1, 128), reach, f32)
        scale_wide = jnp.concatenate([scale] * 8, axis=1)
        east = east_ref[s, 0:1, :] * scale_wide
        for c in range(8):
            centre = (iota((32, 128), 0).astype(f32) + (c * 32 + 0.5)) * scale
            for b in range(8):
                gap = centre - east[:, b * 128 : (b + 1) * 128]
                col_ref[it, c * 32 : (c + 1) * 32, b * 128 : (b + 1) * 128] = jnp.exp2(
                    -(gap * gap)
                ).astype(bf16)
        valid = valid_ref[s]
        rows = []
        for i in range(SUB):
            gap = (base_ref[s] + float(i)) * scale_wide
            rows.append((jnp.exp2(-(gap * gap)) * valid).astype(bf16))
        sub = iota((16, ROWS), 0)
        wide = [r.astype(f32) for r in rows]
        mixed = jnp.where(
            sub == 0, wide[0], jnp.where(sub == 1, wide[1], jnp.where(sub == 2, wide[2], 0.0))
        )
        rowf_ref[it] = mixed[0:8, :]
        w_ref[SUB * CH : SUB * CH + 16, :] = mixed.astype(bf16)
        for c in range(8):
            e = emb_t[s, c * 16 : (c + 1) * 16, :]
            for i in range(SUB):
                w_ref[i * CH + c * 16 : i * CH + (c + 1) * 16, :] = e * rows[i]
        acc_ref[level] += dot_nt(w_ref[...], col_ref[it])
        return carry

    lax.fori_loop(0, 16, splat, 0)

    def inverse(level, i):
        return 1.0 / (acc_ref[level, SUB * CH + i : SUB * CH + i + 1, :] + 1.0)

    for level in range(LEVELS):
        for i in range(SUB):
            feat_ref[level * CH : (level + 1) * CH, i * NLON : (i + 1) * NLON] = (
                acc_ref[level, i * CH : (i + 1) * CH, :] * inverse(level, i)
            ).astype(bf16)

    r512 = iota((512, 512), 0)
    c512 = iota((512, 512), 1)
    w1p_ref[...] = dot(one_where(c512 == (r512 & 127) * 4 + (r512 >> 7)), w1_ref[...]).astype(bf16)
    w1t_ref[...] = dot_nt(eye(512), w1p_ref[...]).astype(bf16)
    bcol_ref[...] = jnp.sum(jnp.where(r512 == c512, b1_ref[...], 0.0), axis=1, keepdims=True)

    for i in range(SUB):
        cells = slice(i * NLON, (i + 1) * NLON)
        for h in range(2):
            rows = slice(h * 256, (h + 1) * 256)
            pre = dot(w1t_ref[rows, :], feat_ref[:, cells]) + bcol_ref[rows, :]
            above = dot(w2_ref[rows, :], cot_ref[:, cells])
            square = pre * pre
            tangent = jnp.tanh(root_two_pi * (pre + cubic * square * pre))
            hid_ref[rows, cells] = (0.5 * pre * (1.0 + tangent)).astype(bf16)
            slope = 0.5 * (1.0 + tangent) + 0.5 * pre * (1.0 - tangent * tangent) * root_two_pi * (
                1.0 + 3.0 * cubic * square
            )
            pg_ref[rows, cells] = (above * slope).astype(bf16)

    back = one_where(c512 == (r512 & 3) * 128 + (r512 >> 2))
    for h in range(2):
        rows = slice(h * 256, (h + 1) * 256)
        first = dot(back, dot_nt(feat_ref[...], pg_ref[rows, :]).astype(bf16)).astype(bf16)
        second = dot_nt(hid_ref[...], cot_ref[rows, :]).astype(bf16)
        for c in range(2):
            at = (h * 2 + c) * 1024
            g_ref[at : at + 512, :] = first[:, c * 128 : (c + 1) * 128]
            g_ref[at + 512 : at + 1024, :] = second[:, c * 128 : (c + 1) * 128]
    bias = dot_nt(jnp.ones((16, CELLS), bf16), pg_ref[...])
    bias_ref[...] = jnp.concatenate(
        [bias[0:1, c * 128 : (c + 1) * 128] for c in range(4)] + [jnp.zeros((4, 128), f32)], axis=0
    )

    for i in range(SUB):
        grad = dot(w1p_ref[...], pg_ref[:, i * NLON : (i + 1) * NLON])
        for level in range(LEVELS):
            sg_ref[level, i * CH : (i + 1) * CH, :] = (
                grad[level * CH : (level + 1) * CH, :] * inverse(level, i)
            ).astype(bf16)

    def spread(s, carry):
        tot_ref[...] = jnp.zeros_like(tot_ref)

        def one_level(level, inner):
            it = s * 4 + level
            for n in range(4):
                lanes = slice(n * 256, (n + 1) * 256)
                along = dot(sg_ref[level], col_ref[it, :, lanes])
                total = tot_ref[:, lanes]
                for i in range(SUB):
                    total = total + along[i * CH : (i + 1) * CH, :] * rowf_ref[it, i : i + 1, lanes]
                tot_ref[:, lanes] = total
            return inner

        lax.fori_loop(0, LEVELS, one_level, 0)
        at = pl.ds(pl.multiple_of(s * PART, PART), PART)
        for q in range(REPS):
            d_ref[q, at, :] = tot_ref[q * PART : (q + 1) * PART, :].astype(bf16)
        return carry

    lax.fori_loop(0, 4, spread, 0)


def reduce_kernel(
    d_ref, g_ref, bias_ref, keys_ref,
    eg_ref, full_ref, bout_ref,
    d_in, table, landing, pick_ref, g1, g2, g3, in_c, in_y, in_z, in_x, bc, by, bz, bx,
    ds, dr, ssem, rsem, gs, gr, bs, br, as_, ar,
):
    me = lax.axis_index("band")
    rep = lax.axis_index("rep")
    core = lax.rem(me, CORES)
    z = lax.rem(me // CORES, ZS)
    y = me // (CORES * ZS)
    barrier = greet(me, rep)
    key = keys_ref[0:1, :]
    within = keys_ref[1:2, :]
    pl.semaphore_wait(barrier, BANDS - 1 + REPS - 1)

    def core_peer(d):
        return me + 1 - 2 * core, rep

    def y_peer(d):
        return lax.rem(y + d, YS) * (CORES * ZS) + z * CORES + core, rep

    def z_peer(d):
        return y * (CORES * ZS) + lax.rem(z + d, ZS) * CORES + core, rep

    def x_peer(d):
        return me, lax.rem(rep + d, REPS)

    def start(src, dst, send, recv, device):
        copy = pltpu.make_async_remote_copy(
            src_ref=src, dst_ref=dst, send_sem=send, recv_sem=recv, device_id=device, device_id_type=MESH
        )
        copy.start()
        return copy

    def rows_at(index, size):
        return pl.ds(pl.multiple_of(index * size, size), size)

    def scatter(src, dst, size, n, mine, peer, base):
        return [
            start(
                src.at[rows_at(lax.rem(mine + d, n), size)], dst.at[d - 1],
                gs.at[base + d - 1], gr.at[base + d - 1], peer(d),
            )
            for d in range(1, n)
        ]

    def bias_round(value, slots, n, mine, peer, base):
        slots[mine] = value
        return [
            start(slots.at[mine], slots.at[mine], bs.at[base + d - 1], br.at[base + d - 1], peer(d))
            for d in range(1, n)
        ]

    def bias_sum(slots, n):
        total = slots[0]
        for k in range(1, n):
            total = total + slots[k]
        return total

    def finish(copies):
        for copy in copies:
            copy.wait()

    def spread_out(offset, size, n, peer, base):
        at = pl.ds(pl.multiple_of(offset, size), size)
        return [
            start(full_ref.at[at], full_ref.at[at], as_.at[base + d - 1], ar.at[base + d - 1], peer(d))
            for d in range(1, n)
        ]

    d_copies = [
        start(d_ref.at[lax.rem(rep + d, REPS)], d_in.at[d - 1], ds.at[d - 1], dr.at[d - 1], x_peer(d))
        for d in range(1, REPS)
    ]
    c_copies = scatter(g_ref, in_c, 2048, CORES, core, core_peer, 0)
    c_bias = bias_round(bias_ref[...], bc, CORES, core, core_peer, 0)
    for part in range(8):
        row_key, _ = row_keys(part * 128, 128)
        pick_ref[part * 128 : (part + 1) * 128, :] = one_where(row_key == key)
    finish(c_copies)
    g1[...] = (g_ref[rows_at(core, 2048), :].astype(f32) + in_c[0].astype(f32)).astype(bf16)
    y_copies = scatter(g1, in_y, 512, YS, y, y_peer, 1)
    finish(c_bias)
    y_bias = bias_round(bias_sum(bc, CORES), by, YS, y, y_peer, 1)
    finish(y_copies)
    total = g1[rows_at(y, 512), :].astype(f32)
    for d in range(YS - 1):
        total = total + in_y[d].astype(f32)
    g2[...] = total.astype(bf16)
    z_copies = scatter(g2, in_z, 64, ZS, z, z_peer, 4)
    finish(y_bias)
    z_bias = bias_round(bias_sum(by, YS), bz, ZS, z, z_peer, 4)
    finish(d_copies)
    part = d_ref[rep].astype(f32)
    for d in range(REPS - 1):
        part = part + d_in[d].astype(f32)
    table[...] = jnp.transpose(part).astype(bf16)
    send_tiles(me, rep, table, landing, ssem, rsem)
    own = rows_at(me, TILE)
    landing[own, :] = table[own, :]
    finish(z_copies)
    total = g2[rows_at(z, 64), :].astype(f32)
    for d in range(ZS - 1):
        total = total + in_z[d].astype(f32)
    g3[...] = total.astype(bf16)
    x_copies = scatter(g3, in_x, 16, REPS, rep, x_peer, 11)
    finish(z_bias)
    x_bias = bias_round(bias_sum(bz, ZS), bx, REPS, rep, x_peer, 11)
    finish(x_copies)
    total = g3[rows_at(rep, 16), :].astype(f32)
    for d in range(REPS - 1):
        total = total + in_x[d].astype(f32)
    at_z = core * 2048 + y * 512 + z * 64
    full_ref[pl.ds(pl.multiple_of(at_z + rep * 16, 16), 16), :] = total.astype(bf16)
    copies = spread_out(at_z + rep * 16, 16, REPS, x_peer, 0)
    finish(x_bias)
    bout_ref[...] = bias_sum(bx, REPS)
    finish(copies)
    copies = spread_out(at_z, 64, ZS, z_peer, 3)
    finish(copies)
    copies = spread_out(core * 2048 + y * 512, 512, YS, y_peer, 10)
    tiles_done(me, rep, table, landing, ssem, rsem).wait()
    turned = dot_nt(eye(128), landing[...]).astype(bf16)
    found = dot(turned, pick_ref[...])
    gradient = jnp.zeros((PART, REPORTS), f32)
    for s in range(4):
        gradient = gradient + jnp.where(within == float(s), found[s * PART : (s + 1) * PART, :], 0.0)
    eg_ref[...] = gradient
    finish(copies)
    finish(spread_out(core * 2048, 2048, CORES, core_peer, 13))


def vmem(n):
    return [pl.BlockSpec(memory_space=pltpu.VMEM)] * n


def sds(shape, dtype):
    return jax.ShapeDtypeStruct(shape, dtype)


def on_device(
    embeddings, route, place, scales, first_weight, first_bias, second_weight, out_cotangent
):
    rr, keys = pl.pallas_call(
        gather_kernel,
        out_shape=[sds((REPS, ROWS, 128), bf16), sds((8, REPORTS), f32)],
        in_specs=vmem(3),
        out_specs=vmem(2),
        scratch_shapes=[
            pltpu.VMEM((ROWS, 128), bf16),
            pltpu.SemaphoreType.DMA,
            pltpu.SemaphoreType.DMA,
            pltpu.SemaphoreType.DMA((REPS,)),
            pltpu.SemaphoreType.DMA((REPS,)),
        ],
        compiler_params=pltpu.CompilerParams(
            collective_id=0, has_side_effects=True, vmem_limit_bytes=32 << 20
        ),
    )(embeddings, route, place)
    cotangent = out_cotangent.reshape(out_cotangent.shape[0], CELLS)
    slot, grads, bias = pl.pallas_call(
        local_kernel,
        out_shape=[
            sds((REPS, 128, ROWS), bf16),
            sds((GROWS, 128), bf16),
            sds((8, 128), f32),
        ],
        in_specs=vmem(1) + [pl.BlockSpec(memory_space=pltpu.SMEM)] + vmem(4),
        out_specs=vmem(3),
        scratch_shapes=[
            pltpu.VMEM((4, CH, ROWS), bf16),
            pltpu.VMEM((128, ROWS), f32),
            pltpu.VMEM((4, 16, ROWS), f32),
            pltpu.VMEM((4, 8, ROWS), f32),
            pltpu.VMEM((4, 16, ROWS), f32),
            pltpu.VMEM((16, NLON, ROWS), bf16),
            pltpu.VMEM((16, 8, ROWS), f32),
            pltpu.VMEM((SUB * CH + 16, ROWS), bf16),
            pltpu.VMEM((LEVELS, SUB * CH + 16, NLON), f32),
            pltpu.VMEM((512, CELLS), bf16),
            pltpu.VMEM((512, HID), bf16),
            pltpu.VMEM((HID, 512), bf16),
            pltpu.VMEM((HID, 1), f32),
            pltpu.VMEM((HID, CELLS), bf16),
            pltpu.VMEM((HID, CELLS), bf16),
            pltpu.VMEM((LEVELS, SUB * CH, NLON), bf16),
            pltpu.VMEM((CH, ROWS), f32),
        ],
        compiler_params=pltpu.CompilerParams(vmem_limit_bytes=52 << 20),
    )(rr, scales, first_weight, first_bias.reshape(1, HID), second_weight, cotangent)
    dma = pltpu.SemaphoreType.DMA
    gradient, full, bias_total = pl.pallas_call(
        reduce_kernel,
        out_shape=[
            sds((PART, REPORTS), f32),
            sds((GROWS, 128), bf16),
            sds((8, 128), f32),
        ],
        in_specs=vmem(4),
        out_specs=vmem(3),
        scratch_shapes=[
            pltpu.VMEM((REPS - 1, 128, ROWS), bf16),
            pltpu.VMEM((ROWS, 128), bf16),
            pltpu.VMEM((ROWS, 128), bf16),
            pltpu.VMEM((ROWS, REPORTS), bf16),
            pltpu.VMEM((2048, 128), bf16),
            pltpu.VMEM((512, 128), bf16),
            pltpu.VMEM((64, 128), bf16),
            pltpu.VMEM((1, 2048, 128), bf16),
            pltpu.VMEM((3, 512, 128), bf16),
            pltpu.VMEM((7, 64, 128), bf16),
            pltpu.VMEM((3, 16, 128), bf16),
            pltpu.VMEM((CORES, 8, 128), f32),
            pltpu.VMEM((YS, 8, 128), f32),
            pltpu.VMEM((ZS, 8, 128), f32),
            pltpu.VMEM((REPS, 8, 128), f32),
            dma((REPS - 1,)), dma((REPS - 1,)),
            dma, dma,
            dma((14,)), dma((14,)),
            dma((14,)), dma((14,)),
            dma((14,)), dma((14,)),
        ],
        compiler_params=pltpu.CompilerParams(
            collective_id=1, has_side_effects=True, vmem_limit_bytes=32 << 20
        ),
    )(slot, grads, bias, keys)
    both = full.reshape(4, 2, 512, 128).transpose(1, 2, 0, 3).reshape(2, 512, 512).astype(f32)
    return (gradient, both[0], bias_total[0:4].reshape(HID), both[1])


def solution(mesh):
    return jax.shard_map(
        on_device,
        mesh=mesh,
        in_specs=(
            P("rep", "band"),
            P("band", None),
            P(None, "band"),
            P(),
            P(),
            P(),
            P(),
            P(None, ("band", "rep"), None),
        ),
        out_specs=(P("rep", "band"), P(), P(), P()),
        check_vma=False,
    )
```

```python
import jax
import jax.numpy as jnp
from jax import lax
from jax.experimental import pallas as pl
from jax.experimental.pallas import tpu as pltpu
from jax.sharding import PartitionSpec as P

MESH = pl.DeviceIdType.MESH
bf16 = jnp.bfloat16
f32 = jnp.float32

root_two_pi = 0.7978845608028654
cubic = 0.044715
half_log2e = 0.8493218002880191

BANDS = 64
REPS = 4
YS, ZS, CORES = 4, 8, 2
CAP = 20
TILE = 16
ROWS = BANDS * TILE
REPORTS = 512
LEVELS = 4
CH = 128
PART = 32
SUB = 3
NLON = 256
LAT = 12.0
CELLS = SUB * NLON
HID = 512
GROWS = 4096


def iota(shape, dim):
    return lax.broadcasted_iota(jnp.int32, shape, dim)


def one_where(cond):
    return jnp.where(cond, 1.0, 0.0).astype(bf16)


def dot(a, b):
    return lax.dot_general(a, b, (((1,), (0,)), ((), ())), preferred_element_type=f32)


def dot_nt(a, b):
    return lax.dot_general(a, b, (((1,), (1,)), ((), ())), preferred_element_type=f32)


def eye(n):
    return one_where(iota((n, n), 0) == iota((n, n), 1))


def row_keys(start, rows):
    row = iota((rows, 1), 0) + start
    band = row >> 4
    ok = row & 15
    key = jnp.where(ok == 15, -1000, (band - 1) * 5 + ok).astype(f32)
    place_band = jnp.where(ok == 15, band, -1000).astype(f32)
    return key, place_band


def report_ranks(route_ref):
    owner = route_ref[...].astype(f32)
    rank = jnp.zeros((1, REPORTS), f32)
    for part in range(4):
        mine = iota((128, REPORTS), 0) + part * 128
        lane = iota((128, REPORTS), 1)
        col = jnp.sum(jnp.where(mine == lane, owner, 0.0), axis=1, keepdims=True)
        rank = rank + jnp.sum(
            jnp.where((col == owner) & (mine < lane), 1.0, 0.0), axis=0, keepdims=True
        )
    return owner, rank


def greet(me, rep):
    barrier = pltpu.get_barrier_semaphore()

    def band_peer(d, carry):
        pl.semaphore_signal(
            barrier, inc=1, device_id=(lax.rem(me + d, BANDS), rep), device_id_type=MESH
        )
        return carry

    lax.fori_loop(1, BANDS, band_peer, 0)
    for d in range(1, REPS):
        pl.semaphore_signal(
            barrier, inc=1, device_id=(me, lax.rem(rep + d, REPS)), device_id_type=MESH
        )
    return barrier


def send_tiles(me, rep, table, landing, send_sem, recv_sem):
    def send(d, carry):
        peer = lax.rem(me + d, BANDS)
        pltpu.make_async_remote_copy(
            src_ref=table.at[pl.ds(pl.multiple_of(peer * TILE, TILE), TILE)],
            dst_ref=landing.at[pl.ds(pl.multiple_of(me * TILE, TILE), TILE)],
            send_sem=send_sem,
            recv_sem=recv_sem,
            device_id=(peer, rep),
            device_id_type=MESH,
        ).start()
        return carry

    lax.fori_loop(1, BANDS, send, 0)


def tiles_done(me, rep, table, landing, send_sem, recv_sem):
    return pltpu.make_async_remote_copy(
        src_ref=table.at[pl.ds(0, ROWS - TILE)],
        dst_ref=landing.at[pl.ds(0, ROWS - TILE)],
        send_sem=send_sem,
        recv_sem=recv_sem,
        device_id=(lax.rem(me + 1, BANDS), rep),
        device_id_type=MESH,
    )


def decode_places(t, rep, expand, base_ref, east_ref, valid_ref):
    lane = iota((1, ROWS), 1)
    ok = lane & 15
    o = (ok >= 5).astype(jnp.int32) + (ok >= 10).astype(jnp.int32) + (ok >= 15).astype(jnp.int32)
    k4 = (ok - 5 * o) * 4
    v = lax.rem(t + 2, 3) + o
    third = jnp.where(v >= 3, v - 3, v)
    code = third * 20 + k4
    lam = iota((64, ROWS), 0)
    low = expand[0:64, :]
    high = expand[64:128, :]
    count = jnp.sum(jnp.where(lam == third + 60, low, 0.0), axis=0, keepdims=True)
    offset = (1 - o).astype(f32) * LAT + (rep * SUB).astype(f32) + 0.5
    for s in range(4):
        hit = lam == code + s
        north = jnp.sum(jnp.where(hit, low, 0.0), axis=0, keepdims=True)
        east = jnp.sum(jnp.where(hit, high, 0.0), axis=0, keepdims=True)
        valid = jnp.where((ok < 15) & ((k4 + s).astype(f32) < count), 1.0, 0.0)
        base_ref[s] = jnp.broadcast_to(offset - north * LAT, (16, ROWS))
        valid_ref[s] = jnp.broadcast_to(valid, (16, ROWS))
        east_ref[s] = jnp.broadcast_to(east * float(NLON), (8, ROWS))


def build_table(emb_ref, place_ref, owner, rank, pick_ref, table):
    quad = jnp.floor(rank * 0.25)
    within = rank - 4.0 * quad
    key = owner * 5.0 + quad
    third = owner - 3.0 * jnp.floor((owner + 0.5) * (1.0 / 3.0))
    emb = emb_ref[...].astype(f32)
    emb_b = jnp.concatenate(
        [jnp.where(within == float(s), emb, 0.0) for s in range(4)], axis=0
    ).astype(bf16)
    lam = iota((128, REPORTS), 0).astype(f32)
    spot = third * 20.0 + rank
    north = place_ref[0:1, :].astype(f32)
    east = place_ref[1:2, :].astype(f32)
    place_b = (
        jnp.where(lam == spot, north, 0.0)
        + jnp.where(lam == spot + 64.0, east, 0.0)
        + jnp.where(lam == third + 60.0, 1.0, 0.0)
    ).astype(bf16)
    for part in range(8):
        rows = slice(part * 128, (part + 1) * 128)
        row_key, place_band = row_keys(part * 128, 128)
        pick = one_where(row_key == key)
        pick_ref[rows, :] = pick
        near = one_where(jnp.abs(place_band - owner) <= 1.0)
        table[rows, :] = (dot_nt(pick, emb_b) + dot_nt(near, place_b)).astype(bf16)
    return within


def kernels(it, scales_ref, base_ref, east_ref, valid_ref, col_ref, rk_ref, mix_ref, rowf_ref):
    s = it >> 2
    reach = scales_ref[it & 3] * LAT
    scale = half_log2e / jnp.full((1, 128), reach, f32)
    scale_wide = jnp.concatenate([scale] * 8, axis=1)
    east = east_ref[s, 0:1, :] * scale_wide
    for c in range(8):
        centre = (iota((32, 128), 0).astype(f32) + (c * 32 + 0.5)) * scale
        for b in range(8):
            gap = centre - east[:, b * 128 : (b + 1) * 128]
            col_ref[it, c * 32 : (c + 1) * 32, b * 128 : (b + 1) * 128] = jnp.exp2(
                -(gap * gap)
            ).astype(bf16)
    valid = valid_ref[s]
    wide = []
    for i in range(SUB):
        gap = (base_ref[s] + float(i)) * scale_wide
        row = (jnp.exp2(-(gap * gap)) * valid).astype(bf16)
        rk_ref[it, i] = row
        wide.append(row.astype(f32))
    sub = iota((16, ROWS), 0)
    mixed = jnp.where(
        sub == 0, wide[0], jnp.where(sub == 1, wide[1], jnp.where(sub == 2, wide[2], 0.0))
    )
    rowf_ref[it] = mixed[0:8, :]
    mix_ref[it] = mixed.astype(bf16)


def grid_kernel(
    emb_ref, route_ref, place_ref, scales_ref, w1_hbm, b1_ref, w2_hbm, cot_hbm,
    eg_ref, grads_ref, bout_ref,
    table, rr_ref, pick_ref, w1_ref, w2_ref, cot_ref,
    emb_t, expand, base_ref, east_ref, valid_ref, col_ref, rk_ref, mix_ref, rowf_ref, w_ref, acc_ref,
    feat_ref, w1p_ref, w1t_ref, bcol_ref, hid_ref, pg_ref, sg_ref,
    d_out, d_in, table2, landing, g0, g1, g2, g3, in_c, in_y, in_z, in_x, full_ref, bc, by, bz, bx,
    loads, ssem, rsem, ssem2, rsem2, xs, xr, ds, dr, gs, gr, bs, br, as_, ar,
):
    me = lax.axis_index("band")
    rep = lax.axis_index("rep")
    core = lax.rem(me, CORES)
    z = lax.rem(me // CORES, ZS)
    y = me // (CORES * ZS)

    def core_peer(d):
        return me + 1 - 2 * core, rep

    def y_peer(d):
        return lax.rem(y + d, YS) * (CORES * ZS) + z * CORES + core, rep

    def z_peer(d):
        return y * (CORES * ZS) + lax.rem(z + d, ZS) * CORES + core, rep

    def x_peer(d):
        return me, lax.rem(rep + d, REPS)

    def start(src, dst, send, recv, device):
        copy = pltpu.make_async_remote_copy(
            src_ref=src, dst_ref=dst, send_sem=send, recv_sem=recv, device_id=device, device_id_type=MESH
        )
        copy.start()
        return copy

    def rows_at(index, size):
        return pl.ds(pl.multiple_of(index * size, size), size)

    def scatter(src, dst, size, n, mine, peer, base):
        return [
            start(
                src.at[rows_at(lax.rem(mine + d, n), size)], dst.at[d - 1],
                gs.at[base + d - 1], gr.at[base + d - 1], peer(d),
            )
            for d in range(1, n)
        ]

    def bias_round(value, slots, n, mine, peer, base):
        slots[mine] = value
        return [
            start(slots.at[mine], slots.at[mine], bs.at[base + d - 1], br.at[base + d - 1], peer(d))
            for d in range(1, n)
        ]

    def bias_sum(slots, n):
        total = slots[0]
        for k in range(1, n):
            total = total + slots[k]
        return total

    def finish(copies):
        for copy in copies:
            copy.wait()

    def spread_out(offset, size, n, peer, base):
        at = pl.ds(pl.multiple_of(offset, size), size)
        return [
            start(full_ref.at[at], full_ref.at[at], as_.at[base + d - 1], ar.at[base + d - 1], peer(d))
            for d in range(1, n)
        ]

    barrier = greet(me, rep)
    held = []
    for k, (src, dst) in enumerate(((w1_hbm, w1_ref), (w2_hbm, w2_ref), (cot_hbm, cot_ref))):
        copy = pltpu.make_async_copy(src, dst, loads.at[k])
        copy.start()
        held.append(copy)

    owner, rank = report_ranks(route_ref)
    within = build_table(emb_ref, place_ref, owner, rank, pick_ref, table)
    pl.semaphore_wait(barrier, BANDS - 1 + REPS - 1)
    mine = rr_ref.at[rep]
    send_tiles(me, rep, table, mine, ssem, rsem)
    own = rows_at(me, TILE)
    rr_ref[rep, own, :] = table[own, :]

    finish(held)
    r512 = iota((512, 512), 0)
    c512 = iota((512, 512), 1)
    w1p_ref[...] = dot(one_where(c512 == (r512 & 127) * 4 + (r512 >> 7)), w1_ref[...]).astype(bf16)
    w1t_ref[...] = dot_nt(eye(512), w1p_ref[...]).astype(bf16)
    bcol_ref[...] = jnp.sum(jnp.where(r512 == c512, b1_ref[...], 0.0), axis=1, keepdims=True)

    done = tiles_done(me, rep, table, mine, ssem, rsem)
    done.wait_recv()
    x_copies = []
    for half in range(2):
        rows = pl.ds(half * 512, 512)
        x_copies.append(
            [
                start(
                    rr_ref.at[rep, rows], rr_ref.at[rep, rows],
                    xs.at[half * 3 + d - 1], xr.at[half * 3 + d - 1], x_peer(d),
                )
                for d in range(1, REPS)
            ]
        )

    ident = eye(128)
    group = one_where(
        ((iota((128, 128), 0) >> 4) == (iota((128, 128), 1) >> 4)) & ((iota((128, 128), 0) & 15) == 15)
    )
    turned = dot_nt(ident, rr_ref[rep]).astype(bf16)
    for b in range(8):
        expand[:, b * 128 : (b + 1) * 128] = dot(turned[:, b * 128 : (b + 1) * 128], group)
    decode_places(me, rep, expand, base_ref, east_ref, valid_ref)
    acc_ref[...] = jnp.zeros_like(acc_ref)

    def make(it, carry):
        kernels(it, scales_ref, base_ref, east_ref, valid_ref, col_ref, rk_ref, mix_ref, rowf_ref)
        return carry

    lax.fori_loop(0, 16, make, 0)

    for half in range(2):
        lanes = slice(half * 512, (half + 1) * 512)
        finish(x_copies[half])
        for q in range(REPS):
            turned = dot_nt(ident, rr_ref[q, lanes, :]).astype(bf16)
            for s in range(4):
                emb_t[s, q * PART : (q + 1) * PART, lanes] = turned[s * PART : (s + 1) * PART, :]

        def splat(it, carry):
            s = it >> 2
            level = it & 3
            rows = [rk_ref[it, i, :, lanes] for i in range(SUB)]
            w_ref[SUB * CH : SUB * CH + 16, lanes] = mix_ref[it, :, lanes]
            for c in range(8):
                e = emb_t[s, c * 16 : (c + 1) * 16, lanes]
                for i in range(SUB):
                    w_ref[i * CH + c * 16 : i * CH + (c + 1) * 16, lanes] = e * rows[i]
            acc_ref[level] += dot_nt(w_ref[:, lanes], col_ref[it, :, lanes])
            return carry

        lax.fori_loop(0, 16, splat, 0)
    done.wait_send()

    def inverse(level, i):
        return 1.0 / (acc_ref[level, SUB * CH + i : SUB * CH + i + 1, :] + 1.0)

    for level in range(LEVELS):
        for i in range(SUB):
            feat_ref[level * CH : (level + 1) * CH, i * NLON : (i + 1) * NLON] = (
                acc_ref[level, i * CH : (i + 1) * CH, :] * inverse(level, i)
            ).astype(bf16)

    for i in range(SUB):
        cells = slice(i * NLON, (i + 1) * NLON)
        for h in range(2):
            rows = slice(h * 256, (h + 1) * 256)
            pre = dot(w1t_ref[rows, :], feat_ref[:, cells]) + bcol_ref[rows, :]
            above = dot(w2_ref[rows, :], cot_ref[i])
            square = pre * pre
            tangent = jnp.tanh(root_two_pi * (pre + cubic * square * pre))
            hid_ref[rows, cells] = (0.5 * pre * (1.0 + tangent)).astype(bf16)
            slope = 0.5 * (1.0 + tangent) + 0.5 * pre * (1.0 - tangent * tangent) * root_two_pi * (
                1.0 + 3.0 * cubic * square
            )
            pg_ref[rows, cells] = (above * slope).astype(bf16)

    back = one_where(c512 == (r512 & 3) * 128 + (r512 >> 2))
    for h in range(2):
        rows = slice(h * 256, (h + 1) * 256)
        first = dot(back, dot_nt(feat_ref[...], pg_ref[rows, :]).astype(bf16)).astype(bf16)
        second = dot_nt(hid_ref[:, 0:NLON], cot_ref[0, rows, :])
        for i in range(1, SUB):
            second = second + dot_nt(hid_ref[:, i * NLON : (i + 1) * NLON], cot_ref[i, rows, :])
        second = second.astype(bf16)
        for c in range(2):
            at = (h * 2 + c) * 1024
            g0[at : at + 512, :] = first[:, c * 128 : (c + 1) * 128]
            g0[at + 512 : at + 1024, :] = second[:, c * 128 : (c + 1) * 128]
    bias = dot_nt(jnp.ones((16, CELLS), bf16), pg_ref[...])
    bias_tile = jnp.concatenate(
        [bias[0:1, c * 128 : (c + 1) * 128] for c in range(4)] + [jnp.zeros((4, 128), f32)], axis=0
    )
    c_copies = scatter(g0, in_c, 2048, CORES, core, core_peer, 0)
    c_bias = bias_round(bias_tile, bc, CORES, core, core_peer, 0)

    for i in range(SUB):
        grad = dot(w1p_ref[...], pg_ref[:, i * NLON : (i + 1) * NLON])
        for level in range(LEVELS):
            sg_ref[level, i * CH : (i + 1) * CH, :] = (
                grad[level * CH : (level + 1) * CH, :] * inverse(level, i)
            ).astype(bf16)

    def spread(n):
        lanes = slice(n * 256, (n + 1) * 256)

        def one_group(s, carry):
            total = None
            for level in range(LEVELS):
                it = s * 4 + level
                along = dot(sg_ref[level], col_ref[it, :, lanes])
                for i in range(SUB):
                    term = along[i * CH : (i + 1) * CH, :] * rowf_ref[it, i : i + 1, lanes]
                    total = term if total is None else total + term
            for q in range(REPS):
                d_out[n, q, rows_at(s, PART), :] = total[q * PART : (q + 1) * PART, :].astype(bf16)
            return carry

        lax.fori_loop(0, 4, one_group, 0)
        return [
            start(
                d_out.at[n, lax.rem(rep + d, REPS)], d_in.at[n, d - 1],
                ds.at[n * 3 + d - 1], dr.at[n * 3 + d - 1], x_peer(d),
            )
            for d in range(1, REPS)
        ]

    def to_feeds(n, copies):
        finish(copies)
        total = d_out[n, rep].astype(f32)
        for d in range(REPS - 1):
            total = total + d_in[n, d].astype(f32)
        table2[n * 256 : (n + 1) * 256, :] = jnp.transpose(total).astype(bf16)

        def send(j, carry):
            peer = n * 16 + lax.rem(j + me, 16)

            @pl.when(peer != me)
            def _():
                pltpu.make_async_remote_copy(
                    src_ref=table2.at[rows_at(peer, TILE)],
                    dst_ref=landing.at[rows_at(me, TILE)],
                    send_sem=ssem2,
                    recv_sem=rsem2,
                    device_id=(peer, rep),
                    device_id_type=MESH,
                ).start()

            return carry

        lax.fori_loop(0, 16, send, 0)

    d0 = spread(0)
    finish(c_copies)
    g1[...] = (g0[rows_at(core, 2048), :].astype(f32) + in_c[0].astype(f32)).astype(bf16)
    y_copies = scatter(g1, in_y, 512, YS, y, y_peer, 1)
    finish(c_bias)
    y_bias = bias_round(bias_sum(bc, CORES), by, YS, y, y_peer, 1)
    d1 = spread(1)
    d2 = spread(2)
    to_feeds(0, d0)
    finish(y_copies)
    total = g1[rows_at(y, 512), :].astype(f32)
    for d in range(YS - 1):
        total = total + in_y[d].astype(f32)
    g2[...] = total.astype(bf16)
    z_copies = scatter(g2, in_z, 64, ZS, z, z_peer, 4)
    finish(y_bias)
    z_bias = bias_round(bias_sum(by, YS), bz, ZS, z, z_peer, 4)
    d3 = spread(3)
    to_feeds(1, d1)
    finish(z_copies)
    total = g2[rows_at(z, 64), :].astype(f32)
    for d in range(ZS - 1):
        total = total + in_z[d].astype(f32)
    g3[...] = total.astype(bf16)
    x_copies = scatter(g3, in_x, 16, REPS, rep, x_peer, 11)
    finish(z_bias)
    x_bias = bias_round(bias_sum(bz, ZS), bx, REPS, rep, x_peer, 11)
    to_feeds(2, d2)
    finish(x_copies)
    total = g3[rows_at(rep, 16), :].astype(f32)
    for d in range(REPS - 1):
        total = total + in_x[d].astype(f32)
    at_z = core * 2048 + y * 512 + z * 64
    full_ref[pl.ds(pl.multiple_of(at_z + rep * 16, 16), 16), :] = total.astype(bf16)
    copies = spread_out(at_z + rep * 16, 16, REPS, x_peer, 0)
    finish(x_bias)
    bias_total = bias_sum(bx, REPS)
    for c in range(4):
        bout_ref[:, c * 128 : (c + 1) * 128] = bias_total[c : c + 1, :]
    finish(copies)
    copies = spread_out(at_z, 64, ZS, z_peer, 3)
    to_feeds(3, d3)
    landing[own, :] = table2[own, :]
    finish(copies)
    copies = spread_out(core * 2048 + y * 512, 512, YS, y_peer, 10)
    tiles_done(me, rep, table2, landing, ssem2, rsem2).wait()
    turned = dot_nt(ident, landing[...]).astype(bf16)
    found = dot(turned, pick_ref[...])
    gradient = jnp.zeros((PART, REPORTS), f32)
    for s in range(4):
        gradient = gradient + jnp.where(within == float(s), found[s * PART : (s + 1) * PART, :], 0.0)
    eg_ref[...] = gradient
    finish(copies)
    finish(spread_out(core * 2048, 2048, CORES, core_peer, 13))
    for c in range(4):
        grads_ref[:, c * 128 : (c + 1) * 128] = full_ref[c * 1024 : (c + 1) * 1024, :]


def sds(shape, dtype):
    return jax.ShapeDtypeStruct(shape, dtype)


def on_device(
    embeddings, route, place, scales, first_weight, first_bias, second_weight, out_cotangent
):
    dma = pltpu.SemaphoreType.DMA
    vm = pltpu.VMEM
    in_vmem = pl.BlockSpec(memory_space=pltpu.VMEM)
    anywhere = pl.BlockSpec(memory_space=pl.ANY)
    gradient, grads, bias = pl.pallas_call(
        grid_kernel,
        out_shape=[sds((PART, REPORTS), f32), sds((1024, 512), bf16), sds((1, HID), f32)],
        in_specs=[
            in_vmem, in_vmem, in_vmem, pl.BlockSpec(memory_space=pltpu.SMEM),
            anywhere, in_vmem, anywhere, anywhere,
        ],
        out_specs=[in_vmem] * 3,
        scratch_shapes=[
            vm((ROWS, 128), bf16), vm((REPS, ROWS, 128), bf16), vm((ROWS, REPORTS), bf16),
            vm((512, HID), bf16), vm((HID, 512), bf16), vm((SUB, 512, NLON), bf16),
            vm((4, CH, ROWS), bf16), vm((128, ROWS), f32),
            vm((4, 16, ROWS), f32), vm((4, 8, ROWS), f32), vm((4, 16, ROWS), f32),
            vm((16, NLON, ROWS), bf16), vm((16, SUB, 16, ROWS), bf16), vm((16, 16, ROWS), bf16),
            vm((16, 8, ROWS), f32), vm((SUB * CH + 16, ROWS), bf16),
            vm((LEVELS, SUB * CH + 16, NLON), f32),
            vm((512, CELLS), bf16), vm((512, HID), bf16), vm((HID, 512), bf16), vm((HID, 1), f32),
            vm((HID, CELLS), bf16), vm((HID, CELLS), bf16), vm((LEVELS, SUB * CH, NLON), bf16),
            vm((4, REPS, 128, 256), bf16), vm((4, REPS - 1, 128, 256), bf16),
            vm((ROWS, 128), bf16), vm((ROWS, 128), bf16),
            vm((GROWS, 128), bf16), vm((2048, 128), bf16), vm((512, 128), bf16), vm((64, 128), bf16),
            vm((1, 2048, 128), bf16), vm((3, 512, 128), bf16), vm((7, 64, 128), bf16), vm((3, 16, 128), bf16),
            vm((GROWS, 128), bf16),
            vm((CORES, 8, 128), f32), vm((YS, 8, 128), f32), vm((ZS, 8, 128), f32), vm((REPS, 8, 128), f32),
            dma((3,)), dma, dma, dma, dma, dma((6,)), dma((6,)), dma((12,)), dma((12,)),
            dma((14,)), dma((14,)), dma((14,)), dma((14,)), dma((14,)), dma((14,)),
        ],
        compiler_params=pltpu.CompilerParams(
            collective_id=0, has_side_effects=True, vmem_limit_bytes=60 << 20
        ),
    )(
        embeddings, route.reshape(1, REPORTS), place, scales,
        first_weight, first_bias.reshape(1, HID), second_weight, out_cotangent.transpose(1, 0, 2),
    )
    return (
        gradient, grads[0:512].astype(f32), bias.reshape(HID), grads[512:1024].astype(f32),
    )


def solution(mesh):
    return jax.shard_map(
        on_device,
        mesh=mesh,
        in_specs=(
            P("rep", "band"),
            P("band", None),
            P(None, "band"),
            P(),
            P(),
            P(),
            P(),
            P(None, ("band", "rep"), None),
        ),
        out_specs=(P("rep", "band"), P(), P(), P()),
        check_vma=False,
    )
```

```python
import jax
import jax.numpy as jnp
from jax import lax
from jax.experimental import pallas as pl
from jax.experimental.pallas import tpu as pltpu
from jax.sharding import PartitionSpec as P

MESH = pl.DeviceIdType.MESH
bf16 = jnp.bfloat16
f32 = jnp.float32

root_two_pi = 0.7978845608028654
cubic = 0.044715
half_log2e = 0.8493218002880191

BANDS = 64
REPS = 4
YS, ZS, CORES = 4, 8, 2
CAP = 20
TILE = 16
ROWS = BANDS * TILE
REPORTS = 512
LEVELS = 4
CH = 128
PART = 32
SUB = 3
NLON = 256
LAT = 12.0
CELLS = SUB * NLON
HID = 512
GROWS = 4096


def iota(shape, dim):
    return lax.broadcasted_iota(jnp.int32, shape, dim)


def one_where(cond):
    return jnp.where(cond, 1.0, 0.0).astype(bf16)


def dot(a, b):
    return lax.dot_general(a, b, (((1,), (0,)), ((), ())), preferred_element_type=f32)


def dot_nt(a, b):
    return lax.dot_general(a, b, (((1,), (1,)), ((), ())), preferred_element_type=f32)


def eye(n):
    return one_where(iota((n, n), 0) == iota((n, n), 1))


def row_keys(start, rows):
    row = iota((rows, 1), 0) + start
    band = row >> 4
    ok = row & 15
    key = jnp.where(ok == 15, -1000, (band - 1) * 5 + ok).astype(f32)
    place_band = jnp.where(ok == 15, band, -1000).astype(f32)
    return key, place_band


def report_ranks(route_ref):
    owner = route_ref[...].astype(f32)
    rank = jnp.zeros((1, REPORTS), f32)
    for part in range(4):
        mine = iota((128, REPORTS), 0) + part * 128
        lane = iota((128, REPORTS), 1)
        col = jnp.sum(jnp.where(mine == lane, owner, 0.0), axis=1, keepdims=True)
        rank = rank + jnp.sum(
            jnp.where((col == owner) & (mine < lane), 1.0, 0.0), axis=0, keepdims=True
        )
    return owner, rank


def send_tiles(me, rep, table, landing, send_sem, recv_sem):
    def send(d, carry):
        peer = lax.rem(me + d, BANDS)
        pltpu.make_async_remote_copy(
            src_ref=table.at[pl.ds(pl.multiple_of(peer * TILE, TILE), TILE)],
            dst_ref=landing.at[pl.ds(pl.multiple_of(me * TILE, TILE), TILE)],
            send_sem=send_sem,
            recv_sem=recv_sem,
            device_id=(peer, rep),
            device_id_type=MESH,
        ).start()
        return carry

    lax.fori_loop(1, BANDS, send, 0)


def tiles_done(me, rep, table, landing, send_sem, recv_sem):
    return pltpu.make_async_remote_copy(
        src_ref=table.at[pl.ds(0, ROWS - TILE)],
        dst_ref=landing.at[pl.ds(0, ROWS - TILE)],
        send_sem=send_sem,
        recv_sem=recv_sem,
        device_id=(lax.rem(me + 1, BANDS), rep),
        device_id_type=MESH,
    )


def decode_places(t, rep, expand, base_ref, east_ref, valid_ref):
    lane = iota((1, ROWS), 1)
    ok = lane & 15
    o = (ok >= 5).astype(jnp.int32) + (ok >= 10).astype(jnp.int32) + (ok >= 15).astype(jnp.int32)
    k4 = (ok - 5 * o) * 4
    v = lax.rem(t + 2, 3) + o
    third = jnp.where(v >= 3, v - 3, v)
    code = third * 20 + k4
    lam = iota((64, ROWS), 0)
    low = expand[0:64, :]
    high = expand[64:128, :]
    count = jnp.sum(jnp.where(lam == third + 60, low, 0.0), axis=0, keepdims=True)
    offset = (1 - o).astype(f32) * LAT + (rep * SUB).astype(f32) + 0.5
    for s in range(4):
        hit = lam == code + s
        north = jnp.sum(jnp.where(hit, low, 0.0), axis=0, keepdims=True)
        east = jnp.sum(jnp.where(hit, high, 0.0), axis=0, keepdims=True)
        valid = jnp.where((ok < 15) & ((k4 + s).astype(f32) < count), 1.0, 0.0)
        base_ref[s] = jnp.broadcast_to(offset - north * LAT, (16, ROWS))
        valid_ref[s] = jnp.broadcast_to(valid, (16, ROWS))
        east_ref[s] = jnp.broadcast_to(east * float(NLON), (8, ROWS))


def build_table(emb_ref, place_ref, owner, rank, pick_ref, table):
    quad = jnp.floor(rank * 0.25)
    within = rank - 4.0 * quad
    key = owner * 5.0 + quad
    third = owner - 3.0 * jnp.floor((owner + 0.5) * (1.0 / 3.0))
    emb = emb_ref[...].astype(f32)
    emb_b = jnp.concatenate(
        [jnp.where(within == float(s), emb, 0.0) for s in range(4)], axis=0
    ).astype(bf16)
    lam = iota((128, REPORTS), 0).astype(f32)
    spot = third * 20.0 + rank
    north = place_ref[0:1, :].astype(f32)
    east = place_ref[1:2, :].astype(f32)
    place_b = (
        jnp.where(lam == spot, north, 0.0)
        + jnp.where(lam == spot + 64.0, east, 0.0)
        + jnp.where(lam == third + 60.0, 1.0, 0.0)
    ).astype(bf16)
    for part in range(8):
        rows = slice(part * 128, (part + 1) * 128)
        row_key, place_band = row_keys(part * 128, 128)
        pick = one_where(row_key == key)
        pick_ref[rows, :] = pick
        near = one_where(jnp.abs(place_band - owner) <= 1.0)
        table[rows, :] = (dot_nt(pick, emb_b) + dot_nt(near, place_b)).astype(bf16)
    return within


def kernels(it, scales_ref, base_ref, east_ref, valid_ref, col_ref, rk_ref, mix_ref, rowf_ref):
    s = it >> 2
    reach = scales_ref[it & 3] * LAT
    scale = half_log2e / jnp.full((1, 128), reach, f32)
    scale_wide = jnp.concatenate([scale] * 8, axis=1)
    east = east_ref[s, 0:1, :] * scale_wide
    for c in range(8):
        centre = (iota((32, 128), 0).astype(f32) + (c * 32 + 0.5)) * scale
        for b in range(8):
            gap = centre - east[:, b * 128 : (b + 1) * 128]
            col_ref[it, c * 32 : (c + 1) * 32, b * 128 : (b + 1) * 128] = jnp.exp2(
                -(gap * gap)
            ).astype(bf16)
    valid = valid_ref[s]
    wide = []
    for i in range(SUB):
        gap = (base_ref[s] + float(i)) * scale_wide
        row = (jnp.exp2(-(gap * gap)) * valid).astype(bf16)
        rk_ref[it, i] = row
        wide.append(row.astype(f32))
    sub = iota((16, ROWS), 0)
    mixed = jnp.where(
        sub == 0, wide[0], jnp.where(sub == 1, wide[1], jnp.where(sub == 2, wide[2], 0.0))
    )
    rowf_ref[it] = mixed[0:8, :]
    mix_ref[it] = mixed.astype(bf16)


def grid_kernel(
    emb_ref, route_ref, place_ref, scales_ref, w1_hbm, b1_ref, w2_hbm, cot_hbm,
    eg_ref, first_ref, second_ref, bout_ref,
    table, rr_ref, pick_ref, w1_ref, w2_ref, cot_ref,
    emb_t, expand, base_ref, east_ref, valid_ref, col_ref, rk_ref, mix_ref, rowf_ref, w_ref, acc_ref,
    feat_ref, w1p_ref, w1t_ref, bcol_ref, hid_ref, pg_ref, sg_ref,
    d_out, d_far, d_near, d_sum, d_last, table2, landing, g0, g1, g2, g3, in_c, in_z, in_x,
    y_far, y_near, y_sum, y_last, full_ref, bc, by, bz, bx, seen_y, seen_c,
    loads, ssem, rsem, ssem2, rsem2, xs, xr, ds, dr, gs, gr, bs, br, as_, ar,
):
    me = lax.axis_index("band")
    rep = lax.axis_index("rep")
    core = lax.rem(me, CORES)
    z = lax.rem(me // CORES, ZS)
    y = me // (CORES * ZS)

    def core_peer(d):
        return me + 1 - 2 * core, rep

    def y_peer(d):
        return lax.rem(y + d, YS) * (CORES * ZS) + z * CORES + core, rep

    def z_peer(d):
        return y * (CORES * ZS) + lax.rem(z + d, ZS) * CORES + core, rep

    def x_peer(d):
        return me, lax.rem(rep + d, REPS)

    def start(src, dst, send, recv, device):
        copy = pltpu.make_async_remote_copy(
            src_ref=src, dst_ref=dst, send_sem=send, recv_sem=recv, device_id=device, device_id_type=MESH
        )
        copy.start()
        return copy

    def rows_at(index, size):
        return pl.ds(pl.multiple_of(index * size, size), size)

    def scatter(src, dst, size, n, mine, peer, base):
        return [
            start(
                src.at[rows_at(lax.rem(mine + d, n), size)], dst.at[d - 1],
                gs.at[base + d - 1], gr.at[base + d - 1], peer(d),
            )
            for d in range(1, n)
        ]

    def bias_round(value, slots, n, mine, peer, base):
        slots[mine] = value
        return [
            start(slots.at[mine], slots.at[mine], bs.at[base + d - 1], br.at[base + d - 1], peer(d))
            for d in range(1, n)
        ]

    def bias_sum(slots, n):
        total = slots[0]
        for k in range(1, n):
            total = total + slots[k]
        return total

    def finish(copies):
        for copy in copies:
            copy.wait()

    def ring_reduce(chunk, bufs, sems, base, peer):
        send, recv = sems
        far, near = bufs[0], bufs[1]
        right, left = peer(1), peer(3)
        return [
            start(chunk(2, 0), far.at[0], send.at[base], recv.at[base], right),
            start(chunk(2, 1), far.at[1], send.at[base + 1], recv.at[base + 1], left),
            start(chunk(1, 1), near.at[0], send.at[base + 2], recv.at[base + 2], right),
            start(chunk(3, 0), near.at[1], send.at[base + 3], recv.at[base + 3], left),
        ]

    def ring_relay(copies, chunk, bufs, sems, base, peer):
        send, recv = sems
        far, out, last = bufs[0], bufs[2], bufs[3]
        relayed = []
        for h, k in ((0, 1), (1, 3)):
            copies[h].wait()
            out[h] = (chunk(k, h)[...].astype(f32) + far[h].astype(f32)).astype(bf16)
            relayed.append(start(out.at[h], last.at[h], send.at[base + 4 + h], recv.at[base + 4 + h], peer(k)))
        return copies[2:] + relayed

    def ring_total(copies, chunk, bufs):
        near, last = bufs[1], bufs[3]
        finish(copies)
        return [
            chunk(0, h)[...].astype(f32) + last[h].astype(f32) + near[1 - h].astype(f32) for h in range(2)
        ]

    def ring_gather(piece, sems, base, peer):
        send, recv = sems
        right, left = peer(1), peer(3)
        one = start(piece(0, 0), piece(0, 0), send.at[base], recv.at[base], right)
        two = start(piece(0, 1), piece(0, 1), send.at[base + 1], recv.at[base + 1], left)
        three = start(piece(0, 1), piece(0, 1), send.at[base + 2], recv.at[base + 2], right)
        four = start(piece(0, 0), piece(0, 0), send.at[base + 3], recv.at[base + 3], left)

        def forward():
            one.wait_recv()
            five = start(piece(3, 0), piece(3, 0), send.at[base + 4], recv.at[base + 4], right)
            two.wait_recv()
            six = start(piece(1, 1), piece(1, 1), send.at[base + 5], recv.at[base + 5], left)

            def rest():
                one.wait_send()
                two.wait_send()
                finish([three, four, five, six])

            return rest

        return forward

    def spread_out(offset, size, n, peer, base):
        at = pl.ds(pl.multiple_of(offset, size), size)
        return [
            start(full_ref.at[at], full_ref.at[at], as_.at[base + d - 1], ar.at[base + d - 1], peer(d))
            for d in range(1, n)
        ]

    barrier = pltpu.get_barrier_semaphore()
    lines = ((core_peer, CORES), (y_peer, YS), (z_peer, ZS), (x_peer, REPS))
    for peer, n in lines:
        for d in range(1, n):
            pl.semaphore_signal(barrier, inc=1, device_id=peer(d), device_id_type=MESH)
    held = []
    for k, (src, dst) in enumerate(((w1_hbm, w1_ref), (w2_hbm, w2_ref), (cot_hbm, cot_ref))):
        copy = pltpu.make_async_copy(src, dst, loads.at[k])
        copy.start()
        held.append(copy)

    owner, rank = report_ranks(route_ref)
    within = build_table(emb_ref, place_ref, owner, rank, pick_ref, table)
    pl.semaphore_wait(barrier, sum(n - 1 for _, n in lines))
    for d in range(1, YS):
        pl.semaphore_signal(seen_y, inc=1, device_id=y_peer(d), device_id_type=MESH)
    pl.semaphore_wait(seen_y, YS - 1)
    pl.semaphore_signal(seen_c, inc=1, device_id=core_peer(1), device_id_type=MESH)
    pl.semaphore_wait(seen_c, 1)
    mine = rr_ref.at[rep]
    send_tiles(me, rep, table, mine, ssem, rsem)
    own = rows_at(me, TILE)
    rr_ref[rep, own, :] = table[own, :]

    finish(held)
    r512 = iota((512, 512), 0)
    c512 = iota((512, 512), 1)
    w1p_ref[...] = dot(one_where(c512 == (r512 & 127) * 4 + (r512 >> 7)), w1_ref[...]).astype(bf16)
    w1t_ref[...] = dot_nt(eye(512), w1p_ref[...]).astype(bf16)
    bcol_ref[...] = jnp.sum(jnp.where(r512 == c512, b1_ref[...], 0.0), axis=1, keepdims=True)

    done = tiles_done(me, rep, table, mine, ssem, rsem)
    done.wait_recv()
    def report_piece(half):
        return lambda k, h: rr_ref.at[lax.rem(rep + k, REPS), pl.ds(half * 512 + h * 256, 256)]

    first_half = ring_gather(report_piece(0), (xs, xr), 0, x_peer)()
    forward_second = ring_gather(report_piece(1), (xs, xr), 6, x_peer)
    ident = eye(128)
    group = one_where(
        ((iota((128, 128), 0) >> 4) == (iota((128, 128), 1) >> 4)) & ((iota((128, 128), 0) & 15) == 15)
    )
    turned = dot_nt(ident, rr_ref[rep]).astype(bf16)
    for b in range(8):
        expand[:, b * 128 : (b + 1) * 128] = dot(turned[:, b * 128 : (b + 1) * 128], group)
    decode_places(me, rep, expand, base_ref, east_ref, valid_ref)
    acc_ref[...] = jnp.zeros_like(acc_ref)

    def make(it, carry):
        kernels(it, scales_ref, base_ref, east_ref, valid_ref, col_ref, rk_ref, mix_ref, rowf_ref)
        return carry

    lax.fori_loop(0, 8, make, 0)
    second_half = forward_second()
    lax.fori_loop(8, 16, make, 0)

    for half in range(2):
        lanes = slice(half * 512, (half + 1) * 512)
        (first_half, second_half)[half]()
        for q in range(REPS):
            turned = dot_nt(ident, rr_ref[q, lanes, :]).astype(bf16)
            for s in range(4):
                emb_t[s, q * PART : (q + 1) * PART, lanes] = turned[s * PART : (s + 1) * PART, :]

        def splat(it, carry):
            s = it >> 2
            level = it & 3
            rows = [rk_ref[it, i, :, lanes] for i in range(SUB)]
            w_ref[SUB * CH : SUB * CH + 16, lanes] = mix_ref[it, :, lanes]
            for c in range(8):
                e = emb_t[s, c * 16 : (c + 1) * 16, lanes]
                for i in range(SUB):
                    w_ref[i * CH + c * 16 : i * CH + (c + 1) * 16, lanes] = e * rows[i]
            acc_ref[level] += dot_nt(w_ref[:, lanes], col_ref[it, :, lanes])
            return carry

        lax.fori_loop(0, 16, splat, 0)
    done.wait_send()

    def inverse(level, i):
        return 1.0 / (acc_ref[level, SUB * CH + i : SUB * CH + i + 1, :] + 1.0)

    for level in range(LEVELS):
        for i in range(SUB):
            feat_ref[level * CH : (level + 1) * CH, i * NLON : (i + 1) * NLON] = (
                acc_ref[level, i * CH : (i + 1) * CH, :] * inverse(level, i)
            ).astype(bf16)

    for i in range(SUB):
        cells = slice(i * NLON, (i + 1) * NLON)
        for h in range(2):
            rows = slice(h * 256, (h + 1) * 256)
            pre = dot(w1t_ref[rows, :], feat_ref[:, cells]) + bcol_ref[rows, :]
            above = dot(w2_ref[rows, :], cot_ref[i])
            square = pre * pre
            tangent = jnp.tanh(root_two_pi * (pre + cubic * square * pre))
            hid_ref[rows, cells] = (0.5 * pre * (1.0 + tangent)).astype(bf16)
            slope = 0.5 * (1.0 + tangent) + 0.5 * pre * (1.0 - tangent * tangent) * root_two_pi * (
                1.0 + 3.0 * cubic * square
            )
            pg_ref[rows, cells] = (above * slope).astype(bf16)

    back = one_where(c512 == (r512 & 3) * 128 + (r512 >> 2))
    for h in range(2):
        rows = slice(h * 256, (h + 1) * 256)
        first = dot(back, dot_nt(feat_ref[...], pg_ref[rows, :]).astype(bf16)).astype(bf16)
        second = dot_nt(hid_ref[:, 0:NLON], cot_ref[0, rows, :])
        for i in range(1, SUB):
            second = second + dot_nt(hid_ref[:, i * NLON : (i + 1) * NLON], cot_ref[i, rows, :])
        second = second.astype(bf16)
        for c in range(2):
            at = (h * 2 + c) * 1024
            g0[at : at + 512, :] = first[:, c * 128 : (c + 1) * 128]
            g0[at + 512 : at + 1024, :] = second[:, c * 128 : (c + 1) * 128]
    bias = dot_nt(jnp.ones((16, CELLS), bf16), pg_ref[...])
    bias_tile = jnp.concatenate(
        [bias[0:1, c * 128 : (c + 1) * 128] for c in range(4)] + [jnp.zeros((4, 128), f32)], axis=0
    )
    c_copies = scatter(g0, in_c, 2048, CORES, core, core_peer, 0)
    c_bias = bias_round(bias_tile, bc, CORES, core, core_peer, 0)

    for i in range(SUB):
        grad = dot(w1p_ref[...], pg_ref[:, i * NLON : (i + 1) * NLON])
        for level in range(LEVELS):
            sg_ref[level, i * CH : (i + 1) * CH, :] = (
                grad[level * CH : (level + 1) * CH, :] * inverse(level, i)
            ).astype(bf16)

    def spread(n):
        lanes = slice(n * 256, (n + 1) * 256)

        def one_group(s, carry):
            total = None
            for level in range(LEVELS):
                it = s * 4 + level
                along = dot(sg_ref[level], col_ref[it, :, lanes])
                for i in range(SUB):
                    term = along[i * CH : (i + 1) * CH, :] * rowf_ref[it, i : i + 1, lanes]
                    total = term if total is None else total + term
            for q in range(REPS):
                d_out[n, q, rows_at(s, PART), :] = total[q * PART : (q + 1) * PART, :].astype(bf16)
            return carry

        lax.fori_loop(0, 4, one_group, 0)
        return ring_reduce(slot_part(n), slot_bufs(n), (ds, dr), n * 6, x_peer)

    def slot_part(n):
        return lambda k, h: d_out.at[n, lax.rem(rep + k, REPS), pl.ds(h * 64, 64)]

    def slot_bufs(n):
        return d_far.at[n], d_near.at[n], d_sum.at[n], d_last.at[n]

    def relay(n, copies):
        return ring_relay(copies, slot_part(n), slot_bufs(n), (ds, dr), n * 6, x_peer)

    def to_feeds(n, copies):
        halves = ring_total(copies, slot_part(n), slot_bufs(n))
        total = jnp.concatenate(halves, axis=0)
        table2[n * 256 : (n + 1) * 256, :] = jnp.transpose(total).astype(bf16)

        def send(j, carry):
            peer = n * 16 + lax.rem(j + me, 16)

            @pl.when(peer != me)
            def _():
                pltpu.make_async_remote_copy(
                    src_ref=table2.at[rows_at(peer, TILE)],
                    dst_ref=landing.at[rows_at(me, TILE)],
                    send_sem=ssem2,
                    recv_sem=rsem2,
                    device_id=(peer, rep),
                    device_id_type=MESH,
                ).start()

            return carry

        lax.fori_loop(0, 16, send, 0)

    def y_part(k, h):
        return g1.at[pl.ds(pl.multiple_of(lax.rem(y + k, YS) * 512 + h * 256, 256), 256)]

    y_bufs = (y_far, y_near, y_sum, y_last)

    finish(c_copies)
    g1[...] = (g0[rows_at(core, 2048), :].astype(f32) + in_c[0].astype(f32)).astype(bf16)
    y_copies = ring_reduce(y_part, y_bufs, (gs, gr), 1, y_peer)
    finish(c_bias)
    y_bias = bias_round(bias_sum(bc, CORES), by, YS, y, y_peer, 1)
    d0 = spread(0)
    y_copies = ring_relay(y_copies, y_part, y_bufs, (gs, gr), 1, y_peer)
    d1 = spread(1)
    d0 = relay(0, d0)
    y_sums = ring_total(y_copies, y_part, y_bufs)
    for h in range(2):
        g2[h * 256 : (h + 1) * 256, :] = y_sums[h].astype(bf16)
    z_copies = scatter(g2, in_z, 64, ZS, z, z_peer, 7)
    finish(y_bias)
    z_bias = bias_round(bias_sum(by, YS), bz, ZS, z, z_peer, 4)
    d2 = spread(2)
    d1 = relay(1, d1)
    to_feeds(0, d0)
    d3 = spread(3)
    d2 = relay(2, d2)
    to_feeds(1, d1)
    finish(z_copies)
    total = g2[rows_at(z, 64), :].astype(f32)
    for d in range(ZS - 1):
        total = total + in_z[d].astype(f32)
    g3[...] = total.astype(bf16)
    x_copies = scatter(g3, in_x, 16, REPS, rep, x_peer, 14)
    d3 = relay(3, d3)
    finish(z_bias)
    x_bias = bias_round(bias_sum(bz, ZS), bx, REPS, rep, x_peer, 11)
    to_feeds(2, d2)
    finish(x_copies)
    total = g3[rows_at(rep, 16), :].astype(f32)
    for d in range(REPS - 1):
        total = total + in_x[d].astype(f32)
    at_z = core * 2048 + y * 512 + z * 64
    full_ref[pl.ds(pl.multiple_of(at_z + rep * 16, 16), 16), :] = total.astype(bf16)
    copies = spread_out(at_z + rep * 16, 16, REPS, x_peer, 0)
    finish(x_bias)
    bias_total = bias_sum(bx, REPS)
    for c in range(4):
        bout_ref[:, c * 128 : (c + 1) * 128] = bias_total[c : c + 1, :]
    finish(copies)
    copies = spread_out(at_z, 64, ZS, z_peer, 3)
    to_feeds(3, d3)
    landing[own, :] = table2[own, :]
    finish(copies)

    def y_block(k, h):
        at = core * 2048 + lax.rem(y + k, YS) * 512 + h * 256
        return full_ref.at[pl.ds(pl.multiple_of(at, 256), 256)]

    y_gathered = ring_gather(y_block, (as_, ar), 10, y_peer)()
    tiles_done(me, rep, table2, landing, ssem2, rsem2).wait()
    turned = dot_nt(ident, landing[...]).astype(bf16)
    found = dot(turned, pick_ref[...])
    gradient = jnp.zeros((PART, REPORTS), f32)
    for s in range(4):
        gradient = gradient + jnp.where(within == float(s), found[s * PART : (s + 1) * PART, :], 0.0)
    eg_ref[...] = gradient
    y_gathered()
    finish(spread_out(core * 2048, 2048, CORES, core_peer, 16))
    for c in range(4):
        lanes = slice(c * 128, (c + 1) * 128)
        first_ref[:, lanes] = full_ref[c * 1024 : c * 1024 + 512, :].astype(f32)
        second_ref[:, lanes] = full_ref[c * 1024 + 512 : (c + 1) * 1024, :].astype(f32)


def sds(shape, dtype):
    return jax.ShapeDtypeStruct(shape, dtype)


def on_device(
    embeddings, route, place, scales, first_weight, first_bias, second_weight, out_cotangent
):
    dma = pltpu.SemaphoreType.DMA
    vm = pltpu.VMEM
    in_vmem = pl.BlockSpec(memory_space=pltpu.VMEM)
    anywhere = pl.BlockSpec(memory_space=pl.ANY)
    gradient, first, second, bias = pl.pallas_call(
        grid_kernel,
        out_shape=[sds((PART, REPORTS), f32), sds((512, 512), f32), sds((512, 512), f32), sds((1, HID), f32)],
        in_specs=[
            in_vmem, in_vmem, in_vmem, pl.BlockSpec(memory_space=pltpu.SMEM),
            anywhere, in_vmem, anywhere, anywhere,
        ],
        out_specs=[in_vmem] * 4,
        scratch_shapes=[
            vm((ROWS, 128), bf16), vm((REPS, ROWS, 128), bf16), vm((ROWS, REPORTS), bf16),
            vm((512, HID), bf16), vm((HID, 512), bf16), vm((SUB, 512, NLON), bf16),
            vm((4, CH, ROWS), bf16), vm((128, ROWS), f32),
            vm((4, 16, ROWS), f32), vm((4, 8, ROWS), f32), vm((4, 16, ROWS), f32),
            vm((16, NLON, ROWS), bf16), vm((16, SUB, 16, ROWS), bf16), vm((16, 16, ROWS), bf16),
            vm((16, 8, ROWS), f32), vm((SUB * CH + 16, ROWS), bf16),
            vm((LEVELS, SUB * CH + 16, NLON), f32),
            vm((512, CELLS), bf16), vm((512, HID), bf16), vm((HID, 512), bf16), vm((HID, 1), f32),
            vm((HID, CELLS), bf16), vm((HID, CELLS), bf16), vm((LEVELS, SUB * CH, NLON), bf16),
            vm((4, REPS, 128, 256), bf16), *([vm((4, 2, 64, 256), bf16)] * 4),
            vm((ROWS, 128), bf16), vm((ROWS, 128), bf16),
            vm((GROWS, 128), bf16), vm((2048, 128), bf16), vm((512, 128), bf16), vm((64, 128), bf16),
            vm((1, 2048, 128), bf16), vm((7, 64, 128), bf16), vm((3, 16, 128), bf16),
            *([vm((2, 256, 128), bf16)] * 4),
            vm((GROWS, 128), bf16),
            vm((CORES, 8, 128), f32), vm((YS, 8, 128), f32), vm((ZS, 8, 128), f32), vm((REPS, 8, 128), f32),
            pltpu.SemaphoreType.REGULAR, pltpu.SemaphoreType.REGULAR,
            dma((3,)), dma, dma, dma, dma, dma((12,)), dma((12,)), dma((24,)), dma((24,)),
            dma((17,)), dma((17,)), dma((14,)), dma((14,)), dma((17,)), dma((17,)),
        ],
        compiler_params=pltpu.CompilerParams(
            collective_id=0, has_side_effects=True, vmem_limit_bytes=60 << 20
        ),
    )(
        embeddings, route.reshape(1, REPORTS), place, scales,
        first_weight, first_bias.reshape(1, HID), second_weight, out_cotangent.transpose(1, 0, 2),
    )
    return (gradient, first, bias.reshape(HID), second)


def solution(mesh):
    return jax.shard_map(
        on_device,
        mesh=mesh,
        in_specs=(
            P("rep", "band"),
            P("band", None),
            P(None, "band"),
            P(),
            P(),
            P(),
            P(),
            P(None, ("band", "rep"), None),
        ),
        out_specs=(P("rep", "band"), P(), P(), P()),
        check_vma=False,
    )
```

```python
import jax
import jax.numpy as jnp
from jax import lax
from jax.experimental import pallas as pl
from jax.experimental.pallas import tpu as pltpu
from jax.sharding import PartitionSpec as P

MESH = pl.DeviceIdType.MESH
bf16 = jnp.bfloat16
f32 = jnp.float32

root_two_pi = 0.7978845608028654
cubic = 0.044715
half_log2e = 0.8493218002880191

BANDS = 64
REPS = 4
YS, ZS, CORES = 4, 8, 2
CAP = 20
TILE = 16
ROWS = BANDS * TILE
REPORTS = 512
LEVELS = 4
CH = 128
PART = 32
SUB = 3
NLON = 256
LAT = 12.0
CELLS = SUB * NLON
HID = 512
GROWS = 4096


def iota(shape, dim):
    return lax.broadcasted_iota(jnp.int32, shape, dim)


def one_where(cond):
    return jnp.where(cond, 1.0, 0.0).astype(bf16)


def dot(a, b):
    return lax.dot_general(a, b, (((1,), (0,)), ((), ())), preferred_element_type=f32)


def dot_nt(a, b):
    return lax.dot_general(a, b, (((1,), (1,)), ((), ())), preferred_element_type=f32)


def eye(n):
    return one_where(iota((n, n), 0) == iota((n, n), 1))


def row_keys(start, rows):
    row = iota((rows, 1), 0) + start
    band = row >> 4
    ok = row & 15
    key = jnp.where(ok == 15, -1000, (band - 1) * 5 + ok).astype(f32)
    place_band = jnp.where(ok == 15, band, -1000).astype(f32)
    return key, place_band


def report_ranks(route_ref):
    owner = route_ref[...].astype(f32)
    rank = jnp.zeros((1, REPORTS), f32)
    for part in range(4):
        mine = iota((128, REPORTS), 0) + part * 128
        lane = iota((128, REPORTS), 1)
        col = jnp.sum(jnp.where(mine == lane, owner, 0.0), axis=1, keepdims=True)
        rank = rank + jnp.sum(
            jnp.where((col == owner) & (mine < lane), 1.0, 0.0), axis=0, keepdims=True
        )
    return owner, rank


def greet(me, rep):
    barrier = pltpu.get_barrier_semaphore()

    def band_peer(d, carry):
        pl.semaphore_signal(
            barrier, inc=1, device_id=(lax.rem(me + d, BANDS), rep), device_id_type=MESH
        )
        return carry

    lax.fori_loop(1, BANDS, band_peer, 0)
    for d in range(1, REPS):
        pl.semaphore_signal(
            barrier, inc=1, device_id=(me, lax.rem(rep + d, REPS)), device_id_type=MESH
        )
    return barrier


def send_tiles(me, rep, table, landing, send_sem, recv_sem):
    def send(d, carry):
        peer = lax.rem(me + d, BANDS)
        pltpu.make_async_remote_copy(
            src_ref=table.at[pl.ds(pl.multiple_of(peer * TILE, TILE), TILE)],
            dst_ref=landing.at[pl.ds(pl.multiple_of(me * TILE, TILE), TILE)],
            send_sem=send_sem,
            recv_sem=recv_sem,
            device_id=(peer, rep),
            device_id_type=MESH,
        ).start()
        return carry

    lax.fori_loop(1, BANDS, send, 0)


def tiles_done(me, rep, table, landing, send_sem, recv_sem):
    return pltpu.make_async_remote_copy(
        src_ref=table.at[pl.ds(0, ROWS - TILE)],
        dst_ref=landing.at[pl.ds(0, ROWS - TILE)],
        send_sem=send_sem,
        recv_sem=recv_sem,
        device_id=(lax.rem(me + 1, BANDS), rep),
        device_id_type=MESH,
    )


def decode_places(t, rep, expand, base_ref, east_ref, valid_ref):
    lane = iota((1, ROWS), 1)
    ok = lane & 15
    o = (ok >= 5).astype(jnp.int32) + (ok >= 10).astype(jnp.int32) + (ok >= 15).astype(jnp.int32)
    k4 = (ok - 5 * o) * 4
    v = lax.rem(t + 2, 3) + o
    third = jnp.where(v >= 3, v - 3, v)
    code = third * 20 + k4
    lam = iota((64, ROWS), 0)
    low = expand[0:64, :]
    high = expand[64:128, :]
    count = jnp.sum(jnp.where(lam == third + 60, low, 0.0), axis=0, keepdims=True)
    offset = (1 - o).astype(f32) * LAT + (rep * SUB).astype(f32) + 0.5
    for s in range(4):
        hit = lam == code + s
        north = jnp.sum(jnp.where(hit, low, 0.0), axis=0, keepdims=True)
        east = jnp.sum(jnp.where(hit, high, 0.0), axis=0, keepdims=True)
        valid = jnp.where((ok < 15) & ((k4 + s).astype(f32) < count), 1.0, 0.0)
        base_ref[s] = jnp.broadcast_to(offset - north * LAT, (16, ROWS))
        valid_ref[s] = jnp.broadcast_to(valid, (16, ROWS))
        east_ref[s] = jnp.broadcast_to(east * float(NLON), (8, ROWS))


def build_table(emb_ref, place_ref, owner, rank, pick_ref, table):
    quad = jnp.floor(rank * 0.25)
    within = rank - 4.0 * quad
    key = owner * 5.0 + quad
    third = owner - 3.0 * jnp.floor((owner + 0.5) * (1.0 / 3.0))
    emb = emb_ref[...].astype(f32)
    emb_b = jnp.concatenate(
        [jnp.where(within == float(s), emb, 0.0) for s in range(4)], axis=0
    ).astype(bf16)
    lam = iota((128, REPORTS), 0).astype(f32)
    spot = third * 20.0 + rank
    north = place_ref[0:1, :].astype(f32)
    east = place_ref[1:2, :].astype(f32)
    place_b = (
        jnp.where(lam == spot, north, 0.0)
        + jnp.where(lam == spot + 64.0, east, 0.0)
        + jnp.where(lam == third + 60.0, 1.0, 0.0)
    ).astype(bf16)
    for part in range(8):
        rows = slice(part * 128, (part + 1) * 128)
        row_key, place_band = row_keys(part * 128, 128)
        pick = one_where(row_key == key)
        pick_ref[rows, :] = pick
        near = one_where(jnp.abs(place_band - owner) <= 1.0)
        table[rows, :] = (dot_nt(pick, emb_b) + dot_nt(near, place_b)).astype(bf16)
    return within


def kernels(it, scales_ref, base_ref, east_ref, valid_ref, col_ref, rk_ref, mix_ref, rowf_ref):
    s = it >> 2
    reach = scales_ref[it & 3] * LAT
    scale = half_log2e / jnp.full((1, 128), reach, f32)
    scale_wide = jnp.concatenate([scale] * 8, axis=1)
    east = east_ref[s, 0:1, :] * scale_wide
    for c in range(8):
        centre = (iota((32, 128), 0).astype(f32) + (c * 32 + 0.5)) * scale
        for b in range(8):
            gap = centre - east[:, b * 128 : (b + 1) * 128]
            col_ref[it, c * 32 : (c + 1) * 32, b * 128 : (b + 1) * 128] = jnp.exp2(
                -(gap * gap)
            ).astype(bf16)
    valid = valid_ref[s]
    wide = []
    for i in range(SUB):
        gap = (base_ref[s] + float(i)) * scale_wide
        row = (jnp.exp2(-(gap * gap)) * valid).astype(bf16)
        rk_ref[it, i] = row
        wide.append(row.astype(f32))
    sub = iota((16, ROWS), 0)
    mixed = jnp.where(
        sub == 0, wide[0], jnp.where(sub == 1, wide[1], jnp.where(sub == 2, wide[2], 0.0))
    )
    rowf_ref[it] = mixed[0:8, :]
    mix_ref[it] = mixed.astype(bf16)


def grid_kernel(
    emb_ref, route_ref, place_ref, scales_ref, w1_hbm, b1_ref, w2_hbm, cot_hbm,
    eg_ref, grads_ref, bout_ref,
    table, rr_ref, pick_ref, w1_ref, w2_ref, cot_ref,
    emb_t, expand, base_ref, east_ref, valid_ref, col_ref, rk_ref, mix_ref, rowf_ref, w_ref, acc_ref,
    feat_ref, w1p_ref, w1t_ref, bcol_ref, hid_ref, pg_ref, sg_ref,
    d_out, d_in, table2, landing, g0, g1, g2, in_c, in_y, in_g, full_ref, bc, by, bz, bx,
    loads, ssem, rsem, ssem2, rsem2, vs, vr, vs2, vr2, xs, xr, ds, dr, gs, gr, bs, br, as_, ar,
):
    me = lax.axis_index("band")
    rep = lax.axis_index("rep")
    core = lax.rem(me, CORES)
    z = lax.rem(me // CORES, ZS)
    y = me // (CORES * ZS)

    def core_peer(d):
        return me + 1 - 2 * core, rep

    def y_peer(d):
        return lax.rem(y + d, YS) * (CORES * ZS) + z * CORES + core, rep

    def z_peer(d):
        return y * (CORES * ZS) + lax.rem(z + d, ZS) * CORES + core, rep

    def x_peer(d):
        return me, lax.rem(rep + d, REPS)

    def start(src, dst, send, recv, device):
        copy = pltpu.make_async_remote_copy(
            src_ref=src, dst_ref=dst, send_sem=send, recv_sem=recv, device_id=device, device_id_type=MESH
        )
        copy.start()
        return copy

    def rows_at(index, size):
        return pl.ds(pl.multiple_of(index * size, size), size)

    def bias_round(value, slots, n, mine, peer, base):
        slots[mine] = value
        return [
            start(slots.at[mine], slots.at[mine], bs.at[base + d - 1], br.at[base + d - 1], peer(d))
            for d in range(1, n)
        ]

    def bias_sum(slots, n):
        total = slots[0]
        for k in range(1, n):
            total = total + slots[k]
        return total

    def finish(copies):
        for copy in copies:
            copy.wait()

    def ring_gather(piece, sems, base, peer):
        send, recv = sems
        right, left = peer(1), peer(3)
        one = start(piece(0, 0), piece(0, 0), send.at[base], recv.at[base], right)
        two = start(piece(0, 1), piece(0, 1), send.at[base + 1], recv.at[base + 1], left)
        three = start(piece(0, 1), piece(0, 1), send.at[base + 2], recv.at[base + 2], right)
        four = start(piece(0, 0), piece(0, 0), send.at[base + 3], recv.at[base + 3], left)

        def forward():
            one.wait_recv()
            five = start(piece(3, 0), piece(3, 0), send.at[base + 4], recv.at[base + 4], right)
            two.wait_recv()
            six = start(piece(1, 1), piece(1, 1), send.at[base + 5], recv.at[base + 5], left)

            def rest():
                one.wait_send()
                two.wait_send()
                finish([three, four, five, six])

            return rest

        return forward

    group_at = z * REPS + rep

    def group_peer(j):
        return y * (CORES * ZS) + (j >> 2) * CORES + core, j & 3

    def to_group(src, src_at, dst, dst_at, send, recv):
        def one(d, carry):
            j = lax.rem(group_at + d, ZS * REPS)
            pltpu.make_async_remote_copy(
                src_ref=src.at[pl.ds(pl.multiple_of(src_at(j), TILE), TILE)],
                dst_ref=dst.at[pl.ds(pl.multiple_of(dst_at, TILE), TILE)],
                send_sem=send, recv_sem=recv, device_id=group_peer(j), device_id_type=MESH,
            ).start()
            return carry

        lax.fori_loop(1, ZS * REPS, one, 0)
        rows = pl.ds(0, (ZS * REPS - 1) * TILE)
        return pltpu.make_async_remote_copy(
            src_ref=src.at[rows], dst_ref=dst.at[rows], send_sem=send, recv_sem=recv,
            device_id=group_peer(lax.rem(group_at + 1, ZS * REPS)), device_id_type=MESH,
        )

    barrier = greet(me, rep)
    held = []
    for k, (src, dst) in enumerate(((w1_hbm, w1_ref), (w2_hbm, w2_ref), (cot_hbm, cot_ref))):
        copy = pltpu.make_async_copy(src, dst, loads.at[k])
        copy.start()
        held.append(copy)

    owner, rank = report_ranks(route_ref)
    within = build_table(emb_ref, place_ref, owner, rank, pick_ref, table)
    pl.semaphore_wait(barrier, BANDS - 1 + REPS - 1)
    mine = rr_ref.at[rep]
    send_tiles(me, rep, table, mine, ssem, rsem)
    own = rows_at(me, TILE)
    rr_ref[rep, own, :] = table[own, :]

    finish(held)
    r512 = iota((512, 512), 0)
    c512 = iota((512, 512), 1)
    w1p_ref[...] = dot(one_where(c512 == (r512 & 127) * 4 + (r512 >> 7)), w1_ref[...]).astype(bf16)
    w1t_ref[...] = dot_nt(eye(512), w1p_ref[...]).astype(bf16)
    bcol_ref[...] = jnp.sum(jnp.where(r512 == c512, b1_ref[...], 0.0), axis=1, keepdims=True)

    done = tiles_done(me, rep, table, mine, ssem, rsem)
    done.wait_recv()
    def report_piece(half):
        return lambda k, h: rr_ref.at[lax.rem(rep + k, REPS), pl.ds(half * 512 + h * 256, 256)]

    first_half = ring_gather(report_piece(0), (xs, xr), 0, x_peer)()
    forward_second = ring_gather(report_piece(1), (xs, xr), 6, x_peer)
    ident = eye(128)
    group = one_where(
        ((iota((128, 128), 0) >> 4) == (iota((128, 128), 1) >> 4)) & ((iota((128, 128), 0) & 15) == 15)
    )
    turned = dot_nt(ident, rr_ref[rep]).astype(bf16)
    for b in range(8):
        expand[:, b * 128 : (b + 1) * 128] = dot(turned[:, b * 128 : (b + 1) * 128], group)
    decode_places(me, rep, expand, base_ref, east_ref, valid_ref)
    acc_ref[...] = jnp.zeros_like(acc_ref)

    def make(it, carry):
        kernels(it, scales_ref, base_ref, east_ref, valid_ref, col_ref, rk_ref, mix_ref, rowf_ref)
        return carry

    lax.fori_loop(0, 8, make, 0)
    second_half = forward_second()
    lax.fori_loop(8, 16, make, 0)

    for half in range(2):
        lanes = slice(half * 512, (half + 1) * 512)
        (first_half, second_half)[half]()
        for q in range(REPS):
            turned = dot_nt(ident, rr_ref[q, lanes, :]).astype(bf16)
            for s in range(4):
                emb_t[s, q * PART : (q + 1) * PART, lanes] = turned[s * PART : (s + 1) * PART, :]

        def splat(it, carry):
            s = it >> 2
            level = it & 3
            rows = [rk_ref[it, i, :, lanes] for i in range(SUB)]
            w_ref[SUB * CH : SUB * CH + 16, lanes] = mix_ref[it, :, lanes]
            for c in range(8):
                e = emb_t[s, c * 16 : (c + 1) * 16, lanes]
                for i in range(SUB):
                    w_ref[i * CH + c * 16 : i * CH + (c + 1) * 16, lanes] = e * rows[i]
            acc_ref[level] += dot_nt(w_ref[:, lanes], col_ref[it, :, lanes])
            return carry

        lax.fori_loop(0, 16, splat, 0)
    done.wait_send()

    def inverse(level, i):
        return 1.0 / (acc_ref[level, SUB * CH + i : SUB * CH + i + 1, :] + 1.0)

    for level in range(LEVELS):
        for i in range(SUB):
            feat_ref[level * CH : (level + 1) * CH, i * NLON : (i + 1) * NLON] = (
                acc_ref[level, i * CH : (i + 1) * CH, :] * inverse(level, i)
            ).astype(bf16)

    for i in range(SUB):
        cells = slice(i * NLON, (i + 1) * NLON)
        for h in range(2):
            rows = slice(h * 256, (h + 1) * 256)
            pre = dot(w1t_ref[rows, :], feat_ref[:, cells]) + bcol_ref[rows, :]
            above = dot(w2_ref[rows, :], cot_ref[i])
            square = pre * pre
            tangent = jnp.tanh(root_two_pi * (pre + cubic * square * pre))
            hid_ref[rows, cells] = (0.5 * pre * (1.0 + tangent)).astype(bf16)
            slope = 0.5 * (1.0 + tangent) + 0.5 * pre * (1.0 - tangent * tangent) * root_two_pi * (
                1.0 + 3.0 * cubic * square
            )
            pg_ref[rows, cells] = (above * slope).astype(bf16)

    back = one_where(c512 == (r512 & 3) * 128 + (r512 >> 2))
    for h in range(2):
        rows = slice(h * 256, (h + 1) * 256)
        first = dot(back, dot_nt(feat_ref[...], pg_ref[rows, :]).astype(bf16)).astype(bf16)
        second = dot_nt(hid_ref[:, 0:NLON], cot_ref[0, rows, :])
        for i in range(1, SUB):
            second = second + dot_nt(hid_ref[:, i * NLON : (i + 1) * NLON], cot_ref[i, rows, :])
        second = second.astype(bf16)
        for c in range(2):
            at = (h * 2 + c) * 1024
            g0[at : at + 512, :] = first[:, c * 128 : (c + 1) * 128]
            g0[at + 512 : at + 1024, :] = second[:, c * 128 : (c + 1) * 128]
    bias = dot_nt(jnp.ones((16, CELLS), bf16), pg_ref[...])
    bias_tile = jnp.concatenate(
        [bias[0:1, c * 128 : (c + 1) * 128] for c in range(4)] + [jnp.zeros((4, 128), f32)], axis=0
    )
    c_copies = []
    for d in (1, 2, 3, 0):
        k = lax.rem(y + d, YS)
        c_copies.append(
            start(g0.at[rows_at((1 - core) * YS + k, 512)], in_c.at[rows_at(k, 512)], gs.at[d], gr.at[d], core_peer(1))
        )
    c_bias = bias_round(bias_tile, bc, CORES, core, core_peer, 0)

    for i in range(SUB):
        grad = dot(w1p_ref[...], pg_ref[:, i * NLON : (i + 1) * NLON])
        for level in range(LEVELS):
            sg_ref[level, i * CH : (i + 1) * CH, :] = (
                grad[level * CH : (level + 1) * CH, :] * inverse(level, i)
            ).astype(bf16)

    def spread(n):
        lanes = slice(n * 256, (n + 1) * 256)

        def one_group(s, carry):
            total = None
            for level in range(LEVELS):
                it = s * 4 + level
                along = dot(sg_ref[level], col_ref[it, :, lanes])
                for i in range(SUB):
                    term = along[i * CH : (i + 1) * CH, :] * rowf_ref[it, i : i + 1, lanes]
                    total = term if total is None else total + term
            for q in range(REPS):
                d_out[n, q, rows_at(s, PART), :] = total[q * PART : (q + 1) * PART, :].astype(bf16)
            return carry

        lax.fori_loop(0, 4, one_group, 0)
        return [
            start(
                d_out.at[n, lax.rem(rep + d, REPS)], d_in.at[n, d - 1],
                ds.at[n * 3 + d - 1], dr.at[n * 3 + d - 1], x_peer(d),
            )
            for d in range(1, REPS)
        ]

    def to_feeds(n, copies):
        finish(copies)
        total = d_out[n, rep].astype(f32)
        for d in range(REPS - 1):
            total = total + d_in[n, d].astype(f32)
        table2[n * 256 : (n + 1) * 256, :] = jnp.transpose(total).astype(bf16)

        def send(j, carry):
            peer = n * 16 + lax.rem(j + me, 16)

            @pl.when(peer != me)
            def _():
                pltpu.make_async_remote_copy(
                    src_ref=table2.at[rows_at(peer, TILE)],
                    dst_ref=landing.at[rows_at(me, TILE)],
                    send_sem=ssem2,
                    recv_sem=rsem2,
                    device_id=(peer, rep),
                    device_id_type=MESH,
                ).start()

            return carry

        lax.fori_loop(0, 16, send, 0)

    d0 = spread(0)
    y_copies = []
    for d, copy in zip((1, 2, 3, 0), c_copies):
        k = lax.rem(y + d, YS)
        copy.wait()
        g1[rows_at(k, 512), :] = (
            g0[rows_at(core * YS + k, 512), :].astype(f32) + in_c[rows_at(k, 512), :].astype(f32)
        ).astype(bf16)
        if d:
            y_copies.append(start(g1.at[rows_at(k, 512)], in_y.at[d - 1], gs.at[3 + d], gr.at[3 + d], y_peer(d)))
    finish(c_bias)
    y_bias = bias_round(bias_sum(bc, CORES), by, YS, y, y_peer, 1)
    d1 = spread(1)
    d2 = spread(2)
    finish(y_copies)
    total = g1[rows_at(y, 512), :].astype(f32)
    for d in range(YS - 1):
        total = total + in_y[d].astype(f32)
    g2[...] = total.astype(bf16)
    own_tile = rows_at(group_at, TILE)
    in_g[own_tile, :] = g2[own_tile, :]
    scattered = to_group(g2, lambda j: j * TILE, in_g, group_at * TILE, vs, vr)
    finish(y_bias)
    z_bias = bias_round(bias_sum(by, YS), bz, ZS, z, z_peer, 4)
    to_feeds(0, d0)
    d3 = spread(3)
    scattered.wait()
    total = in_g[0:TILE, :].astype(f32)
    for j in range(1, ZS * REPS):
        total = total + in_g[j * TILE : (j + 1) * TILE, :].astype(f32)
    block_at = core * 2048 + y * 512
    full_ref[pl.ds(pl.multiple_of(block_at + group_at * TILE, TILE), TILE), :] = total.astype(bf16)
    gathered = to_group(
        full_ref, lambda j: block_at + group_at * TILE, full_ref, block_at + group_at * TILE, vs2, vr2
    )
    to_feeds(1, d1)
    finish(z_bias)
    x_bias = bias_round(bias_sum(bz, ZS), bx, REPS, rep, x_peer, 11)
    to_feeds(2, d2)
    gathered.wait()

    def block(k):
        return full_ref.at[rows_at(core * YS + k, 512)]

    def to_core(d):
        k = lax.rem(y + YS - d, YS)
        return start(block(k), block(k), as_.at[3 + d], ar.at[3 + d], core_peer(1))

    blocks = [start(block(y), block(y), as_.at[d - 1], ar.at[d - 1], y_peer(d)) for d in range(1, YS)]
    crossing = [to_core(0)]
    to_feeds(3, d3)
    landing[own, :] = table2[own, :]
    finish(x_bias)
    bias_total = bias_sum(bx, REPS)
    for c in range(4):
        bout_ref[:, c * 128 : (c + 1) * 128] = bias_total[c : c + 1, :]
    for d in (1, 3, 2):
        blocks[d - 1].wait()
        crossing.append(to_core(d))
    tiles_done(me, rep, table2, landing, ssem2, rsem2).wait()
    turned = dot_nt(ident, landing[...]).astype(bf16)
    found = dot(turned, pick_ref[...])
    gradient = jnp.zeros((PART, REPORTS), f32)
    for s in range(4):
        gradient = gradient + jnp.where(within == float(s), found[s * PART : (s + 1) * PART, :], 0.0)
    eg_ref[...] = gradient
    finish(crossing)
    for c in range(4):
        grads_ref[:, c * 128 : (c + 1) * 128] = full_ref[c * 1024 : (c + 1) * 1024, :]


def sds(shape, dtype):
    return jax.ShapeDtypeStruct(shape, dtype)


def on_device(
    embeddings, route, place, scales, first_weight, first_bias, second_weight, out_cotangent
):
    dma = pltpu.SemaphoreType.DMA
    vm = pltpu.VMEM
    in_vmem = pl.BlockSpec(memory_space=pltpu.VMEM)
    anywhere = pl.BlockSpec(memory_space=pl.ANY)
    gradient, grads, bias = pl.pallas_call(
        grid_kernel,
        out_shape=[sds((PART, REPORTS), f32), sds((1024, 512), bf16), sds((1, HID), f32)],
        in_specs=[
            in_vmem, in_vmem, in_vmem, pl.BlockSpec(memory_space=pltpu.SMEM),
            anywhere, in_vmem, anywhere, anywhere,
        ],
        out_specs=[in_vmem] * 3,
        scratch_shapes=[
            vm((ROWS, 128), bf16), vm((REPS, ROWS, 128), bf16), vm((ROWS, REPORTS), bf16),
            vm((512, HID), bf16), vm((HID, 512), bf16), vm((SUB, 512, NLON), bf16),
            vm((4, CH, ROWS), bf16), vm((128, ROWS), f32),
            vm((4, 16, ROWS), f32), vm((4, 8, ROWS), f32), vm((4, 16, ROWS), f32),
            vm((16, NLON, ROWS), bf16), vm((16, SUB, 16, ROWS), bf16), vm((16, 16, ROWS), bf16),
            vm((16, 8, ROWS), f32), vm((SUB * CH + 16, ROWS), bf16),
            vm((LEVELS, SUB * CH + 16, NLON), f32),
            vm((512, CELLS), bf16), vm((512, HID), bf16), vm((HID, 512), bf16), vm((HID, 1), f32),
            vm((HID, CELLS), bf16), vm((HID, CELLS), bf16), vm((LEVELS, SUB * CH, NLON), bf16),
            vm((4, REPS, 128, 256), bf16), vm((4, REPS - 1, 128, 256), bf16),
            vm((ROWS, 128), bf16), vm((ROWS, 128), bf16),
            vm((GROWS, 128), bf16), vm((2048, 128), bf16), vm((512, 128), bf16),
            vm((2048, 128), bf16), vm((3, 512, 128), bf16), vm((512, 128), bf16),
            vm((GROWS, 128), bf16),
            vm((CORES, 8, 128), f32), vm((YS, 8, 128), f32), vm((ZS, 8, 128), f32), vm((REPS, 8, 128), f32),
            dma((3,)), dma, dma, dma, dma, dma, dma, dma, dma,
            dma((12,)), dma((12,)), dma((12,)), dma((12,)),
            dma((7,)), dma((7,)), dma((14,)), dma((14,)), dma((7,)), dma((7,)),
        ],
        compiler_params=pltpu.CompilerParams(
            collective_id=0, has_side_effects=True, vmem_limit_bytes=60 << 20
        ),
    )(
        embeddings, route.reshape(1, REPORTS), place, scales,
        first_weight, first_bias.reshape(1, HID), second_weight, out_cotangent.transpose(1, 0, 2),
    )
    return (
        gradient, grads[0:512].astype(f32), bias.reshape(HID), grads[512:1024].astype(f32),
    )


def solution(mesh):
    return jax.shard_map(
        on_device,
        mesh=mesh,
        in_specs=(
            P("rep", "band"),
            P("band", None),
            P(None, "band"),
            P(),
            P(),
            P(),
            P(),
            P(None, ("band", "rep"), None),
        ),
        out_specs=(P("rep", "band"), P(), P(), P()),
        check_vma=False,
    )
```

```python
import jax
import jax.numpy as jnp
from jax import lax
from jax.experimental import pallas as pl
from jax.experimental.pallas import tpu as pltpu
from jax.sharding import PartitionSpec as P

MESH = pl.DeviceIdType.MESH
bf16 = jnp.bfloat16
f32 = jnp.float32

root_two_pi = 0.7978845608028654
cubic = 0.044715
half_log2e = 0.8493218002880191

BANDS = 64
REPS = 4
YS, ZS, CORES = 4, 8, 2
CAP = 20
TILE = 16
ROWS = BANDS * TILE
REPORTS = 512
LEVELS = 4
CH = 128
PART = 32
SUB = 3
NLON = 256
LAT = 12.0
CELLS = SUB * NLON
HID = 512
GROWS = 4096


def iota(shape, dim):
    return lax.broadcasted_iota(jnp.int32, shape, dim)


def one_where(cond):
    return jnp.where(cond, 1.0, 0.0).astype(bf16)


def dot(a, b):
    return lax.dot_general(a, b, (((1,), (0,)), ((), ())), preferred_element_type=f32)


def dot_nt(a, b):
    return lax.dot_general(a, b, (((1,), (1,)), ((), ())), preferred_element_type=f32)


def eye(n):
    return one_where(iota((n, n), 0) == iota((n, n), 1))


def row_keys(start, rows):
    row = iota((rows, 1), 0) + start
    band = row >> 4
    ok = row & 15
    key = jnp.where(ok == 15, -1000, (band - 1) * 5 + ok).astype(f32)
    place_band = jnp.where(ok == 15, band, -1000).astype(f32)
    return key, place_band


def report_ranks(route_ref):
    owner = route_ref[...].astype(f32)
    rank = jnp.zeros((1, REPORTS), f32)
    for part in range(4):
        mine = iota((128, REPORTS), 0) + part * 128
        lane = iota((128, REPORTS), 1)
        col = jnp.sum(jnp.where(mine == lane, owner, 0.0), axis=1, keepdims=True)
        rank = rank + jnp.sum(
            jnp.where((col == owner) & (mine < lane), 1.0, 0.0), axis=0, keepdims=True
        )
    return owner, rank


def greet(me, rep):
    barrier = pltpu.get_barrier_semaphore()

    def band_peer(d, carry):
        pl.semaphore_signal(
            barrier, inc=1, device_id=(lax.rem(me + d, BANDS), rep), device_id_type=MESH
        )
        return carry

    lax.fori_loop(1, BANDS, band_peer, 0)
    for d in range(1, REPS):
        pl.semaphore_signal(
            barrier, inc=1, device_id=(me, lax.rem(rep + d, REPS)), device_id_type=MESH
        )
    return barrier


def send_tiles(me, rep, table, landing, send_sem, recv_sem):
    def send(d, carry):
        peer = lax.rem(me + d, BANDS)
        pltpu.make_async_remote_copy(
            src_ref=table.at[pl.ds(pl.multiple_of(peer * TILE, TILE), TILE)],
            dst_ref=landing.at[pl.ds(pl.multiple_of(me * TILE, TILE), TILE)],
            send_sem=send_sem,
            recv_sem=recv_sem,
            device_id=(peer, rep),
            device_id_type=MESH,
        ).start()
        return carry

    lax.fori_loop(1, BANDS, send, 0)


def tiles_done(me, rep, table, landing, send_sem, recv_sem):
    return pltpu.make_async_remote_copy(
        src_ref=table.at[pl.ds(0, ROWS - TILE)],
        dst_ref=landing.at[pl.ds(0, ROWS - TILE)],
        send_sem=send_sem,
        recv_sem=recv_sem,
        device_id=(lax.rem(me + 1, BANDS), rep),
        device_id_type=MESH,
    )


def decode_places(t, rep, expand, base_ref, east_ref, valid_ref):
    lane = iota((1, ROWS), 1)
    ok = lane & 15
    o = (ok >= 5).astype(jnp.int32) + (ok >= 10).astype(jnp.int32) + (ok >= 15).astype(jnp.int32)
    k4 = (ok - 5 * o) * 4
    v = lax.rem(t + 2, 3) + o
    third = jnp.where(v >= 3, v - 3, v)
    code = third * 20 + k4
    lam = iota((64, ROWS), 0)
    low = expand[0:64, :]
    high = expand[64:128, :]
    count = jnp.sum(jnp.where(lam == third + 60, low, 0.0), axis=0, keepdims=True)
    offset = (1 - o).astype(f32) * LAT + (rep * SUB).astype(f32) + 0.5
    for s in range(4):
        hit = lam == code + s
        north = jnp.sum(jnp.where(hit, low, 0.0), axis=0, keepdims=True)
        east = jnp.sum(jnp.where(hit, high, 0.0), axis=0, keepdims=True)
        valid = jnp.where((ok < 15) & ((k4 + s).astype(f32) < count), 1.0, 0.0)
        base_ref[s] = jnp.broadcast_to(offset - north * LAT, (16, ROWS))
        valid_ref[s] = jnp.broadcast_to(valid, (16, ROWS))
        east_ref[s] = jnp.broadcast_to(east * float(NLON), (8, ROWS))


def build_table(emb_ref, place_ref, owner, rank, pick_ref, table):
    quad = jnp.floor(rank * 0.25)
    within = rank - 4.0 * quad
    key = owner * 5.0 + quad
    third = owner - 3.0 * jnp.floor((owner + 0.5) * (1.0 / 3.0))
    emb = emb_ref[...].astype(f32)
    emb_b = jnp.concatenate(
        [jnp.where(within == float(s), emb, 0.0) for s in range(4)], axis=0
    ).astype(bf16)
    lam = iota((128, REPORTS), 0).astype(f32)
    spot = third * 20.0 + rank
    north = place_ref[0:1, :].astype(f32)
    east = place_ref[1:2, :].astype(f32)
    place_b = (
        jnp.where(lam == spot, north, 0.0)
        + jnp.where(lam == spot + 64.0, east, 0.0)
        + jnp.where(lam == third + 60.0, 1.0, 0.0)
    ).astype(bf16)
    for part in range(8):
        rows = slice(part * 128, (part + 1) * 128)
        row_key, place_band = row_keys(part * 128, 128)
        pick = one_where(row_key == key)
        pick_ref[rows, :] = pick
        near = one_where(jnp.abs(place_band - owner) <= 1.0)
        table[rows, :] = (dot_nt(pick, emb_b) + dot_nt(near, place_b)).astype(bf16)
    return within


def kernels(it, scales_ref, base_ref, east_ref, valid_ref, col_ref, rk_ref, mix_ref, rowf_ref):
    s = it >> 2
    reach = scales_ref[it & 3] * LAT
    scale = half_log2e / jnp.full((1, 128), reach, f32)
    scale_wide = jnp.concatenate([scale] * 8, axis=1)
    east = east_ref[s, 0:1, :] * scale_wide
    for c in range(8):
        centre = (iota((32, 128), 0).astype(f32) + (c * 32 + 0.5)) * scale
        for b in range(8):
            gap = centre - east[:, b * 128 : (b + 1) * 128]
            col_ref[it, c * 32 : (c + 1) * 32, b * 128 : (b + 1) * 128] = jnp.exp2(
                -(gap * gap)
            ).astype(bf16)
    valid = valid_ref[s]
    wide = []
    for i in range(SUB):
        gap = (base_ref[s] + float(i)) * scale_wide
        row = (jnp.exp2(-(gap * gap)) * valid).astype(bf16)
        rk_ref[it, i] = row
        wide.append(row.astype(f32))
    sub = iota((16, ROWS), 0)
    mixed = jnp.where(
        sub == 0, wide[0], jnp.where(sub == 1, wide[1], jnp.where(sub == 2, wide[2], 0.0))
    )
    rowf_ref[it] = mixed[0:8, :]
    mix_ref[it] = mixed.astype(bf16)


def grid_kernel(
    emb_ref, route_ref, place_ref, scales_ref, w1_hbm, b1_ref, w2_hbm, cot_hbm,
    eg_ref, first_ref, second_ref,
    table, rr_ref, pick_ref, w1_ref, w2_ref, cot_ref,
    emb_t, expand, base_ref, east_ref, valid_ref, col_ref, rk_ref, mix_ref, rowf_ref, w_ref, acc_ref,
    feat_ref, w1p_ref, w1t_ref, bcol_ref, hid_ref, pg_ref, sg_ref,
    d_out, d_in, table2, landing, g0, g1, g2, in_c, in_y, in_g, full_ref, bc, by, bz, bx,
    loads, ssem, rsem, ssem2, rsem2, vs, vr, vs2, vr2, xs, xr, ds, dr, gs, gr, bs, br, as_, ar,
):
    me = lax.axis_index("band")
    rep = lax.axis_index("rep")
    core = lax.rem(me, CORES)
    z = lax.rem(me // CORES, ZS)
    y = me // (CORES * ZS)

    def core_peer(d):
        return me + 1 - 2 * core, rep

    def y_peer(d):
        return lax.rem(y + d, YS) * (CORES * ZS) + z * CORES + core, rep

    def z_peer(d):
        return y * (CORES * ZS) + lax.rem(z + d, ZS) * CORES + core, rep

    def x_peer(d):
        return me, lax.rem(rep + d, REPS)

    def start(src, dst, send, recv, device):
        copy = pltpu.make_async_remote_copy(
            src_ref=src, dst_ref=dst, send_sem=send, recv_sem=recv, device_id=device, device_id_type=MESH
        )
        copy.start()
        return copy

    def rows_at(index, size):
        return pl.ds(pl.multiple_of(index * size, size), size)

    def bias_round(value, slots, n, mine, peer, base):
        slots[mine] = value
        return [
            start(slots.at[mine], slots.at[mine], bs.at[base + d - 1], br.at[base + d - 1], peer(d))
            for d in range(1, n)
        ]

    def bias_sum(slots, n):
        total = slots[0]
        for k in range(1, n):
            total = total + slots[k]
        return total

    def finish(copies):
        for copy in copies:
            copy.wait()

    def ring_gather(piece, sems, base, peer):
        send, recv = sems
        right, left = peer(1), peer(3)
        one = start(piece(0, 0), piece(0, 0), send.at[base], recv.at[base], right)
        two = start(piece(0, 1), piece(0, 1), send.at[base + 1], recv.at[base + 1], left)
        three = start(piece(0, 1), piece(0, 1), send.at[base + 2], recv.at[base + 2], right)
        four = start(piece(0, 0), piece(0, 0), send.at[base + 3], recv.at[base + 3], left)

        def forward():
            one.wait_recv()
            five = start(piece(3, 0), piece(3, 0), send.at[base + 4], recv.at[base + 4], right)
            two.wait_recv()
            six = start(piece(1, 1), piece(1, 1), send.at[base + 5], recv.at[base + 5], left)

            def rest():
                one.wait_send()
                two.wait_send()
                finish([three, four, five, six])

            return rest

        return forward

    group_at = z * REPS + rep

    def group_peer(j):
        return y * (CORES * ZS) + (j >> 2) * CORES + core, j & 3

    def to_group(src, src_at, dst, dst_at, send, recv):
        def one(d, carry):
            j = lax.rem(group_at + d, ZS * REPS)
            pltpu.make_async_remote_copy(
                src_ref=src.at[pl.ds(pl.multiple_of(src_at(j), TILE), TILE)],
                dst_ref=dst.at[pl.ds(pl.multiple_of(dst_at, TILE), TILE)],
                send_sem=send, recv_sem=recv, device_id=group_peer(j), device_id_type=MESH,
            ).start()
            return carry

        lax.fori_loop(1, ZS * REPS, one, 0)
        rows = pl.ds(0, (ZS * REPS - 1) * TILE)
        return pltpu.make_async_remote_copy(
            src_ref=src.at[rows], dst_ref=dst.at[rows], send_sem=send, recv_sem=recv,
            device_id=group_peer(lax.rem(group_at + 1, ZS * REPS)), device_id_type=MESH,
        )

    barrier = greet(me, rep)
    held = []
    for k, (src, dst) in enumerate(((w1_hbm, w1_ref), (w2_hbm, w2_ref), (cot_hbm, cot_ref))):
        copy = pltpu.make_async_copy(src, dst, loads.at[k])
        copy.start()
        held.append(copy)

    owner, rank = report_ranks(route_ref)
    within = build_table(emb_ref, place_ref, owner, rank, pick_ref, table)
    pl.semaphore_wait(barrier, BANDS - 1 + REPS - 1)
    mine = rr_ref.at[rep]
    send_tiles(me, rep, table, mine, ssem, rsem)
    own = rows_at(me, TILE)
    rr_ref[rep, own, :] = table[own, :]

    finish(held)
    r512 = iota((512, 512), 0)
    c512 = iota((512, 512), 1)
    w1p_ref[...] = dot(one_where(c512 == (r512 & 127) * 4 + (r512 >> 7)), w1_ref[...]).astype(bf16)
    w1t_ref[...] = dot_nt(eye(512), w1p_ref[...]).astype(bf16)
    bcol_ref[...] = jnp.sum(jnp.where(r512 == c512, b1_ref[...], 0.0), axis=1, keepdims=True)

    done = tiles_done(me, rep, table, mine, ssem, rsem)
    done.wait_recv()
    def report_piece(half):
        return lambda k, h: rr_ref.at[lax.rem(rep + k, REPS), pl.ds(half * 512 + h * 256, 256)]

    forward_first = ring_gather(report_piece(0), (xs, xr), 0, x_peer)
    ident = eye(128)
    group = one_where(
        ((iota((128, 128), 0) >> 4) == (iota((128, 128), 1) >> 4)) & ((iota((128, 128), 0) & 15) == 15)
    )
    turned = dot_nt(ident, rr_ref[rep]).astype(bf16)
    for b in range(8):
        expand[:, b * 128 : (b + 1) * 128] = dot(turned[:, b * 128 : (b + 1) * 128], group)
    decode_places(me, rep, expand, base_ref, east_ref, valid_ref)
    acc_ref[...] = jnp.zeros_like(acc_ref)

    def make(it, carry):
        kernels(it, scales_ref, base_ref, east_ref, valid_ref, col_ref, rk_ref, mix_ref, rowf_ref)
        return carry

    lax.fori_loop(0, 16, make, 0)
    first_half = forward_first()
    forward_second = ring_gather(report_piece(1), (xs, xr), 6, x_peer)

    for half in range(2):
        lanes = slice(half * 512, (half + 1) * 512)
        if half == 0:
            first_half()
            second_half = forward_second()
        else:
            second_half()
        for q in range(REPS):
            turned = dot_nt(ident, rr_ref[q, lanes, :]).astype(bf16)
            for s in range(4):
                emb_t[s, q * PART : (q + 1) * PART, lanes] = turned[s * PART : (s + 1) * PART, :]

        def splat(it, carry):
            s = it >> 2
            level = it & 3
            rows = [rk_ref[it, i, :, lanes] for i in range(SUB)]
            w_ref[SUB * CH : SUB * CH + 16, lanes] = mix_ref[it, :, lanes]
            for c in range(8):
                e = emb_t[s, c * 16 : (c + 1) * 16, lanes]
                for i in range(SUB):
                    w_ref[i * CH + c * 16 : i * CH + (c + 1) * 16, lanes] = e * rows[i]
            acc_ref[level] += dot_nt(w_ref[:, lanes], col_ref[it, :, lanes])
            return carry

        lax.fori_loop(0, 16, splat, 0)
    done.wait_send()

    def inverse(level, i):
        return 1.0 / (acc_ref[level, SUB * CH + i : SUB * CH + i + 1, :] + 1.0)

    for level in range(LEVELS):
        for i in range(SUB):
            feat_ref[level * CH : (level + 1) * CH, i * NLON : (i + 1) * NLON] = (
                acc_ref[level, i * CH : (i + 1) * CH, :] * inverse(level, i)
            ).astype(bf16)

    for i in range(SUB):
        cells = slice(i * NLON, (i + 1) * NLON)
        for h in range(2):
            rows = slice(h * 256, (h + 1) * 256)
            pre = dot(w1t_ref[rows, :], feat_ref[:, cells]) + bcol_ref[rows, :]
            above = dot(w2_ref[rows, :], cot_ref[i])
            square = pre * pre
            tangent = jnp.tanh(root_two_pi * (pre + cubic * square * pre))
            hid_ref[rows, cells] = (0.5 * pre * (1.0 + tangent)).astype(bf16)
            slope = 0.5 * (1.0 + tangent) + 0.5 * pre * (1.0 - tangent * tangent) * root_two_pi * (
                1.0 + 3.0 * cubic * square
            )
            pg_ref[rows, cells] = (above * slope).astype(bf16)

    back = one_where(c512 == (r512 & 3) * 128 + (r512 >> 2))
    for h in range(2):
        rows = slice(h * 256, (h + 1) * 256)
        first = dot(back, dot_nt(feat_ref[...], pg_ref[rows, :]).astype(bf16)).astype(bf16)
        second = dot_nt(hid_ref[:, 0:NLON], cot_ref[0, rows, :])
        for i in range(1, SUB):
            second = second + dot_nt(hid_ref[:, i * NLON : (i + 1) * NLON], cot_ref[i, rows, :])
        second = second.astype(bf16)
        for c in range(2):
            at = (h * 2 + c) * 1024
            g0[at : at + 512, :] = first[:, c * 128 : (c + 1) * 128]
            g0[at + 512 : at + 1024, :] = second[:, c * 128 : (c + 1) * 128]
    bias = dot_nt(jnp.ones((16, CELLS), bf16), pg_ref[...])
    bias_tile = jnp.concatenate(
        [bias[0:1, c * 128 : (c + 1) * 128] for c in range(4)] + [jnp.zeros((4, 128), f32)], axis=0
    )
    c_copies = []
    for d in (1, 2, 3, 0):
        k = lax.rem(y + d, YS)
        c_copies.append(
            start(g0.at[rows_at((1 - core) * YS + k, 512)], in_c.at[rows_at(k, 512)], gs.at[d], gr.at[d], core_peer(1))
        )
    c_bias = bias_round(bias_tile, bc, CORES, core, core_peer, 0)

    for i in range(SUB):
        grad = dot(w1p_ref[...], pg_ref[:, i * NLON : (i + 1) * NLON])
        for level in range(LEVELS):
            sg_ref[level, i * CH : (i + 1) * CH, :] = (
                grad[level * CH : (level + 1) * CH, :] * inverse(level, i)
            ).astype(bf16)

    def spread(n):
        lanes = slice(n * 256, (n + 1) * 256)

        def one_group(s, carry):
            total = None
            for level in range(LEVELS):
                it = s * 4 + level
                along = dot(sg_ref[level], col_ref[it, :, lanes])
                for i in range(SUB):
                    term = along[i * CH : (i + 1) * CH, :] * rowf_ref[it, i : i + 1, lanes]
                    total = term if total is None else total + term
            for q in range(REPS):
                d_out[n, q, rows_at(s, PART), :] = total[q * PART : (q + 1) * PART, :].astype(bf16)
            return carry

        lax.fori_loop(0, 4, one_group, 0)
        return [
            start(
                d_out.at[n, lax.rem(rep + d, REPS)], d_in.at[n, d - 1],
                ds.at[n * 3 + d - 1], dr.at[n * 3 + d - 1], x_peer(d),
            )
            for d in range(1, REPS)
        ]

    def to_feeds(n, copies):
        finish(copies)
        total = d_out[n, rep].astype(f32)
        for d in range(REPS - 1):
            total = total + d_in[n, d].astype(f32)
        table2[n * 256 : (n + 1) * 256, :] = jnp.transpose(total).astype(bf16)

        def send(j, carry):
            peer = n * 16 + lax.rem(j + me, 16)

            @pl.when(peer != me)
            def _():
                pltpu.make_async_remote_copy(
                    src_ref=table2.at[rows_at(peer, TILE)],
                    dst_ref=landing.at[rows_at(me, TILE)],
                    send_sem=ssem2,
                    recv_sem=rsem2,
                    device_id=(peer, rep),
                    device_id_type=MESH,
                ).start()

            return carry

        lax.fori_loop(0, 16, send, 0)

    y_copies = []
    for d, copy in zip((1, 2, 3, 0), c_copies):
        k = lax.rem(y + d, YS)
        copy.wait()
        g1[rows_at(k, 512), :] = (
            g0[rows_at(core * YS + k, 512), :].astype(f32) + in_c[rows_at(k, 512), :].astype(f32)
        ).astype(bf16)
        if d:
            y_copies.append(start(g1.at[rows_at(k, 512)], in_y.at[d - 1], gs.at[3 + d], gr.at[3 + d], y_peer(d)))
    finish(c_bias)
    y_bias = bias_round(bias_sum(bc, CORES), by, YS, y, y_peer, 1)
    d0 = spread(0)
    d1 = spread(1)
    d2 = spread(2)
    finish(y_copies)
    total = g1[rows_at(y, 512), :].astype(f32)
    for d in range(YS - 1):
        total = total + in_y[d].astype(f32)
    g2[...] = total.astype(bf16)
    own_tile = rows_at(group_at, TILE)
    in_g[own_tile, :] = g2[own_tile, :]
    scattered = to_group(g2, lambda j: j * TILE, in_g, group_at * TILE, vs, vr)
    finish(y_bias)
    z_bias = bias_round(bias_sum(by, YS), bz, ZS, z, z_peer, 4)
    to_feeds(0, d0)
    d3 = spread(3)
    scattered.wait()
    total = in_g[0:TILE, :].astype(f32)
    for j in range(1, ZS * REPS):
        total = total + in_g[j * TILE : (j + 1) * TILE, :].astype(f32)
    block_at = core * 2048 + y * 512
    full_ref[pl.ds(pl.multiple_of(block_at + group_at * TILE, TILE), TILE), :] = total.astype(bf16)
    gathered = to_group(
        full_ref, lambda j: block_at + group_at * TILE, full_ref, block_at + group_at * TILE, vs2, vr2
    )
    to_feeds(1, d1)
    finish(z_bias)
    x_bias = bias_round(bias_sum(bz, ZS), bx, REPS, rep, x_peer, 11)
    to_feeds(2, d2)
    gathered.wait()

    def block(k):
        return full_ref.at[rows_at(core * YS + k, 512)]

    def to_core(d):
        k = lax.rem(y + YS - d, YS)
        return start(block(k), block(k), as_.at[3 + d], ar.at[3 + d], core_peer(1))

    blocks = [start(block(y), block(y), as_.at[d - 1], ar.at[d - 1], y_peer(d)) for d in range(1, YS)]
    crossing = [to_core(0)]
    to_feeds(3, d3)
    landing[own, :] = table2[own, :]
    finish(x_bias)
    bias_total = bias_sum(bx, REPS)
    bias_row = jnp.concatenate([bias_total[c : c + 1, :] for c in range(4)], axis=1)
    eg_ref[PART : PART + 8, :] = jnp.broadcast_to(bias_row, (8, HID))
    for d in (1, 3, 2):
        blocks[d - 1].wait()
        crossing.append(to_core(d))
    tiles_done(me, rep, table2, landing, ssem2, rsem2).wait()
    turned = dot_nt(ident, landing[...]).astype(bf16)
    found = dot(turned, pick_ref[...])
    gradient = jnp.zeros((PART, REPORTS), f32)
    for s in range(4):
        gradient = gradient + jnp.where(within == float(s), found[s * PART : (s + 1) * PART, :], 0.0)
    eg_ref[0:PART, :] = gradient
    finish(crossing)
    for c in range(4):
        lanes = slice(c * 128, (c + 1) * 128)
        first_ref[:, lanes] = full_ref[c * 1024 : c * 1024 + 512, :]
        second_ref[:, lanes] = full_ref[c * 1024 + 512 : (c + 1) * 1024, :]


def sds(shape, dtype):
    return jax.ShapeDtypeStruct(shape, dtype)


def on_device(
    embeddings, route, place, scales, first_weight, first_bias, second_weight, out_cotangent
):
    dma = pltpu.SemaphoreType.DMA
    vm = pltpu.VMEM
    in_vmem = pl.BlockSpec(memory_space=pltpu.VMEM)
    anywhere = pl.BlockSpec(memory_space=pl.ANY)
    gradient, first, second = pl.pallas_call(
        grid_kernel,
        out_shape=[sds((PART + 8, REPORTS), f32), sds((512, 512), bf16), sds((512, 512), bf16)],
        in_specs=[
            in_vmem, in_vmem, in_vmem, pl.BlockSpec(memory_space=pltpu.SMEM),
            anywhere, in_vmem, anywhere, anywhere,
        ],
        out_specs=[in_vmem] * 3,
        scratch_shapes=[
            vm((ROWS, 128), bf16), vm((REPS, ROWS, 128), bf16), vm((ROWS, REPORTS), bf16),
            vm((512, HID), bf16), vm((HID, 512), bf16), vm((SUB, 512, NLON), bf16),
            vm((4, CH, ROWS), bf16), vm((128, ROWS), f32),
            vm((4, 16, ROWS), f32), vm((4, 8, ROWS), f32), vm((4, 16, ROWS), f32),
            vm((16, NLON, ROWS), bf16), vm((16, SUB, 16, ROWS), bf16), vm((16, 16, ROWS), bf16),
            vm((16, 8, ROWS), f32), vm((SUB * CH + 16, ROWS), bf16),
            vm((LEVELS, SUB * CH + 16, NLON), f32),
            vm((512, CELLS), bf16), vm((512, HID), bf16), vm((HID, 512), bf16), vm((HID, 1), f32),
            vm((HID, CELLS), bf16), vm((HID, CELLS), bf16), vm((LEVELS, SUB * CH, NLON), bf16),
            vm((4, REPS, 128, 256), bf16), vm((4, REPS - 1, 128, 256), bf16),
            vm((ROWS, 128), bf16), vm((ROWS, 128), bf16),
            vm((GROWS, 128), bf16), vm((2048, 128), bf16), vm((512, 128), bf16),
            vm((2048, 128), bf16), vm((3, 512, 128), bf16), vm((512, 128), bf16),
            vm((GROWS, 128), bf16),
            vm((CORES, 8, 128), f32), vm((YS, 8, 128), f32), vm((ZS, 8, 128), f32), vm((REPS, 8, 128), f32),
            dma((3,)), dma, dma, dma, dma, dma, dma, dma, dma,
            dma((12,)), dma((12,)), dma((12,)), dma((12,)),
            dma((7,)), dma((7,)), dma((14,)), dma((14,)), dma((7,)), dma((7,)),
        ],
        compiler_params=pltpu.CompilerParams(
            collective_id=0, has_side_effects=True, vmem_limit_bytes=60 << 20
        ),
    )(
        embeddings, route.reshape(1, REPORTS), place, scales,
        first_weight, first_bias.reshape(1, HID), second_weight, out_cotangent.transpose(1, 0, 2),
    )
    return (gradient[0:PART], first.astype(f32), gradient[PART], second.astype(f32))


def solution(mesh):
    return jax.shard_map(
        on_device,
        mesh=mesh,
        in_specs=(
            P("rep", "band"),
            P("band", None),
            P(None, "band"),
            P(),
            P(),
            P(),
            P(),
            P(None, ("band", "rep"), None),
        ),
        out_specs=(P("rep", "band"), P(), P(), P()),
        check_vma=False,
    )
```

```python
import jax
import jax.numpy as jnp
from jax import lax
from jax.experimental import pallas as pl
from jax.experimental.pallas import tpu as pltpu
from jax.sharding import PartitionSpec as P

MESH = pl.DeviceIdType.MESH
bf16 = jnp.bfloat16
f32 = jnp.float32

root_two_pi = 0.7978845608028654
cubic = 0.044715
half_log2e = 0.8493218002880191

BANDS = 64
REPS = 4
YS, ZS, CORES = 4, 8, 2
CAP = 20
TILE = 16
ROWS = BANDS * TILE
REPORTS = 512
LEVELS = 4
CH = 128
PART = 32
SUB = 3
NLON = 256
LAT = 12.0
CELLS = SUB * NLON
HID = 512
GROWS = 4096


def iota(shape, dim):
    return lax.broadcasted_iota(jnp.int32, shape, dim)


def one_where(cond):
    return jnp.where(cond, 1.0, 0.0).astype(bf16)


def dot(a, b):
    return lax.dot_general(a, b, (((1,), (0,)), ((), ())), preferred_element_type=f32)


def dot_nt(a, b):
    return lax.dot_general(a, b, (((1,), (1,)), ((), ())), preferred_element_type=f32)


def eye(n):
    return one_where(iota((n, n), 0) == iota((n, n), 1))


def row_keys(start, rows):
    row = iota((rows, 1), 0) + start
    band = row >> 4
    ok = row & 15
    key = jnp.where(ok == 15, -1000, (band - 1) * 5 + ok).astype(f32)
    place_band = jnp.where(ok == 15, band, -1000).astype(f32)
    return key, place_band


def report_ranks(route_ref):
    owner = route_ref[...].astype(f32)
    rank = jnp.zeros((1, REPORTS), f32)
    for part in range(4):
        mine = iota((128, REPORTS), 0) + part * 128
        lane = iota((128, REPORTS), 1)
        col = jnp.sum(jnp.where(mine == lane, owner, 0.0), axis=1, keepdims=True)
        rank = rank + jnp.sum(
            jnp.where((col == owner) & (mine < lane), 1.0, 0.0), axis=0, keepdims=True
        )
    return owner, rank


def greet(me, rep):
    barrier = pltpu.get_barrier_semaphore()

    def band_peer(d, carry):
        pl.semaphore_signal(
            barrier, inc=1, device_id=(((me + d) & (BANDS - 1)), rep), device_id_type=MESH
        )
        return carry

    lax.fori_loop(0, 9, lambda g, c: [band_peer(g * 7 + k, c) for k in range(1, 8)][0], 0)
    for d in range(1, REPS):
        pl.semaphore_signal(
            barrier, inc=1, device_id=(me, ((rep + d) & (REPS - 1))), device_id_type=MESH
        )
    return barrier


def send_tiles(me, rep, table, landing, send_sem, recv_sem):
    def send(d, carry):
        peer = ((me + d) & (BANDS - 1))
        pltpu.make_async_remote_copy(
            src_ref=table.at[pl.ds(pl.multiple_of(peer * TILE, TILE), TILE)],
            dst_ref=landing.at[pl.ds(pl.multiple_of(me * TILE, TILE), TILE)],
            send_sem=send_sem,
            recv_sem=recv_sem,
            device_id=(peer, rep),
            device_id_type=MESH,
        ).start()
        return carry

    lax.fori_loop(0, 9, lambda g, c: [send(g * 7 + k, c) for k in range(1, 8)][0], 0)


def tiles_done(me, rep, table, landing, send_sem, recv_sem):
    return pltpu.make_async_remote_copy(
        src_ref=table.at[pl.ds(0, ROWS - TILE)],
        dst_ref=landing.at[pl.ds(0, ROWS - TILE)],
        send_sem=send_sem,
        recv_sem=recv_sem,
        device_id=(((me + 1) & (BANDS - 1)), rep),
        device_id_type=MESH,
    )


def decode_places(t, rep, expand, base_ref, east_ref, valid_ref):
    lane = iota((1, ROWS), 1)
    ok = lane & 15
    o = (ok >= 5).astype(jnp.int32) + (ok >= 10).astype(jnp.int32) + (ok >= 15).astype(jnp.int32)
    k4 = (ok - 5 * o) * 4
    v = lax.rem(t + 2, 3) + o
    third = jnp.where(v >= 3, v - 3, v)
    code = third * 20 + k4
    lam = iota((64, ROWS), 0)
    low = expand[0:64, :]
    high = expand[64:128, :]
    count = jnp.sum(jnp.where(lam == third + 60, low, 0.0), axis=0, keepdims=True)
    offset = (1 - o).astype(f32) * LAT + (rep * SUB).astype(f32) + 0.5
    for s in range(4):
        hit = lam == code + s
        north = jnp.sum(jnp.where(hit, low, 0.0), axis=0, keepdims=True)
        east = jnp.sum(jnp.where(hit, high, 0.0), axis=0, keepdims=True)
        valid = jnp.where((ok < 15) & ((k4 + s).astype(f32) < count), 1.0, 0.0)
        base_ref[s] = jnp.broadcast_to(offset - north * LAT, (16, ROWS))
        valid_ref[s] = jnp.broadcast_to(valid, (16, ROWS))
        east_ref[s] = jnp.broadcast_to(east * float(NLON), (8, ROWS))


def build_table(emb_ref, place_ref, owner, rank, pick_ref, table):
    quad = jnp.floor(rank * 0.25)
    within = rank - 4.0 * quad
    key = owner * 5.0 + quad
    third = owner - 3.0 * jnp.floor((owner + 0.5) * (1.0 / 3.0))
    emb = emb_ref[...].astype(f32)
    emb_b = jnp.concatenate(
        [jnp.where(within == float(s), emb, 0.0) for s in range(4)], axis=0
    ).astype(bf16)
    lam = iota((128, REPORTS), 0).astype(f32)
    spot = third * 20.0 + rank
    north = place_ref[0:1, :].astype(f32)
    east = place_ref[1:2, :].astype(f32)
    place_b = (
        jnp.where(lam == spot, north, 0.0)
        + jnp.where(lam == spot + 64.0, east, 0.0)
        + jnp.where(lam == third + 60.0, 1.0, 0.0)
    ).astype(bf16)
    for part in range(8):
        rows = slice(part * 128, (part + 1) * 128)
        row_key, place_band = row_keys(part * 128, 128)
        pick = one_where(row_key == key)
        pick_ref[rows, :] = pick
        near = one_where(jnp.abs(place_band - owner) <= 1.0)
        table[rows, :] = (dot_nt(pick, emb_b) + dot_nt(near, place_b)).astype(bf16)
    return within


def kernels(it, scales_ref, base_ref, east_ref, valid_ref, col_ref, rk_ref, mix_ref, rowf_ref):
    s = it >> 2
    reach = scales_ref[it & 3] * LAT
    scale = half_log2e / jnp.full((1, 128), reach, f32)
    scale_wide = jnp.concatenate([scale] * 8, axis=1)
    east = east_ref[s, 0:1, :] * scale_wide
    for c in range(8):
        centre = (iota((32, 128), 0).astype(f32) + (c * 32 + 0.5)) * scale
        for b in range(8):
            gap = centre - east[:, b * 128 : (b + 1) * 128]
            col_ref[it, c * 32 : (c + 1) * 32, b * 128 : (b + 1) * 128] = jnp.exp2(
                -(gap * gap)
            ).astype(bf16)
    valid = valid_ref[s]
    wide = []
    for i in range(SUB):
        gap = (base_ref[s] + float(i)) * scale_wide
        row = (jnp.exp2(-(gap * gap)) * valid).astype(bf16)
        rk_ref[it, i] = row
        wide.append(row.astype(f32))
    sub = iota((16, ROWS), 0)
    mixed = jnp.where(
        sub == 0, wide[0], jnp.where(sub == 1, wide[1], jnp.where(sub == 2, wide[2], 0.0))
    )
    rowf_ref[it] = mixed[0:8, :]
    mix_ref[it] = mixed.astype(bf16)


def grid_kernel(
    emb_ref, route_ref, place_ref, scales_ref, w1_hbm, b1_ref, w2_hbm, cot_hbm,
    eg_ref, first_ref, second_ref,
    table, rr_ref, pick_ref, w1_ref, w2_ref, cot_ref,
    emb_t, expand, base_ref, east_ref, valid_ref, col_ref, rk_ref, mix_ref, rowf_ref, w_ref, acc_ref,
    feat_ref, w1p_ref, w1t_ref, bcol_ref, hid_ref, pg_ref, sg_ref,
    d_out, d_in, table2, landing, g0, g1, g2, in_c, in_y, in_g, full_ref, bc, by, bz, bx,
    loads, ssem, rsem, ssem2, rsem2, vs, vr, vs2, vr2, xs, xr, ds, dr, gs, gr, bs, br, as_, ar,
):
    me = lax.axis_index("band")
    rep = lax.axis_index("rep")
    core = ((me) & (CORES - 1))
    z = (me >> 1) & (ZS - 1)
    y = me >> 4

    def core_peer(d):
        return me + 1 - 2 * core, rep

    def y_peer(d):
        return ((y + d) & (YS - 1)) * (CORES * ZS) + z * CORES + core, rep

    def z_peer(d):
        return y * (CORES * ZS) + ((z + d) & (ZS - 1)) * CORES + core, rep

    def x_peer(d):
        return me, ((rep + d) & (REPS - 1))

    def start(src, dst, send, recv, device):
        copy = pltpu.make_async_remote_copy(
            src_ref=src, dst_ref=dst, send_sem=send, recv_sem=recv, device_id=device, device_id_type=MESH
        )
        copy.start()
        return copy

    def rows_at(index, size):
        return pl.ds(pl.multiple_of(index * size, size), size)

    def bias_round(value, slots, n, mine, peer, base):
        slots[mine] = value
        return [
            start(slots.at[mine], slots.at[mine], bs.at[base + d - 1], br.at[base + d - 1], peer(d))
            for d in range(1, n)
        ]

    def bias_sum(slots, n):
        total = slots[0]
        for k in range(1, n):
            total = total + slots[k]
        return total

    def finish(copies):
        for copy in copies:
            copy.wait()

    def ring_gather(piece, sems, base, peer):
        send, recv = sems
        right, left = peer(1), peer(3)
        one = start(piece(0, 0), piece(0, 0), send.at[base], recv.at[base], right)
        two = start(piece(0, 1), piece(0, 1), send.at[base + 1], recv.at[base + 1], left)
        three = start(piece(0, 1), piece(0, 1), send.at[base + 2], recv.at[base + 2], right)
        four = start(piece(0, 0), piece(0, 0), send.at[base + 3], recv.at[base + 3], left)

        def forward():
            one.wait_recv()
            five = start(piece(3, 0), piece(3, 0), send.at[base + 4], recv.at[base + 4], right)
            two.wait_recv()
            six = start(piece(1, 1), piece(1, 1), send.at[base + 5], recv.at[base + 5], left)

            def rest():
                one.wait_send()
                two.wait_send()
                finish([three, four, five, six])

            return rest

        return forward

    group_at = z * REPS + rep

    def group_peer(j):
        return y * (CORES * ZS) + (j >> 2) * CORES + core, j & 3

    def to_group(src, src_at, dst, dst_at, send, recv):
        def one(d, carry):
            j = ((group_at + d) & (ZS * REPS - 1))
            pltpu.make_async_remote_copy(
                src_ref=src.at[pl.ds(pl.multiple_of(src_at(j), TILE), TILE)],
                dst_ref=dst.at[pl.ds(pl.multiple_of(dst_at, TILE), TILE)],
                send_sem=send, recv_sem=recv, device_id=group_peer(j), device_id_type=MESH,
            ).start()
            return carry

        for d in range(1, ZS * REPS):
            one(d, 0)
        rows = pl.ds(0, (ZS * REPS - 1) * TILE)
        return pltpu.make_async_remote_copy(
            src_ref=src.at[rows], dst_ref=dst.at[rows], send_sem=send, recv_sem=recv,
            device_id=group_peer(((group_at + 1) & (ZS * REPS - 1))), device_id_type=MESH,
        )

    barrier = greet(me, rep)
    held = []
    for k, (src, dst) in enumerate(((w1_hbm, w1_ref), (w2_hbm, w2_ref), (cot_hbm, cot_ref))):
        copy = pltpu.make_async_copy(src, dst, loads.at[k])
        copy.start()
        held.append(copy)

    owner, rank = report_ranks(route_ref)
    within = build_table(emb_ref, place_ref, owner, rank, pick_ref, table)
    pl.semaphore_wait(barrier, BANDS - 1 + REPS - 1)
    mine = rr_ref.at[rep]
    send_tiles(me, rep, table, mine, ssem, rsem)
    own = rows_at(me, TILE)
    rr_ref[rep, own, :] = table[own, :]

    finish(held)
    r512 = iota((512, 512), 0)
    c512 = iota((512, 512), 1)
    w1p_ref[...] = dot(one_where(c512 == (r512 & 127) * 4 + (r512 >> 7)), w1_ref[...]).astype(bf16)
    w1t_ref[...] = dot_nt(eye(512), w1p_ref[...]).astype(bf16)
    bcol_ref[...] = jnp.sum(jnp.where(r512 == c512, b1_ref[...], 0.0), axis=1, keepdims=True)

    done = tiles_done(me, rep, table, mine, ssem, rsem)
    done.wait_recv()
    def report_piece(half):
        return lambda k, h: rr_ref.at[((rep + k) & (REPS - 1)), pl.ds(half * 512 + h * 256, 256)]

    forward_first = ring_gather(report_piece(0), (xs, xr), 0, x_peer)
    ident = eye(128)
    group = one_where(
        ((iota((128, 128), 0) >> 4) == (iota((128, 128), 1) >> 4)) & ((iota((128, 128), 0) & 15) == 15)
    )
    turned = dot_nt(ident, rr_ref[rep]).astype(bf16)
    for b in range(8):
        expand[:, b * 128 : (b + 1) * 128] = dot(turned[:, b * 128 : (b + 1) * 128], group)
    decode_places(me, rep, expand, base_ref, east_ref, valid_ref)
    acc_ref[...] = jnp.zeros_like(acc_ref)

    def make(it, carry):
        kernels(it, scales_ref, base_ref, east_ref, valid_ref, col_ref, rk_ref, mix_ref, rowf_ref)
        return carry

    lax.fori_loop(0, 16, make, 0)
    first_half = forward_first()
    forward_second = ring_gather(report_piece(1), (xs, xr), 6, x_peer)

    for half in range(2):
        lanes = slice(half * 512, (half + 1) * 512)
        if half == 0:
            first_half()
            second_half = forward_second()
        else:
            second_half()
        for q in range(REPS):
            turned = dot_nt(ident, rr_ref[q, lanes, :]).astype(bf16)
            for s in range(4):
                emb_t[s, q * PART : (q + 1) * PART, lanes] = turned[s * PART : (s + 1) * PART, :]

        def splat(it, carry):
            s = it >> 2
            level = it & 3
            rows = [rk_ref[it, i, :, lanes] for i in range(SUB)]
            w_ref[SUB * CH : SUB * CH + 16, lanes] = mix_ref[it, :, lanes]
            for c in range(8):
                e = emb_t[s, c * 16 : (c + 1) * 16, lanes]
                for i in range(SUB):
                    w_ref[i * CH + c * 16 : i * CH + (c + 1) * 16, lanes] = e * rows[i]
            acc_ref[level] += dot_nt(w_ref[:, lanes], col_ref[it, :, lanes])
            return carry

        lax.fori_loop(0, 16, splat, 0)
    done.wait_send()

    def inverse(level, i):
        return 1.0 / (acc_ref[level, SUB * CH + i : SUB * CH + i + 1, :] + 1.0)

    for level in range(LEVELS):
        for i in range(SUB):
            feat_ref[level * CH : (level + 1) * CH, i * NLON : (i + 1) * NLON] = (
                acc_ref[level, i * CH : (i + 1) * CH, :] * inverse(level, i)
            ).astype(bf16)

    for i in range(SUB):
        cells = slice(i * NLON, (i + 1) * NLON)
        for h in range(2):
            rows = slice(h * 256, (h + 1) * 256)
            pre = dot(w1t_ref[rows, :], feat_ref[:, cells]) + bcol_ref[rows, :]
            above = dot(w2_ref[rows, :], cot_ref[i])
            square = pre * pre
            tangent = jnp.tanh(root_two_pi * (pre + cubic * square * pre))
            hid_ref[rows, cells] = (0.5 * pre * (1.0 + tangent)).astype(bf16)
            slope = 0.5 * (1.0 + tangent) + 0.5 * pre * (1.0 - tangent * tangent) * root_two_pi * (
                1.0 + 3.0 * cubic * square
            )
            pg_ref[rows, cells] = (above * slope).astype(bf16)

    back = one_where(c512 == (r512 & 3) * 128 + (r512 >> 2))
    for h in range(2):
        rows = slice(h * 256, (h + 1) * 256)
        first = dot(back, dot_nt(feat_ref[...], pg_ref[rows, :]).astype(bf16)).astype(bf16)
        second = dot_nt(hid_ref[:, 0:NLON], cot_ref[0, rows, :])
        for i in range(1, SUB):
            second = second + dot_nt(hid_ref[:, i * NLON : (i + 1) * NLON], cot_ref[i, rows, :])
        second = second.astype(bf16)
        for c in range(2):
            at = (h * 2 + c) * 1024
            g0[at : at + 512, :] = first[:, c * 128 : (c + 1) * 128]
            g0[at + 512 : at + 1024, :] = second[:, c * 128 : (c + 1) * 128]
    bias = dot_nt(jnp.ones((16, CELLS), bf16), pg_ref[...])
    bias_tile = jnp.concatenate(
        [bias[0:1, c * 128 : (c + 1) * 128] for c in range(4)] + [jnp.zeros((4, 128), f32)], axis=0
    )
    c_copies = []
    for d in (1, 2, 3, 0):
        k = ((y + d) & (YS - 1))
        c_copies.append(
            start(g0.at[rows_at((1 - core) * YS + k, 512)], in_c.at[rows_at(k, 512)], gs.at[d], gr.at[d], core_peer(1))
        )
    c_bias = bias_round(bias_tile, bc, CORES, core, core_peer, 0)

    for i in range(SUB):
        grad = dot(w1p_ref[...], pg_ref[:, i * NLON : (i + 1) * NLON])
        for level in range(LEVELS):
            sg_ref[level, i * CH : (i + 1) * CH, :] = (
                grad[level * CH : (level + 1) * CH, :] * inverse(level, i)
            ).astype(bf16)

    def spread(n):
        lanes = slice(n * 256, (n + 1) * 256)

        def one_group(s, carry):
            total = None
            for level in range(LEVELS):
                it = s * 4 + level
                along = dot(sg_ref[level], col_ref[it, :, lanes])
                for i in range(SUB):
                    term = along[i * CH : (i + 1) * CH, :] * rowf_ref[it, i : i + 1, lanes]
                    total = term if total is None else total + term
            for q in range(REPS):
                d_out[n, q, rows_at(s, PART), :] = total[q * PART : (q + 1) * PART, :].astype(bf16)
            return carry

        lax.fori_loop(0, 4, one_group, 0)
        return [
            start(
                d_out.at[n, ((rep + d) & (REPS - 1))], d_in.at[n, d - 1],
                ds.at[n * 3 + d - 1], dr.at[n * 3 + d - 1], x_peer(d),
            )
            for d in range(1, REPS)
        ]

    def to_feeds(n, copies):
        finish(copies)
        total = d_out[n, rep].astype(f32)
        for d in range(REPS - 1):
            total = total + d_in[n, d].astype(f32)
        table2[n * 256 : (n + 1) * 256, :] = jnp.transpose(total).astype(bf16)

        def send(j, carry):
            peer = n * 16 + ((j + me) & 15)

            @pl.when(peer != me)
            def _():
                pltpu.make_async_remote_copy(
                    src_ref=table2.at[rows_at(peer, TILE)],
                    dst_ref=landing.at[rows_at(me, TILE)],
                    send_sem=ssem2,
                    recv_sem=rsem2,
                    device_id=(peer, rep),
                    device_id_type=MESH,
                ).start()

            return carry

        lax.fori_loop(0, 4, lambda g, c: [send(g * 4 + k, c) for k in range(4)][0], 0)

    y_copies = []
    for d, copy in zip((1, 2, 3, 0), c_copies):
        k = ((y + d) & (YS - 1))
        copy.wait()
        g1[rows_at(k, 512), :] = (
            g0[rows_at(core * YS + k, 512), :].astype(f32) + in_c[rows_at(k, 512), :].astype(f32)
        ).astype(bf16)
        if d:
            y_copies.append(start(g1.at[rows_at(k, 512)], in_y.at[d - 1], gs.at[3 + d], gr.at[3 + d], y_peer(d)))
    finish(c_bias)
    y_bias = bias_round(bias_sum(bc, CORES), by, YS, y, y_peer, 1)
    d0 = spread(0)
    d1 = spread(1)
    d2 = spread(2)
    finish(y_copies)
    total = g1[rows_at(y, 512), :].astype(f32)
    for d in range(YS - 1):
        total = total + in_y[d].astype(f32)
    g2[...] = total.astype(bf16)
    own_tile = rows_at(group_at, TILE)
    in_g[own_tile, :] = g2[own_tile, :]
    scattered = to_group(g2, lambda j: j * TILE, in_g, group_at * TILE, vs, vr)
    finish(y_bias)
    z_bias = bias_round(bias_sum(by, YS), bz, ZS, z, z_peer, 4)
    to_feeds(0, d0)
    d3 = spread(3)
    scattered.wait()
    total = in_g[0:TILE, :].astype(f32)
    for j in range(1, ZS * REPS):
        total = total + in_g[j * TILE : (j + 1) * TILE, :].astype(f32)
    block_at = core * 2048 + y * 512
    full_ref[pl.ds(pl.multiple_of(block_at + group_at * TILE, TILE), TILE), :] = total.astype(bf16)
    gathered = to_group(
        full_ref, lambda j: block_at + group_at * TILE, full_ref, block_at + group_at * TILE, vs2, vr2
    )
    to_feeds(1, d1)
    finish(z_bias)
    x_bias = bias_round(bias_sum(bz, ZS), bx, REPS, rep, x_peer, 11)
    to_feeds(2, d2)
    gathered.wait()

    def block(k):
        return full_ref.at[rows_at(core * YS + k, 512)]

    def to_core(d):
        k = ((y + YS - d) & (YS - 1))
        return start(block(k), block(k), as_.at[3 + d], ar.at[3 + d], core_peer(1))

    blocks = [start(block(y), block(y), as_.at[d - 1], ar.at[d - 1], y_peer(d)) for d in range(1, YS)]
    crossing = [to_core(0)]
    to_feeds(3, d3)
    landing[own, :] = table2[own, :]
    finish(x_bias)
    bias_total = bias_sum(bx, REPS)
    bias_row = jnp.concatenate([bias_total[c : c + 1, :] for c in range(4)], axis=1)
    eg_ref[PART : PART + 8, :] = jnp.broadcast_to(bias_row, (8, HID))
    for d in (1, 3, 2):
        blocks[d - 1].wait()
        crossing.append(to_core(d))
    tiles_done(me, rep, table2, landing, ssem2, rsem2).wait()
    turned = dot_nt(ident, landing[...]).astype(bf16)
    found = dot(turned, pick_ref[...])
    gradient = jnp.zeros((PART, REPORTS), f32)
    for s in range(4):
        gradient = gradient + jnp.where(within == float(s), found[s * PART : (s + 1) * PART, :], 0.0)
    eg_ref[0:PART, :] = gradient
    finish(crossing)
    for c in range(4):
        lanes = slice(c * 128, (c + 1) * 128)
        first_ref[:, lanes] = full_ref[c * 1024 : c * 1024 + 512, :]
        second_ref[:, lanes] = full_ref[c * 1024 + 512 : (c + 1) * 1024, :]


def sds(shape, dtype):
    return jax.ShapeDtypeStruct(shape, dtype)


def on_device(
    embeddings, route, place, scales, first_weight, first_bias, second_weight, out_cotangent
):
    dma = pltpu.SemaphoreType.DMA
    vm = pltpu.VMEM
    in_vmem = pl.BlockSpec(memory_space=pltpu.VMEM)
    anywhere = pl.BlockSpec(memory_space=pl.ANY)
    gradient, first, second = pl.pallas_call(
        grid_kernel,
        out_shape=[sds((PART + 8, REPORTS), f32), sds((512, 512), bf16), sds((512, 512), bf16)],
        in_specs=[
            in_vmem, in_vmem, in_vmem, pl.BlockSpec(memory_space=pltpu.SMEM),
            anywhere, in_vmem, anywhere, anywhere,
        ],
        out_specs=[in_vmem] * 3,
        scratch_shapes=[
            vm((ROWS, 128), bf16), vm((REPS, ROWS, 128), bf16), vm((ROWS, REPORTS), bf16),
            vm((512, HID), bf16), vm((HID, 512), bf16), vm((SUB, 512, NLON), bf16),
            vm((4, CH, ROWS), bf16), vm((128, ROWS), f32),
            vm((4, 16, ROWS), f32), vm((4, 8, ROWS), f32), vm((4, 16, ROWS), f32),
            vm((16, NLON, ROWS), bf16), vm((16, SUB, 16, ROWS), bf16), vm((16, 16, ROWS), bf16),
            vm((16, 8, ROWS), f32), vm((SUB * CH + 16, ROWS), bf16),
            vm((LEVELS, SUB * CH + 16, NLON), f32),
            vm((512, CELLS), bf16), vm((512, HID), bf16), vm((HID, 512), bf16), vm((HID, 1), f32),
            vm((HID, CELLS), bf16), vm((HID, CELLS), bf16), vm((LEVELS, SUB * CH, NLON), bf16),
            vm((4, REPS, 128, 256), bf16), vm((4, REPS - 1, 128, 256), bf16),
            vm((ROWS, 128), bf16), vm((ROWS, 128), bf16),
            vm((GROWS, 128), bf16), vm((2048, 128), bf16), vm((512, 128), bf16),
            vm((2048, 128), bf16), vm((3, 512, 128), bf16), vm((512, 128), bf16),
            vm((GROWS, 128), bf16),
            vm((CORES, 8, 128), f32), vm((YS, 8, 128), f32), vm((ZS, 8, 128), f32), vm((REPS, 8, 128), f32),
            dma((3,)), dma, dma, dma, dma, dma, dma, dma, dma,
            dma((12,)), dma((12,)), dma((12,)), dma((12,)),
            dma((7,)), dma((7,)), dma((14,)), dma((14,)), dma((7,)), dma((7,)),
        ],
        compiler_params=pltpu.CompilerParams(
            collective_id=0, has_side_effects=True, vmem_limit_bytes=53 << 20
        ),
    )(
        embeddings, route.reshape(1, REPORTS), place, scales,
        first_weight, first_bias.reshape(1, HID), second_weight, out_cotangent.transpose(1, 0, 2),
    )
    return (gradient[0:PART], first.astype(f32), gradient[PART], second.astype(f32))


def solution(mesh):
    return jax.shard_map(
        on_device,
        mesh=mesh,
        in_specs=(
            P("rep", "band"),
            P("band", None),
            P(None, "band"),
            P(),
            P(),
            P(),
            P(),
            P(None, ("band", "rep"), None),
        ),
        out_specs=(P("rep", "band"), P(), P(), P()),
        check_vma=False,
    )
```

```python
import jax
import jax.numpy as jnp
from jax import lax
from jax.experimental import pallas as pl
from jax.experimental.pallas import tpu as pltpu
from jax.sharding import PartitionSpec as P

MESH = pl.DeviceIdType.MESH
bf16 = jnp.bfloat16
f32 = jnp.float32

root_two_pi = 0.7978845608028654
cubic = 0.044715
half_log2e = 0.8493218002880191

BANDS = 64
REPS = 4
YS, ZS, CORES = 4, 8, 2
CAP = 20
TILE = 16
ROWS = BANDS * TILE
REPORTS = 512
LEVELS = 4
CH = 128
PART = 32
SUB = 3
NLON = 256
LAT = 12.0
CELLS = SUB * NLON
HID = 512
GROWS = 4096


def iota(shape, dim):
    return lax.broadcasted_iota(jnp.int32, shape, dim)


def one_where(cond):
    return jnp.where(cond, 1.0, 0.0).astype(bf16)


def dot(a, b):
    return lax.dot_general(a, b, (((1,), (0,)), ((), ())), preferred_element_type=f32)


def dot_nt(a, b):
    return lax.dot_general(a, b, (((1,), (1,)), ((), ())), preferred_element_type=f32)


def eye(n):
    return one_where(iota((n, n), 0) == iota((n, n), 1))


def row_keys(start, rows):
    row = iota((rows, 1), 0) + start
    band = row >> 4
    ok = row & 15
    key = jnp.where(ok == 15, -1000, (band - 1) * 5 + ok).astype(f32)
    place_band = jnp.where(ok == 15, band, -1000).astype(f32)
    return key, place_band


def report_ranks(route_ref):
    owner = route_ref[...].astype(f32)
    rank = jnp.zeros((1, REPORTS), f32)
    for part in range(4):
        mine = iota((128, REPORTS), 0) + part * 128
        lane = iota((128, REPORTS), 1)
        col = jnp.sum(jnp.where(mine == lane, owner, 0.0), axis=1, keepdims=True)
        rank = rank + jnp.sum(
            jnp.where((col == owner) & (mine < lane), 1.0, 0.0), axis=0, keepdims=True
        )
    return owner, rank


def greet(me, rep):
    barrier = pltpu.get_barrier_semaphore()

    def band_peer(d, carry):
        pl.semaphore_signal(
            barrier, inc=1, device_id=(((me + d) & (BANDS - 1)), rep), device_id_type=MESH
        )
        return carry

    lax.fori_loop(0, 9, lambda g, c: [band_peer(g * 7 + k, c) for k in range(1, 8)][0], 0)
    for d in range(1, REPS):
        pl.semaphore_signal(
            barrier, inc=1, device_id=(me, ((rep + d) & (REPS - 1))), device_id_type=MESH
        )
    return barrier


def send_tiles(me, rep, table, landing, send_sem, recv_sem):
    def send(d, carry):
        peer = ((me + d) & (BANDS - 1))
        pltpu.make_async_remote_copy(
            src_ref=table.at[pl.ds(pl.multiple_of(peer * TILE, TILE), TILE)],
            dst_ref=landing.at[pl.ds(pl.multiple_of(me * TILE, TILE), TILE)],
            send_sem=send_sem,
            recv_sem=recv_sem,
            device_id=(peer, rep),
            device_id_type=MESH,
        ).start()
        return carry

    lax.fori_loop(0, 9, lambda g, c: [send(g * 7 + k, c) for k in range(1, 8)][0], 0)


def tiles_done(me, rep, table, landing, send_sem, recv_sem):
    return pltpu.make_async_remote_copy(
        src_ref=table.at[pl.ds(0, ROWS - TILE)],
        dst_ref=landing.at[pl.ds(0, ROWS - TILE)],
        send_sem=send_sem,
        recv_sem=recv_sem,
        device_id=(((me + 1) & (BANDS - 1)), rep),
        device_id_type=MESH,
    )


def decode_places(t, rep, expand, base_ref, east_ref, valid_ref):
    lane = iota((1, ROWS), 1)
    ok = lane & 15
    o = (ok >= 5).astype(jnp.int32) + (ok >= 10).astype(jnp.int32) + (ok >= 15).astype(jnp.int32)
    k4 = (ok - 5 * o) * 4
    v = lax.rem(t + 2, 3) + o
    third = jnp.where(v >= 3, v - 3, v)
    code = third * 20 + k4
    lam = iota((64, ROWS), 0)
    low = expand[0:64, :]
    high = expand[64:128, :]
    count = jnp.sum(jnp.where(lam == third + 60, low, 0.0), axis=0, keepdims=True)
    offset = (1 - o).astype(f32) * LAT + (rep * SUB).astype(f32) + 0.5
    for s in range(4):
        hit = lam == code + s
        north = jnp.sum(jnp.where(hit, low, 0.0), axis=0, keepdims=True)
        east = jnp.sum(jnp.where(hit, high, 0.0), axis=0, keepdims=True)
        valid = jnp.where((ok < 15) & ((k4 + s).astype(f32) < count), 1.0, 0.0)
        base_ref[s] = jnp.broadcast_to(offset - north * LAT, (16, ROWS))
        valid_ref[s] = jnp.broadcast_to(valid, (16, ROWS))
        east_ref[s] = jnp.broadcast_to(east * float(NLON), (8, ROWS))


def build_table(emb_ref, place_ref, owner, rank, pick_ref, table):
    quad = jnp.floor(rank * 0.25)
    within = rank - 4.0 * quad
    key = owner * 5.0 + quad
    third = owner - 3.0 * jnp.floor((owner + 0.5) * (1.0 / 3.0))
    emb = emb_ref[...].astype(f32)
    emb_b = jnp.concatenate(
        [jnp.where(within == float(s), emb, 0.0) for s in range(4)], axis=0
    ).astype(bf16)
    lam = iota((128, REPORTS), 0).astype(f32)
    spot = third * 20.0 + rank
    north = place_ref[0:1, :].astype(f32)
    east = place_ref[1:2, :].astype(f32)
    place_b = (
        jnp.where(lam == spot, north, 0.0)
        + jnp.where(lam == spot + 64.0, east, 0.0)
        + jnp.where(lam == third + 60.0, 1.0, 0.0)
    ).astype(bf16)
    for part in range(8):
        rows = slice(part * 128, (part + 1) * 128)
        row_key, place_band = row_keys(part * 128, 128)
        pick = one_where(row_key == key)
        pick_ref[rows, :] = pick
        near = one_where(jnp.abs(place_band - owner) <= 1.0)
        table[rows, :] = (dot_nt(pick, emb_b) + dot_nt(near, place_b)).astype(bf16)
    return within


def kernels(it, scales_ref, base_ref, east_ref, valid_ref, col_ref, rk_ref, mix_ref, rowf_ref):
    s = it >> 2
    reach = scales_ref[it & 3] * LAT
    scale = half_log2e / jnp.full((1, 128), reach, f32)
    scale_wide = jnp.concatenate([scale] * 8, axis=1)
    east = east_ref[s, 0:1, :] * scale_wide
    for c in range(8):
        centre = (iota((32, 128), 0).astype(f32) + (c * 32 + 0.5)) * scale
        for b in range(8):
            gap = centre - east[:, b * 128 : (b + 1) * 128]
            col_ref[it, c * 32 : (c + 1) * 32, b * 128 : (b + 1) * 128] = jnp.exp2(
                -(gap * gap)
            ).astype(bf16)
    valid = valid_ref[s]
    wide = []
    for i in range(SUB):
        gap = (base_ref[s] + float(i)) * scale_wide
        row = (jnp.exp2(-(gap * gap)) * valid).astype(bf16)
        rk_ref[it, i] = row
        wide.append(row.astype(f32))
    sub = iota((16, ROWS), 0)
    mixed = jnp.where(
        sub == 0, wide[0], jnp.where(sub == 1, wide[1], jnp.where(sub == 2, wide[2], 0.0))
    )
    rowf_ref[it] = mixed[0:8, :]
    mix_ref[it] = mixed.astype(bf16)


def grid_kernel(
    emb_ref, route_ref, place_ref, scales_ref, w1_hbm, b1_ref, w2_hbm, cot_hbm,
    eg_ref, grads_ref, bout_ref,
    table, rr_ref, pick_ref, w1_ref, w2_ref, cot_ref,
    emb_t, expand, base_ref, east_ref, valid_ref, col_ref, rk_ref, mix_ref, rowf_ref, w_ref, acc_ref,
    feat_ref, w1p_ref, w1t_ref, bcol_ref, hid_ref, pg_ref, sg_ref,
    d_out, d_in, table2, landing, g0, g1, g2, in_c, in_y, in_g, full_ref, bc, by, bz, bx,
    loads, ssem, rsem, ssem2, rsem2, vs, vr, vs2, vr2, xs, xr, ds, dr, gs, gr, bs, br, as_, ar,
):
    me = lax.axis_index("band")
    rep = lax.axis_index("rep")
    core = ((me) & (CORES - 1))
    z = (me >> 1) & (ZS - 1)
    y = me >> 4

    def core_peer(d):
        return me + 1 - 2 * core, rep

    def y_peer(d):
        return ((y + d) & (YS - 1)) * (CORES * ZS) + z * CORES + core, rep

    def z_peer(d):
        return y * (CORES * ZS) + ((z + d) & (ZS - 1)) * CORES + core, rep

    def x_peer(d):
        return me, ((rep + d) & (REPS - 1))

    def start(src, dst, send, recv, device):
        copy = pltpu.make_async_remote_copy(
            src_ref=src, dst_ref=dst, send_sem=send, recv_sem=recv, device_id=device, device_id_type=MESH
        )
        copy.start()
        return copy

    def rows_at(index, size):
        return pl.ds(pl.multiple_of(index * size, size), size)

    def bias_round(value, slots, n, mine, peer, base):
        slots[mine] = value
        return [
            start(slots.at[mine], slots.at[mine], bs.at[base + d - 1], br.at[base + d - 1], peer(d))
            for d in range(1, n)
        ]

    def bias_sum(slots, n):
        total = slots[0]
        for k in range(1, n):
            total = total + slots[k]
        return total

    def finish(copies):
        for copy in copies:
            copy.wait()

    def ring_gather(piece, sems, base, peer):
        send, recv = sems
        right, left = peer(1), peer(3)
        one = start(piece(0, 0), piece(0, 0), send.at[base], recv.at[base], right)
        two = start(piece(0, 1), piece(0, 1), send.at[base + 1], recv.at[base + 1], left)
        three = start(piece(0, 1), piece(0, 1), send.at[base + 2], recv.at[base + 2], right)
        four = start(piece(0, 0), piece(0, 0), send.at[base + 3], recv.at[base + 3], left)

        def forward():
            one.wait_recv()
            five = start(piece(3, 0), piece(3, 0), send.at[base + 4], recv.at[base + 4], right)
            two.wait_recv()
            six = start(piece(1, 1), piece(1, 1), send.at[base + 5], recv.at[base + 5], left)

            def rest():
                one.wait_send()
                two.wait_send()
                finish([three, four, five, six])

            return rest

        return forward

    group_at = z * REPS + rep

    def group_peer(j):
        return y * (CORES * ZS) + (j >> 2) * CORES + core, j & 3

    def to_group(src, src_at, dst, dst_at, send, recv):
        def one(d, carry):
            j = ((group_at + d) & (ZS * REPS - 1))
            pltpu.make_async_remote_copy(
                src_ref=src.at[pl.ds(pl.multiple_of(src_at(j), TILE), TILE)],
                dst_ref=dst.at[pl.ds(pl.multiple_of(dst_at, TILE), TILE)],
                send_sem=send, recv_sem=recv, device_id=group_peer(j), device_id_type=MESH,
            ).start()
            return carry

        for d in range(1, ZS * REPS):
            one(d, 0)
        rows = pl.ds(0, (ZS * REPS - 1) * TILE)
        return pltpu.make_async_remote_copy(
            src_ref=src.at[rows], dst_ref=dst.at[rows], send_sem=send, recv_sem=recv,
            device_id=group_peer(((group_at + 1) & (ZS * REPS - 1))), device_id_type=MESH,
        )

    barrier = greet(me, rep)
    held = []
    for k, (src, dst) in enumerate(((w1_hbm, w1_ref), (w2_hbm, w2_ref), (cot_hbm, cot_ref))):
        copy = pltpu.make_async_copy(src, dst, loads.at[k])
        copy.start()
        held.append(copy)

    owner, rank = report_ranks(route_ref)
    within = build_table(emb_ref, place_ref, owner, rank, pick_ref, table)
    pl.semaphore_wait(barrier, BANDS - 1 + REPS - 1)
    mine = rr_ref.at[rep]
    send_tiles(me, rep, table, mine, ssem, rsem)
    own = rows_at(me, TILE)
    rr_ref[rep, own, :] = table[own, :]

    finish(held)
    r512 = iota((512, 512), 0)
    c512 = iota((512, 512), 1)
    w1p_ref[...] = dot(one_where(c512 == (r512 & 127) * 4 + (r512 >> 7)), w1_ref[...]).astype(bf16)
    w1t_ref[...] = dot_nt(eye(512), w1p_ref[...]).astype(bf16)
    bcol_ref[...] = jnp.sum(jnp.where(r512 == c512, b1_ref[...], 0.0), axis=1, keepdims=True)

    done = tiles_done(me, rep, table, mine, ssem, rsem)
    done.wait_recv()
    def report_piece(half):
        return lambda k, h: rr_ref.at[((rep + k) & (REPS - 1)), pl.ds(half * 512 + h * 256, 256)]

    forward_first = ring_gather(report_piece(0), (xs, xr), 0, x_peer)
    ident = eye(128)
    group = one_where(
        ((iota((128, 128), 0) >> 4) == (iota((128, 128), 1) >> 4)) & ((iota((128, 128), 0) & 15) == 15)
    )
    turned = dot_nt(ident, rr_ref[rep]).astype(bf16)
    for b in range(8):
        expand[:, b * 128 : (b + 1) * 128] = dot(turned[:, b * 128 : (b + 1) * 128], group)
    decode_places(me, rep, expand, base_ref, east_ref, valid_ref)
    acc_ref[...] = jnp.zeros_like(acc_ref)

    def make(it, carry):
        kernels(it, scales_ref, base_ref, east_ref, valid_ref, col_ref, rk_ref, mix_ref, rowf_ref)
        return carry

    lax.fori_loop(0, 16, make, 0)
    first_half = forward_first()
    forward_second = ring_gather(report_piece(1), (xs, xr), 6, x_peer)

    for half in range(2):
        lanes = slice(half * 512, (half + 1) * 512)
        if half == 0:
            first_half()
            second_half = forward_second()
        else:
            second_half()
        for q in range(REPS):
            turned = dot_nt(ident, rr_ref[q, lanes, :]).astype(bf16)
            for s in range(4):
                emb_t[s, q * PART : (q + 1) * PART, lanes] = turned[s * PART : (s + 1) * PART, :]

        def splat(it, carry):
            s = it >> 2
            level = it & 3
            rows = [rk_ref[it, i, :, lanes] for i in range(SUB)]
            w_ref[SUB * CH : SUB * CH + 16, lanes] = mix_ref[it, :, lanes]
            for c in range(8):
                e = emb_t[s, c * 16 : (c + 1) * 16, lanes]
                for i in range(SUB):
                    w_ref[i * CH + c * 16 : i * CH + (c + 1) * 16, lanes] = e * rows[i]
            acc_ref[level] += dot_nt(w_ref[:, lanes], col_ref[it, :, lanes])
            return carry

        lax.fori_loop(0, 16, splat, 0)
    done.wait_send()

    def inverse(level, i):
        return 1.0 / (acc_ref[level, SUB * CH + i : SUB * CH + i + 1, :] + 1.0)

    for level in range(LEVELS):
        for i in range(SUB):
            feat_ref[level * CH : (level + 1) * CH, i * NLON : (i + 1) * NLON] = (
                acc_ref[level, i * CH : (i + 1) * CH, :] * inverse(level, i)
            ).astype(bf16)

    for i in range(SUB):
        cells = slice(i * NLON, (i + 1) * NLON)
        for h in range(2):
            rows = slice(h * 256, (h + 1) * 256)
            pre = dot(w1t_ref[rows, :], feat_ref[:, cells]) + bcol_ref[rows, :]
            above = dot(w2_ref[rows, :], cot_ref[i])
            square = pre * pre
            tangent = jnp.tanh(root_two_pi * (pre + cubic * square * pre))
            hid_ref[rows, cells] = (0.5 * pre * (1.0 + tangent)).astype(bf16)
            slope = 0.5 * (1.0 + tangent) + 0.5 * pre * (1.0 - tangent * tangent) * root_two_pi * (
                1.0 + 3.0 * cubic * square
            )
            pg_ref[rows, cells] = (above * slope).astype(bf16)

    back = one_where(c512 == (r512 & 3) * 128 + (r512 >> 2))
    for h in range(2):
        rows = slice(h * 256, (h + 1) * 256)
        first = dot(back, dot_nt(feat_ref[...], pg_ref[rows, :]).astype(bf16)).astype(bf16)
        second = dot_nt(hid_ref[:, 0:NLON], cot_ref[0, rows, :])
        for i in range(1, SUB):
            second = second + dot_nt(hid_ref[:, i * NLON : (i + 1) * NLON], cot_ref[i, rows, :])
        second = second.astype(bf16)
        for c in range(2):
            at = (h * 2 + c) * 1024
            g0[at : at + 512, :] = first[:, c * 128 : (c + 1) * 128]
            g0[at + 512 : at + 1024, :] = second[:, c * 128 : (c + 1) * 128]
    bias = dot_nt(jnp.ones((16, CELLS), bf16), pg_ref[...])
    bias_tile = jnp.concatenate(
        [bias[0:1, c * 128 : (c + 1) * 128] for c in range(4)] + [jnp.zeros((4, 128), f32)], axis=0
    )
    c_copies = []
    for d in (1, 2, 3, 0):
        k = ((y + d) & (YS - 1))
        c_copies.append(
            start(g0.at[rows_at((1 - core) * YS + k, 512)], in_c.at[rows_at(k, 512)], gs.at[d], gr.at[d], core_peer(1))
        )
    c_bias = bias_round(bias_tile, bc, CORES, core, core_peer, 0)

    for i in range(SUB):
        grad = dot(w1p_ref[...], pg_ref[:, i * NLON : (i + 1) * NLON])
        for level in range(LEVELS):
            sg_ref[level, i * CH : (i + 1) * CH, :] = (
                grad[level * CH : (level + 1) * CH, :] * inverse(level, i)
            ).astype(bf16)

    def spread(n):
        lanes = slice(n * 256, (n + 1) * 256)

        def one_group(s, carry):
            total = None
            for level in range(LEVELS):
                it = s * 4 + level
                along = dot(sg_ref[level], col_ref[it, :, lanes])
                for i in range(SUB):
                    term = along[i * CH : (i + 1) * CH, :] * rowf_ref[it, i : i + 1, lanes]
                    total = term if total is None else total + term
            for q in range(REPS):
                d_out[n, q, rows_at(s, PART), :] = total[q * PART : (q + 1) * PART, :].astype(bf16)
            return carry

        lax.fori_loop(0, 4, one_group, 0)
        return [
            start(
                d_out.at[n, ((rep + d) & (REPS - 1))], d_in.at[n, d - 1],
                ds.at[n * 3 + d - 1], dr.at[n * 3 + d - 1], x_peer(d),
            )
            for d in range(1, REPS)
        ]

    def to_feeds(n, copies):
        finish(copies)
        total = d_out[n, rep].astype(f32)
        for d in range(REPS - 1):
            total = total + d_in[n, d].astype(f32)
        table2[n * 256 : (n + 1) * 256, :] = jnp.transpose(total).astype(bf16)

        def send(j, carry):
            peer = n * 16 + ((j + me) & 15)

            @pl.when(peer != me)
            def _():
                pltpu.make_async_remote_copy(
                    src_ref=table2.at[rows_at(peer, TILE)],
                    dst_ref=landing.at[rows_at(me, TILE)],
                    send_sem=ssem2,
                    recv_sem=rsem2,
                    device_id=(peer, rep),
                    device_id_type=MESH,
                ).start()

            return carry

        lax.fori_loop(0, 4, lambda g, c: [send(g * 4 + k, c) for k in range(4)][0], 0)

    y_copies = []
    for d, copy in zip((1, 2, 3, 0), c_copies):
        k = ((y + d) & (YS - 1))
        copy.wait()
        g1[rows_at(k, 512), :] = (
            g0[rows_at(core * YS + k, 512), :].astype(f32) + in_c[rows_at(k, 512), :].astype(f32)
        ).astype(bf16)
        if d:
            y_copies.append(start(g1.at[rows_at(k, 512)], in_y.at[d - 1], gs.at[3 + d], gr.at[3 + d], y_peer(d)))
    finish(c_bias)
    y_bias = bias_round(bias_sum(bc, CORES), by, YS, y, y_peer, 1)
    d0 = spread(0)
    d1 = spread(1)
    d2 = spread(2)
    finish(y_copies)
    total = g1[rows_at(y, 512), :].astype(f32)
    for d in range(YS - 1):
        total = total + in_y[d].astype(f32)
    g2[...] = total.astype(bf16)
    own_tile = rows_at(group_at, TILE)
    in_g[own_tile, :] = g2[own_tile, :]
    scattered = to_group(g2, lambda j: j * TILE, in_g, group_at * TILE, vs, vr)
    finish(y_bias)
    z_bias = bias_round(bias_sum(by, YS), bz, ZS, z, z_peer, 4)
    to_feeds(0, d0)
    d3 = spread(3)
    scattered.wait()
    total = in_g[0:TILE, :].astype(f32)
    for j in range(1, ZS * REPS):
        total = total + in_g[j * TILE : (j + 1) * TILE, :].astype(f32)
    block_at = core * 2048 + y * 512
    full_ref[pl.ds(pl.multiple_of(block_at + group_at * TILE, TILE), TILE), :] = total.astype(bf16)
    gathered = to_group(
        full_ref, lambda j: block_at + group_at * TILE, full_ref, block_at + group_at * TILE, vs2, vr2
    )
    to_feeds(1, d1)
    finish(z_bias)
    x_bias = bias_round(bias_sum(bz, ZS), bx, REPS, rep, x_peer, 11)
    to_feeds(2, d2)
    gathered.wait()

    def block(k):
        return full_ref.at[rows_at(core * YS + k, 512)]

    def to_core(d):
        k = ((y + YS - d) & (YS - 1))
        return start(block(k), block(k), as_.at[3 + d], ar.at[3 + d], core_peer(1))

    blocks = [start(block(y), block(y), as_.at[d - 1], ar.at[d - 1], y_peer(d)) for d in range(1, YS)]
    crossing = [to_core(0)]
    to_feeds(3, d3)
    landing[own, :] = table2[own, :]
    finish(x_bias)
    bias_total = bias_sum(bx, REPS)
    for c in range(4):
        bout_ref[:, c * 128 : (c + 1) * 128] = bias_total[c : c + 1, :]
    for d in (1, 3, 2):
        blocks[d - 1].wait()
        crossing.append(to_core(d))
    tiles_done(me, rep, table2, landing, ssem2, rsem2).wait()
    turned = dot_nt(ident, landing[...]).astype(bf16)
    found = dot(turned, pick_ref[...])
    gradient = jnp.zeros((PART, REPORTS), f32)
    for s in range(4):
        gradient = gradient + jnp.where(within == float(s), found[s * PART : (s + 1) * PART, :], 0.0)
    eg_ref[...] = gradient
    finish(crossing)
    for c in range(4):
        grads_ref[:, c * 128 : (c + 1) * 128] = full_ref[c * 1024 : (c + 1) * 1024, :]


def sds(shape, dtype):
    return jax.ShapeDtypeStruct(shape, dtype)


def on_device(
    embeddings, route, place, scales, first_weight, first_bias, second_weight, out_cotangent
):
    dma = pltpu.SemaphoreType.DMA
    vm = pltpu.VMEM
    in_vmem = pl.BlockSpec(memory_space=pltpu.VMEM)
    anywhere = pl.BlockSpec(memory_space=pl.ANY)
    gradient, grads, bias = pl.pallas_call(
        grid_kernel,
        out_shape=[sds((PART, REPORTS), f32), sds((1024, 512), bf16), sds((1, HID), f32)],
        in_specs=[
            in_vmem, in_vmem, in_vmem, pl.BlockSpec(memory_space=pltpu.SMEM),
            anywhere, in_vmem, anywhere, anywhere,
        ],
        out_specs=[in_vmem] * 3,
        scratch_shapes=[
            vm((ROWS, 128), bf16), vm((REPS, ROWS, 128), bf16), vm((ROWS, REPORTS), bf16),
            vm((512, HID), bf16), vm((HID, 512), bf16), vm((SUB, 512, NLON), bf16),
            vm((4, CH, ROWS), bf16), vm((128, ROWS), f32),
            vm((4, 16, ROWS), f32), vm((4, 8, ROWS), f32), vm((4, 16, ROWS), f32),
            vm((16, NLON, ROWS), bf16), vm((16, SUB, 16, ROWS), bf16), vm((16, 16, ROWS), bf16),
            vm((16, 8, ROWS), f32), vm((SUB * CH + 16, ROWS), bf16),
            vm((LEVELS, SUB * CH + 16, NLON), f32),
            vm((512, CELLS), bf16), vm((512, HID), bf16), vm((HID, 512), bf16), vm((HID, 1), f32),
            vm((HID, CELLS), bf16), vm((HID, CELLS), bf16), vm((LEVELS, SUB * CH, NLON), bf16),
            vm((4, REPS, 128, 256), bf16), vm((4, REPS - 1, 128, 256), bf16),
            vm((ROWS, 128), bf16), vm((ROWS, 128), bf16),
            vm((GROWS, 128), bf16), vm((2048, 128), bf16), vm((512, 128), bf16),
            vm((2048, 128), bf16), vm((3, 512, 128), bf16), vm((512, 128), bf16),
            vm((GROWS, 128), bf16),
            vm((CORES, 8, 128), f32), vm((YS, 8, 128), f32), vm((ZS, 8, 128), f32), vm((REPS, 8, 128), f32),
            dma((3,)), dma, dma, dma, dma, dma, dma, dma, dma,
            dma((12,)), dma((12,)), dma((12,)), dma((12,)),
            dma((7,)), dma((7,)), dma((14,)), dma((14,)), dma((7,)), dma((7,)),
        ],
        compiler_params=pltpu.CompilerParams(
            collective_id=0, has_side_effects=True, vmem_limit_bytes=60 << 20
        ),
    )(
        embeddings, route.reshape(1, REPORTS), place, scales,
        first_weight, first_bias.reshape(1, HID), second_weight, out_cotangent.transpose(1, 0, 2),
    )
    return (gradient, grads[0:512].astype(f32), bias.reshape(HID), grads[512:1024].astype(f32))


def solution(mesh):
    return jax.shard_map(
        on_device,
        mesh=mesh,
        in_specs=(
            P("rep", "band"),
            P("band", None),
            P(None, "band"),
            P(),
            P(),
            P(),
            P(),
            P(None, ("band", "rep"), None),
        ),
        out_specs=(P("rep", "band"), P(), P(), P()),
        check_vma=False,
    )
```

```python
import jax
import jax.numpy as jnp
from jax import lax
from jax.experimental import pallas as pl
from jax.experimental.pallas import tpu as pltpu
from jax.sharding import PartitionSpec as P

MESH = pl.DeviceIdType.MESH
bf16 = jnp.bfloat16
f32 = jnp.float32

root_two_pi = 0.7978845608028654
cubic = 0.044715
half_log2e = 0.8493218002880191

BANDS = 64
REPS = 4
YS, ZS, CORES = 4, 8, 2
CAP = 20
TILE = 16
ROWS = BANDS * TILE
REPORTS = 512
LEVELS = 4
CH = 128
PART = 32
SUB = 3
NLON = 256
LAT = 12.0
CELLS = SUB * NLON
HID = 512
GROWS = 4096


def iota(shape, dim):
    return lax.broadcasted_iota(jnp.int32, shape, dim)


def one_where(cond):
    return jnp.where(cond, 1.0, 0.0).astype(bf16)


def dot(a, b):
    return lax.dot_general(a, b, (((1,), (0,)), ((), ())), preferred_element_type=f32)


def dot_nt(a, b):
    return lax.dot_general(a, b, (((1,), (1,)), ((), ())), preferred_element_type=f32)


def eye(n):
    return one_where(iota((n, n), 0) == iota((n, n), 1))


def row_keys(start, rows):
    row = iota((rows, 1), 0) + start
    band = row >> 4
    ok = row & 15
    key = jnp.where(ok == 15, -1000, (band - 1) * 5 + ok).astype(f32)
    place_band = jnp.where(ok == 15, band, -1000).astype(f32)
    return key, place_band


def report_ranks(route_ref):
    owner = route_ref[...].astype(f32)
    rank = jnp.zeros((1, REPORTS), f32)
    for part in range(4):
        mine = iota((128, REPORTS), 0) + part * 128
        lane = iota((128, REPORTS), 1)
        col = jnp.sum(jnp.where(mine == lane, owner, 0.0), axis=1, keepdims=True)
        rank = rank + jnp.sum(
            jnp.where((col == owner) & (mine < lane), 1.0, 0.0), axis=0, keepdims=True
        )
    return owner, rank


def greet(me, rep):
    barrier = pltpu.get_barrier_semaphore()

    def band_peer(d, carry):
        pl.semaphore_signal(
            barrier, inc=1, device_id=(((me + d) & (BANDS - 1)), rep), device_id_type=MESH
        )
        return carry

    lax.fori_loop(0, 9, lambda g, c: [band_peer(g * 7 + k, c) for k in range(1, 8)][0], 0)
    for d in range(1, REPS):
        pl.semaphore_signal(
            barrier, inc=1, device_id=(me, ((rep + d) & (REPS - 1))), device_id_type=MESH
        )
    return barrier


def send_tiles(me, rep, table, landing, send_sem, recv_sem):
    def send(d, carry):
        peer = ((me + d) & (BANDS - 1))
        pltpu.make_async_remote_copy(
            src_ref=table.at[pl.ds(pl.multiple_of(peer * TILE, TILE), TILE)],
            dst_ref=landing.at[pl.ds(pl.multiple_of(me * TILE, TILE), TILE)],
            send_sem=send_sem,
            recv_sem=recv_sem,
            device_id=(peer, rep),
            device_id_type=MESH,
        ).start()
        return carry

    lax.fori_loop(0, 9, lambda g, c: [send(g * 7 + k, c) for k in range(1, 8)][0], 0)


def tiles_done(me, rep, table, landing, send_sem, recv_sem):
    return pltpu.make_async_remote_copy(
        src_ref=table.at[pl.ds(0, ROWS - TILE)],
        dst_ref=landing.at[pl.ds(0, ROWS - TILE)],
        send_sem=send_sem,
        recv_sem=recv_sem,
        device_id=(((me + 1) & (BANDS - 1)), rep),
        device_id_type=MESH,
    )


def decode_places(t, rep, expand, base_ref, east_ref, valid_ref):
    lane = iota((1, ROWS), 1)
    ok = lane & 15
    o = (ok >= 5).astype(jnp.int32) + (ok >= 10).astype(jnp.int32) + (ok >= 15).astype(jnp.int32)
    k4 = (ok - 5 * o) * 4
    v = lax.rem(t + 2, 3) + o
    third = jnp.where(v >= 3, v - 3, v)
    code = third * 20 + k4
    lam = iota((64, ROWS), 0)
    low = expand[0:64, :]
    high = expand[64:128, :]
    count = jnp.sum(jnp.where(lam == third + 60, low, 0.0), axis=0, keepdims=True)
    offset = (1 - o).astype(f32) * LAT + (rep * SUB).astype(f32) + 0.5
    for s in range(4):
        hit = lam == code + s
        north = jnp.sum(jnp.where(hit, low, 0.0), axis=0, keepdims=True)
        east = jnp.sum(jnp.where(hit, high, 0.0), axis=0, keepdims=True)
        valid = jnp.where((ok < 15) & ((k4 + s).astype(f32) < count), 1.0, 0.0)
        base_ref[s] = jnp.broadcast_to(offset - north * LAT, (16, ROWS))
        valid_ref[s] = jnp.broadcast_to(valid, (16, ROWS))
        east_ref[s] = jnp.broadcast_to(east * float(NLON), (8, ROWS))


def build_table(emb_ref, place_ref, owner, rank, pick_ref, near_ref, table):
    quad = jnp.floor(rank * 0.25)
    within = rank - 4.0 * quad
    key = owner * 5.0 + quad
    third = owner - 3.0 * jnp.floor((owner + 0.5) * (1.0 / 3.0))
    emb = emb_ref[...].astype(f32)
    emb_b = jnp.concatenate(
        [jnp.where(within == float(s), emb, 0.0) for s in range(4)], axis=0
    ).astype(bf16)
    lam = iota((128, REPORTS), 0).astype(f32)
    spot = third * 20.0 + rank
    north = place_ref[0:1, :].astype(f32)
    east = place_ref[1:2, :].astype(f32)
    place_b = (
        jnp.where(lam == spot, north, 0.0)
        + jnp.where(lam == spot + 64.0, east, 0.0)
        + jnp.where(lam == third + 60.0, 1.0, 0.0)
    ).astype(bf16)
    for part in range(8):
        rows = slice(part * 128, (part + 1) * 128)
        row_key, place_band = row_keys(part * 128, 128)
        pick = one_where(row_key == key)
        pick_ref[rows, :] = pick
        near_ref[rows, :] = one_where(jnp.abs(place_band - owner) <= 1.0)
    table[...] = (dot_nt(pick_ref[...], emb_b) + dot_nt(near_ref[...], place_b)).astype(bf16)
    return within


def kernels(it, scales_ref, base_ref, east_ref, valid_ref, col_ref, rk_ref, mix_ref, rowf_ref):
    s = it >> 2
    reach = scales_ref[it & 3] * LAT
    scale = half_log2e / jnp.full((1, 128), reach, f32)
    scale_wide = jnp.concatenate([scale] * 8, axis=1)
    east = east_ref[s, 0:1, :] * scale_wide
    for c in range(8):
        centre = (iota((32, 128), 0).astype(f32) + (c * 32 + 0.5)) * scale
        for b in range(8):
            gap = centre - east[:, b * 128 : (b + 1) * 128]
            col_ref[it, c * 32 : (c + 1) * 32, b * 128 : (b + 1) * 128] = jnp.exp2(
                -(gap * gap)
            ).astype(bf16)
    valid = valid_ref[s]
    wide = []
    for i in range(SUB):
        gap = (base_ref[s] + float(i)) * scale_wide
        row = (jnp.exp2(-(gap * gap)) * valid).astype(bf16)
        rk_ref[it, i] = row
        wide.append(row.astype(f32))
    sub = iota((16, ROWS), 0)
    mixed = jnp.where(
        sub == 0, wide[0], jnp.where(sub == 1, wide[1], jnp.where(sub == 2, wide[2], 0.0))
    )
    rowf_ref[it] = mixed[0:8, :]
    mix_ref[it] = mixed.astype(bf16)


def grid_kernel(
    emb_ref, route_ref, place_ref, scales_ref, w1_hbm, b1_ref, w2_hbm, cot_hbm,
    eg_ref, grads_ref, bout_ref,
    table, rr_ref, pick_ref, near_ref, w1_ref, w2_ref, cot_ref,
    emb_t, expand, base_ref, east_ref, valid_ref, col_ref, rk_ref, mix_ref, rowf_ref, w_ref, acc_ref,
    feat_ref, w1p_ref, w1t_ref, bcol_ref, hid_ref, pg_ref, sg_ref,
    d_out, d_in, table2, landing, g0, g1, g2, in_c, in_y, in_g, full_ref, bc, by, bz, bx,
    loads, ssem, rsem, ssem2, rsem2, vs, vr, vs2, vr2, xs, xr, ds, dr, gs, gr, bs, br, as_, ar,
):
    me = lax.axis_index("band")
    rep = lax.axis_index("rep")
    core = ((me) & (CORES - 1))
    z = (me >> 1) & (ZS - 1)
    y = me >> 4

    def core_peer(d):
        return me + 1 - 2 * core, rep

    def y_peer(d):
        return ((y + d) & (YS - 1)) * (CORES * ZS) + z * CORES + core, rep

    def z_peer(d):
        return y * (CORES * ZS) + ((z + d) & (ZS - 1)) * CORES + core, rep

    def x_peer(d):
        return me, ((rep + d) & (REPS - 1))

    def start(src, dst, send, recv, device):
        copy = pltpu.make_async_remote_copy(
            src_ref=src, dst_ref=dst, send_sem=send, recv_sem=recv, device_id=device, device_id_type=MESH
        )
        copy.start()
        return copy

    def rows_at(index, size):
        return pl.ds(pl.multiple_of(index * size, size), size)

    def bias_round(value, slots, n, mine, peer, base):
        slots[mine] = value
        return [
            start(slots.at[mine], slots.at[mine], bs.at[base + d - 1], br.at[base + d - 1], peer(d))
            for d in range(1, n)
        ]

    def bias_sum(slots, n):
        total = slots[0]
        for k in range(1, n):
            total = total + slots[k]
        return total

    def finish(copies):
        for copy in copies:
            copy.wait()

    def ring_gather(piece, sems, base, peer):
        send, recv = sems
        right, left = peer(1), peer(3)
        one = start(piece(0, 0), piece(0, 0), send.at[base], recv.at[base], right)
        two = start(piece(0, 1), piece(0, 1), send.at[base + 1], recv.at[base + 1], left)
        three = start(piece(0, 1), piece(0, 1), send.at[base + 2], recv.at[base + 2], right)
        four = start(piece(0, 0), piece(0, 0), send.at[base + 3], recv.at[base + 3], left)

        def forward():
            one.wait_recv()
            five = start(piece(3, 0), piece(3, 0), send.at[base + 4], recv.at[base + 4], right)
            two.wait_recv()
            six = start(piece(1, 1), piece(1, 1), send.at[base + 5], recv.at[base + 5], left)

            def rest():
                one.wait_send()
                two.wait_send()
                finish([three, four, five, six])

            return rest

        return forward

    group_at = z * REPS + rep

    def group_peer(j):
        return y * (CORES * ZS) + (j >> 2) * CORES + core, j & 3

    def to_group(src, src_at, dst, dst_at, send, recv):
        def one(d, carry):
            j = ((group_at + d) & (ZS * REPS - 1))
            pltpu.make_async_remote_copy(
                src_ref=src.at[pl.ds(pl.multiple_of(src_at(j), TILE), TILE)],
                dst_ref=dst.at[pl.ds(pl.multiple_of(dst_at, TILE), TILE)],
                send_sem=send, recv_sem=recv, device_id=group_peer(j), device_id_type=MESH,
            ).start()
            return carry

        for d in range(1, ZS * REPS):
            one(d, 0)
        rows = pl.ds(0, (ZS * REPS - 1) * TILE)
        return pltpu.make_async_remote_copy(
            src_ref=src.at[rows], dst_ref=dst.at[rows], send_sem=send, recv_sem=recv,
            device_id=group_peer(((group_at + 1) & (ZS * REPS - 1))), device_id_type=MESH,
        )

    barrier = greet(me, rep)
    held = []
    for k, (src, dst) in enumerate(((w1_hbm, w1_ref), (w2_hbm, w2_ref), (cot_hbm, cot_ref))):
        copy = pltpu.make_async_copy(src, dst, loads.at[k])
        copy.start()
        held.append(copy)

    owner, rank = report_ranks(route_ref)
    within = build_table(emb_ref, place_ref, owner, rank, pick_ref, near_ref, table)
    pl.semaphore_wait(barrier, BANDS - 1 + REPS - 1)
    mine = rr_ref.at[rep]
    send_tiles(me, rep, table, mine, ssem, rsem)
    own = rows_at(me, TILE)
    rr_ref[rep, own, :] = table[own, :]

    finish(held)
    r512 = iota((512, 512), 0)
    c512 = iota((512, 512), 1)
    w1p_ref[...] = dot(one_where(c512 == (r512 & 127) * 4 + (r512 >> 7)), w1_ref[...]).astype(bf16)
    w1t_ref[...] = dot_nt(eye(512), w1p_ref[...]).astype(bf16)
    bcol_ref[...] = jnp.sum(jnp.where(r512 == c512, b1_ref[...], 0.0), axis=1, keepdims=True)

    done = tiles_done(me, rep, table, mine, ssem, rsem)
    done.wait_recv()
    def report_piece(half):
        return lambda k, h: rr_ref.at[((rep + k) & (REPS - 1)), pl.ds(half * 512 + h * 256, 256)]

    forward_first = ring_gather(report_piece(0), (xs, xr), 0, x_peer)
    ident = eye(128)
    group = one_where(
        ((iota((128, 128), 0) >> 4) == (iota((128, 128), 1) >> 4)) & ((iota((128, 128), 0) & 15) == 15)
    )
    turned = dot_nt(ident, rr_ref[rep]).astype(bf16)
    for b in range(8):
        expand[:, b * 128 : (b + 1) * 128] = dot(turned[:, b * 128 : (b + 1) * 128], group)
    decode_places(me, rep, expand, base_ref, east_ref, valid_ref)
    acc_ref[...] = jnp.zeros_like(acc_ref)

    def make(it, carry):
        kernels(it, scales_ref, base_ref, east_ref, valid_ref, col_ref, rk_ref, mix_ref, rowf_ref)
        return carry

    lax.fori_loop(0, 16, make, 0)
    first_half = forward_first()
    forward_second = ring_gather(report_piece(1), (xs, xr), 6, x_peer)

    for half in range(2):
        lanes = slice(half * 512, (half + 1) * 512)
        if half == 0:
            first_half()
            second_half = forward_second()
        else:
            second_half()
        for q in range(REPS):
            turned = dot_nt(ident, rr_ref[q, lanes, :]).astype(bf16)
            for s in range(4):
                emb_t[s, q * PART : (q + 1) * PART, lanes] = turned[s * PART : (s + 1) * PART, :]

        def splat(it, carry):
            s = it >> 2
            level = it & 3
            rows = [rk_ref[it, i, :, lanes] for i in range(SUB)]
            w_ref[SUB * CH : SUB * CH + 16, lanes] = mix_ref[it, :, lanes]
            for c in range(8):
                e = emb_t[s, c * 16 : (c + 1) * 16, lanes]
                for i in range(SUB):
                    w_ref[i * CH + c * 16 : i * CH + (c + 1) * 16, lanes] = e * rows[i]
            acc_ref[level] += dot_nt(w_ref[:, lanes], col_ref[it, :, lanes])
            return carry

        lax.fori_loop(0, 16, splat, 0)
    done.wait_send()

    def inverse(level, i):
        return 1.0 / (acc_ref[level, SUB * CH + i : SUB * CH + i + 1, :] + 1.0)

    for level in range(LEVELS):
        for i in range(SUB):
            feat_ref[level * CH : (level + 1) * CH, i * NLON : (i + 1) * NLON] = (
                acc_ref[level, i * CH : (i + 1) * CH, :] * inverse(level, i)
            ).astype(bf16)

    for i in range(SUB):
        cells = slice(i * NLON, (i + 1) * NLON)
        for h in range(2):
            rows = slice(h * 256, (h + 1) * 256)
            pre = dot(w1t_ref[rows, :], feat_ref[:, cells]) + bcol_ref[rows, :]
            above = dot(w2_ref[rows, :], cot_ref[i])
            square = pre * pre
            tangent = jnp.tanh(root_two_pi * (pre + cubic * square * pre))
            hid_ref[rows, cells] = (0.5 * pre * (1.0 + tangent)).astype(bf16)
            slope = 0.5 * (1.0 + tangent) + 0.5 * pre * (1.0 - tangent * tangent) * root_two_pi * (
                1.0 + 3.0 * cubic * square
            )
            pg_ref[rows, cells] = (above * slope).astype(bf16)

    back = one_where(c512 == (r512 & 3) * 128 + (r512 >> 2))
    for h in range(2):
        rows = slice(h * 256, (h + 1) * 256)
        first = dot(back, dot_nt(feat_ref[...], pg_ref[rows, :]).astype(bf16)).astype(bf16)
        second = dot_nt(hid_ref[:, 0:NLON], cot_ref[0, rows, :])
        for i in range(1, SUB):
            second = second + dot_nt(hid_ref[:, i * NLON : (i + 1) * NLON], cot_ref[i, rows, :])
        second = second.astype(bf16)
        for c in range(2):
            at = (h * 2 + c) * 1024
            g0[at : at + 512, :] = first[:, c * 128 : (c + 1) * 128]
            g0[at + 512 : at + 1024, :] = second[:, c * 128 : (c + 1) * 128]
    bias = dot_nt(jnp.ones((16, CELLS), bf16), pg_ref[...])
    bias_tile = jnp.concatenate(
        [bias[0:1, c * 128 : (c + 1) * 128] for c in range(4)] + [jnp.zeros((4, 128), f32)], axis=0
    )
    c_copies = []
    for d in (1, 2, 3, 0):
        k = ((y + d) & (YS - 1))
        c_copies.append(
            start(g0.at[rows_at((1 - core) * YS + k, 512)], in_c.at[rows_at(k, 512)], gs.at[d], gr.at[d], core_peer(1))
        )
    c_bias = bias_round(bias_tile, bc, CORES, core, core_peer, 0)

    for i in range(SUB):
        grad = dot(w1p_ref[...], pg_ref[:, i * NLON : (i + 1) * NLON])
        for level in range(LEVELS):
            sg_ref[level, i * CH : (i + 1) * CH, :] = (
                grad[level * CH : (level + 1) * CH, :] * inverse(level, i)
            ).astype(bf16)

    def spread(n):
        lanes = slice(n * 256, (n + 1) * 256)

        def one_group(s, carry):
            total = None
            for level in range(LEVELS):
                it = s * 4 + level
                along = dot(sg_ref[level], col_ref[it, :, lanes])
                for i in range(SUB):
                    term = along[i * CH : (i + 1) * CH, :] * rowf_ref[it, i : i + 1, lanes]
                    total = term if total is None else total + term
            for q in range(REPS):
                d_out[n, q, rows_at(s, PART), :] = total[q * PART : (q + 1) * PART, :].astype(bf16)
            return carry

        lax.fori_loop(0, 4, one_group, 0)
        return [
            start(
                d_out.at[n, ((rep + d) & (REPS - 1))], d_in.at[n, d - 1],
                ds.at[n * 3 + d - 1], dr.at[n * 3 + d - 1], x_peer(d),
            )
            for d in range(1, REPS)
        ]

    def to_feeds(n, copies):
        finish(copies)
        total = d_out[n, rep].astype(f32)
        for d in range(REPS - 1):
            total = total + d_in[n, d].astype(f32)
        table2[n * 256 : (n + 1) * 256, :] = jnp.transpose(total).astype(bf16)

        def send(j, carry):
            peer = n * 16 + ((j + me) & 15)

            @pl.when(peer != me)
            def _():
                pltpu.make_async_remote_copy(
                    src_ref=table2.at[rows_at(peer, TILE)],
                    dst_ref=landing.at[rows_at(me, TILE)],
                    send_sem=ssem2,
                    recv_sem=rsem2,
                    device_id=(peer, rep),
                    device_id_type=MESH,
                ).start()

            return carry

        lax.fori_loop(0, 4, lambda g, c: [send(g * 4 + k, c) for k in range(4)][0], 0)

    y_copies = []
    for d, copy in zip((1, 2, 3, 0), c_copies):
        k = ((y + d) & (YS - 1))
        copy.wait()
        g1[rows_at(k, 512), :] = (
            g0[rows_at(core * YS + k, 512), :].astype(f32) + in_c[rows_at(k, 512), :].astype(f32)
        ).astype(bf16)
        if d:
            y_copies.append(start(g1.at[rows_at(k, 512)], in_y.at[d - 1], gs.at[3 + d], gr.at[3 + d], y_peer(d)))
    finish(c_bias)
    y_bias = bias_round(bias_sum(bc, CORES), by, YS, y, y_peer, 1)
    d0 = spread(0)
    d1 = spread(1)
    d2 = spread(2)
    finish(y_copies)
    total = g1[rows_at(y, 512), :].astype(f32)
    for d in range(YS - 1):
        total = total + in_y[d].astype(f32)
    g2[...] = total.astype(bf16)
    own_tile = rows_at(group_at, TILE)
    in_g[own_tile, :] = g2[own_tile, :]
    scattered = to_group(g2, lambda j: j * TILE, in_g, group_at * TILE, vs, vr)
    finish(y_bias)
    z_bias = bias_round(bias_sum(by, YS), bz, ZS, z, z_peer, 4)
    to_feeds(0, d0)
    d3 = spread(3)
    scattered.wait()
    total = in_g[0:TILE, :].astype(f32)
    for j in range(1, ZS * REPS):
        total = total + in_g[j * TILE : (j + 1) * TILE, :].astype(f32)
    block_at = core * 2048 + y * 512
    full_ref[pl.ds(pl.multiple_of(block_at + group_at * TILE, TILE), TILE), :] = total.astype(bf16)
    gathered = to_group(
        full_ref, lambda j: block_at + group_at * TILE, full_ref, block_at + group_at * TILE, vs2, vr2
    )
    to_feeds(1, d1)
    finish(z_bias)
    x_bias = bias_round(bias_sum(bz, ZS), bx, REPS, rep, x_peer, 11)
    to_feeds(2, d2)
    gathered.wait()

    def block(k):
        return full_ref.at[rows_at(core * YS + k, 512)]

    def to_core(d):
        k = ((y + YS - d) & (YS - 1))
        return start(block(k), block(k), as_.at[3 + d], ar.at[3 + d], core_peer(1))

    blocks = [start(block(y), block(y), as_.at[d - 1], ar.at[d - 1], y_peer(d)) for d in range(1, YS)]
    crossing = [to_core(0)]
    to_feeds(3, d3)
    landing[own, :] = table2[own, :]
    finish(x_bias)
    bias_total = bias_sum(bx, REPS)
    for c in range(4):
        bout_ref[:, c * 128 : (c + 1) * 128] = bias_total[c : c + 1, :]
    for d in (1, 3, 2):
        blocks[d - 1].wait()
        crossing.append(to_core(d))
    tiles_done(me, rep, table2, landing, ssem2, rsem2).wait()
    turned = dot_nt(ident, landing[...]).astype(bf16)
    found = dot(turned, pick_ref[...])
    gradient = jnp.zeros((PART, REPORTS), f32)
    for s in range(4):
        gradient = gradient + jnp.where(within == float(s), found[s * PART : (s + 1) * PART, :], 0.0)
    eg_ref[...] = gradient
    finish(crossing)
    for c in range(4):
        grads_ref[:, c * 128 : (c + 1) * 128] = full_ref[c * 1024 : (c + 1) * 1024, :]


def sds(shape, dtype):
    return jax.ShapeDtypeStruct(shape, dtype)


def on_device(
    embeddings, route, place, scales, first_weight, first_bias, second_weight, out_cotangent
):
    dma = pltpu.SemaphoreType.DMA
    vm = pltpu.VMEM
    in_vmem = pl.BlockSpec(memory_space=pltpu.VMEM)
    anywhere = pl.BlockSpec(memory_space=pl.ANY)
    gradient, grads, bias = pl.pallas_call(
        grid_kernel,
        out_shape=[sds((PART, REPORTS), f32), sds((1024, 512), bf16), sds((1, HID), f32)],
        in_specs=[
            in_vmem, in_vmem, in_vmem, pl.BlockSpec(memory_space=pltpu.SMEM),
            anywhere, in_vmem, anywhere, anywhere,
        ],
        out_specs=[in_vmem] * 3,
        scratch_shapes=[
            vm((ROWS, 128), bf16), vm((REPS, ROWS, 128), bf16), vm((ROWS, REPORTS), bf16), vm((ROWS, REPORTS), bf16),
            vm((512, HID), bf16), vm((HID, 512), bf16), vm((SUB, 512, NLON), bf16),
            vm((4, CH, ROWS), bf16), vm((128, ROWS), f32),
            vm((4, 16, ROWS), f32), vm((4, 8, ROWS), f32), vm((4, 16, ROWS), f32),
            vm((16, NLON, ROWS), bf16), vm((16, SUB, 16, ROWS), bf16), vm((16, 16, ROWS), bf16),
            vm((16, 8, ROWS), f32), vm((SUB * CH + 16, ROWS), bf16),
            vm((LEVELS, SUB * CH + 16, NLON), f32),
            vm((512, CELLS), bf16), vm((512, HID), bf16), vm((HID, 512), bf16), vm((HID, 1), f32),
            vm((HID, CELLS), bf16), vm((HID, CELLS), bf16), vm((LEVELS, SUB * CH, NLON), bf16),
            vm((4, REPS, 128, 256), bf16), vm((4, REPS - 1, 128, 256), bf16),
            vm((ROWS, 128), bf16), vm((ROWS, 128), bf16),
            vm((GROWS, 128), bf16), vm((2048, 128), bf16), vm((512, 128), bf16),
            vm((2048, 128), bf16), vm((3, 512, 128), bf16), vm((512, 128), bf16),
            vm((GROWS, 128), bf16),
            vm((CORES, 8, 128), f32), vm((YS, 8, 128), f32), vm((ZS, 8, 128), f32), vm((REPS, 8, 128), f32),
            dma((3,)), dma, dma, dma, dma, dma, dma, dma, dma,
            dma((12,)), dma((12,)), dma((12,)), dma((12,)),
            dma((7,)), dma((7,)), dma((14,)), dma((14,)), dma((7,)), dma((7,)),
        ],
        compiler_params=pltpu.CompilerParams(
            collective_id=0, has_side_effects=True, vmem_limit_bytes=60 << 20
        ),
    )(
        embeddings, route.reshape(1, REPORTS), place, scales,
        first_weight, first_bias.reshape(1, HID), second_weight, out_cotangent.transpose(1, 0, 2),
    )
    return (gradient, grads[0:512].astype(f32), bias.reshape(HID), grads[512:1024].astype(f32))


def solution(mesh):
    return jax.shard_map(
        on_device,
        mesh=mesh,
        in_specs=(
            P("rep", "band"),
            P("band", None),
            P(None, "band"),
            P(),
            P(),
            P(),
            P(),
            P(None, ("band", "rep"), None),
        ),
        out_specs=(P("rep", "band"), P(), P(), P()),
        check_vma=False,
    )
```

```python
import jax
import jax.numpy as jnp
from jax import lax
from jax.experimental import pallas as pl
from jax.experimental.pallas import tpu as pltpu
from jax.sharding import PartitionSpec as P

MESH = pl.DeviceIdType.MESH
bf16 = jnp.bfloat16
f32 = jnp.float32

root_two_pi = 0.7978845608028654
cubic = 0.044715
half_log2e = 0.8493218002880191

BANDS = 64
REPS = 4
YS, ZS, CORES = 4, 8, 2
CAP = 20
TILE = 16
ROWS = BANDS * TILE
REPORTS = 512
LEVELS = 4
CH = 128
PART = 32
SUB = 3
NLON = 256
LAT = 12.0
CELLS = SUB * NLON
HID = 512
GROWS = 4096


def hops(k, n):
    return min(k % n, n - k % n)


BANDS_FAR_FIRST = sorted(range(1, BANDS), key=lambda d: -hops(d >> 4, YS) - hops(d >> 1, ZS))
GROUP_FAR_FIRST = sorted(range(1, ZS * REPS), key=lambda d: -hops(d >> 2, ZS) - hops(d, REPS))


def iota(shape, dim):
    return lax.broadcasted_iota(jnp.int32, shape, dim)


def one_where(cond):
    return jnp.where(cond, 1.0, 0.0).astype(bf16)


def dot(a, b):
    return lax.dot_general(a, b, (((1,), (0,)), ((), ())), preferred_element_type=f32)


def dot_nt(a, b):
    return lax.dot_general(a, b, (((1,), (1,)), ((), ())), preferred_element_type=f32)


def eye(n):
    return one_where(iota((n, n), 0) == iota((n, n), 1))


def row_keys(start, rows):
    row = iota((rows, 1), 0) + start
    band = row >> 4
    ok = row & 15
    key = jnp.where(ok == 15, -1000, (band - 1) * 5 + ok).astype(f32)
    place_band = jnp.where(ok == 15, band, -1000).astype(f32)
    return key, place_band


def report_ranks(route_ref):
    owner = route_ref[...].astype(f32)
    rank = jnp.zeros((1, REPORTS), f32)
    for part in range(4):
        mine = iota((128, REPORTS), 0) + part * 128
        lane = iota((128, REPORTS), 1)
        col = jnp.sum(jnp.where(mine == lane, owner, 0.0), axis=1, keepdims=True)
        rank = rank + jnp.sum(
            jnp.where((col == owner) & (mine < lane), 1.0, 0.0), axis=0, keepdims=True
        )
    return owner, rank


def greet(me, rep):
    barrier = pltpu.get_barrier_semaphore()

    def band_peer(d, carry):
        pl.semaphore_signal(
            barrier, inc=1, device_id=(((me + d) & (BANDS - 1)), rep), device_id_type=MESH
        )
        return carry

    lax.fori_loop(0, 9, lambda g, c: [band_peer(g * 7 + k, c) for k in range(1, 8)][0], 0)
    for d in range(1, REPS):
        pl.semaphore_signal(
            barrier, inc=1, device_id=(me, ((rep + d) & (REPS - 1))), device_id_type=MESH
        )
    return barrier


def send_tiles(me, rep, table, landing, send_sem, recv_sem):
    def send(d, carry):
        peer = ((me + d) & (BANDS - 1))
        pltpu.make_async_remote_copy(
            src_ref=table.at[pl.ds(pl.multiple_of(peer * TILE, TILE), TILE)],
            dst_ref=landing.at[pl.ds(pl.multiple_of(me * TILE, TILE), TILE)],
            send_sem=send_sem,
            recv_sem=recv_sem,
            device_id=(peer, rep),
            device_id_type=MESH,
        ).start()
        return carry

    for d in BANDS_FAR_FIRST:
        send(d, 0)


def tiles_done(me, rep, table, landing, send_sem, recv_sem):
    return pltpu.make_async_remote_copy(
        src_ref=table.at[pl.ds(0, ROWS - TILE)],
        dst_ref=landing.at[pl.ds(0, ROWS - TILE)],
        send_sem=send_sem,
        recv_sem=recv_sem,
        device_id=(((me + 1) & (BANDS - 1)), rep),
        device_id_type=MESH,
    )


def decode_places(t, rep, expand, base_ref, east_ref, valid_ref):
    lane = iota((1, ROWS), 1)
    ok = lane & 15
    o = (ok >= 5).astype(jnp.int32) + (ok >= 10).astype(jnp.int32) + (ok >= 15).astype(jnp.int32)
    k4 = (ok - 5 * o) * 4
    v = lax.rem(t + 2, 3) + o
    third = jnp.where(v >= 3, v - 3, v)
    code = third * 20 + k4
    lam = iota((64, ROWS), 0)
    low = expand[0:64, :]
    high = expand[64:128, :]
    count = jnp.sum(jnp.where(lam == third + 60, low, 0.0), axis=0, keepdims=True)
    offset = (1 - o).astype(f32) * LAT + (rep * SUB).astype(f32) + 0.5
    for s in range(4):
        hit = lam == code + s
        north = jnp.sum(jnp.where(hit, low, 0.0), axis=0, keepdims=True)
        east = jnp.sum(jnp.where(hit, high, 0.0), axis=0, keepdims=True)
        valid = jnp.where((ok < 15) & ((k4 + s).astype(f32) < count), 1.0, 0.0)
        base_ref[s] = jnp.broadcast_to(offset - north * LAT, (16, ROWS))
        valid_ref[s] = jnp.broadcast_to(valid, (16, ROWS))
        east_ref[s] = jnp.broadcast_to(east * float(NLON), (8, ROWS))


def build_table(emb_ref, place_ref, owner, rank, pick_ref, table):
    quad = jnp.floor(rank * 0.25)
    within = rank - 4.0 * quad
    key = owner * 5.0 + quad
    third = owner - 3.0 * jnp.floor((owner + 0.5) * (1.0 / 3.0))
    emb = emb_ref[...].astype(f32)
    emb_b = jnp.concatenate(
        [jnp.where(within == float(s), emb, 0.0) for s in range(4)], axis=0
    ).astype(bf16)
    lam = iota((128, REPORTS), 0).astype(f32)
    spot = third * 20.0 + rank
    north = place_ref[0:1, :].astype(f32)
    east = place_ref[1:2, :].astype(f32)
    place_b = (
        jnp.where(lam == spot, north, 0.0)
        + jnp.where(lam == spot + 64.0, east, 0.0)
        + jnp.where(lam == third + 60.0, 1.0, 0.0)
    ).astype(bf16)
    for part in range(8):
        rows = slice(part * 128, (part + 1) * 128)
        row_key, place_band = row_keys(part * 128, 128)
        pick = one_where(row_key == key)
        pick_ref[rows, :] = pick
        near = one_where(jnp.abs(place_band - owner) <= 1.0)
        table[rows, :] = (dot_nt(pick, emb_b) + dot_nt(near, place_b)).astype(bf16)
    return within


def kernels(it, scales_ref, base_ref, east_ref, valid_ref, col_ref, rk_ref, mix_ref, rowf_ref):
    s = it >> 2
    reach = scales_ref[it & 3] * LAT
    scale = half_log2e / jnp.full((1, 128), reach, f32)
    scale_wide = jnp.concatenate([scale] * 8, axis=1)
    east = east_ref[s, 0:1, :] * scale_wide
    for c in range(8):
        centre = (iota((32, 128), 0).astype(f32) + (c * 32 + 0.5)) * scale
        for b in range(8):
            gap = centre - east[:, b * 128 : (b + 1) * 128]
            col_ref[it, c * 32 : (c + 1) * 32, b * 128 : (b + 1) * 128] = jnp.exp2(
                -(gap * gap)
            ).astype(bf16)
    valid = valid_ref[s]
    wide = []
    for i in range(SUB):
        gap = (base_ref[s] + float(i)) * scale_wide
        row = (jnp.exp2(-(gap * gap)) * valid).astype(bf16)
        rk_ref[it, i] = row
        wide.append(row.astype(f32))
    sub = iota((16, ROWS), 0)
    mixed = jnp.where(
        sub == 0, wide[0], jnp.where(sub == 1, wide[1], jnp.where(sub == 2, wide[2], 0.0))
    )
    rowf_ref[it] = mixed[0:8, :]
    mix_ref[it] = mixed.astype(bf16)


def grid_kernel(
    emb_ref, route_ref, place_ref, scales_ref, w1_hbm, b1_ref, w2_hbm, cot_hbm,
    eg_ref, grads_ref, bout_ref,
    table, rr_ref, pick_ref, w1_ref, w2_ref, cot_ref,
    emb_t, expand, base_ref, east_ref, valid_ref, col_ref, rk_ref, mix_ref, rowf_ref, w_ref, acc_ref,
    feat_ref, w1p_ref, w1t_ref, bcol_ref, hid_ref, pg_ref, sg_ref,
    d_out, d_in, table2, landing, g0, g1, g2, in_c, in_y, in_g, full_ref, bc, by, bz, bx,
    loads, ssem, rsem, ssem2, rsem2, vs, vr, vs2, vr2, xs, xr, ds, dr, gs, gr, bs, br, as_, ar,
):
    me = lax.axis_index("band")
    rep = lax.axis_index("rep")
    core = ((me) & (CORES - 1))
    z = (me >> 1) & (ZS - 1)
    y = me >> 4

    def core_peer(d):
        return me + 1 - 2 * core, rep

    def y_peer(d):
        return ((y + d) & (YS - 1)) * (CORES * ZS) + z * CORES + core, rep

    def z_peer(d):
        return y * (CORES * ZS) + ((z + d) & (ZS - 1)) * CORES + core, rep

    def x_peer(d):
        return me, ((rep + d) & (REPS - 1))

    def start(src, dst, send, recv, device):
        copy = pltpu.make_async_remote_copy(
            src_ref=src, dst_ref=dst, send_sem=send, recv_sem=recv, device_id=device, device_id_type=MESH
        )
        copy.start()
        return copy

    def rows_at(index, size):
        return pl.ds(pl.multiple_of(index * size, size), size)

    def bias_round(value, slots, n, mine, peer, base):
        slots[mine] = value
        return [
            start(slots.at[mine], slots.at[mine], bs.at[base + d - 1], br.at[base + d - 1], peer(d))
            for d in range(1, n)
        ]

    def bias_sum(slots, n):
        total = slots[0]
        for k in range(1, n):
            total = total + slots[k]
        return total

    def finish(copies):
        for copy in copies:
            copy.wait()

    def ring_gather(piece, sems, base, peer):
        send, recv = sems
        right, left = peer(1), peer(3)
        one = start(piece(0, 0), piece(0, 0), send.at[base], recv.at[base], right)
        two = start(piece(0, 1), piece(0, 1), send.at[base + 1], recv.at[base + 1], left)
        three = start(piece(0, 1), piece(0, 1), send.at[base + 2], recv.at[base + 2], right)
        four = start(piece(0, 0), piece(0, 0), send.at[base + 3], recv.at[base + 3], left)

        def forward():
            one.wait_recv()
            five = start(piece(3, 0), piece(3, 0), send.at[base + 4], recv.at[base + 4], right)
            two.wait_recv()
            six = start(piece(1, 1), piece(1, 1), send.at[base + 5], recv.at[base + 5], left)

            def rest():
                one.wait_send()
                two.wait_send()
                finish([three, four, five, six])

            return rest

        return forward

    group_at = z * REPS + rep

    def group_peer(j):
        return y * (CORES * ZS) + (j >> 2) * CORES + core, j & 3

    def to_group(src, src_at, dst, dst_at, send, recv):
        def one(d, carry):
            j = ((group_at + d) & (ZS * REPS - 1))
            pltpu.make_async_remote_copy(
                src_ref=src.at[pl.ds(pl.multiple_of(src_at(j), TILE), TILE)],
                dst_ref=dst.at[pl.ds(pl.multiple_of(dst_at, TILE), TILE)],
                send_sem=send, recv_sem=recv, device_id=group_peer(j), device_id_type=MESH,
            ).start()
            return carry

        for d in GROUP_FAR_FIRST:
            one(d, 0)
        rows = pl.ds(0, (ZS * REPS - 1) * TILE)
        return pltpu.make_async_remote_copy(
            src_ref=src.at[rows], dst_ref=dst.at[rows], send_sem=send, recv_sem=recv,
            device_id=group_peer(((group_at + 1) & (ZS * REPS - 1))), device_id_type=MESH,
        )

    barrier = greet(me, rep)
    held = []
    for k, (src, dst) in enumerate(((w1_hbm, w1_ref), (w2_hbm, w2_ref), (cot_hbm, cot_ref))):
        copy = pltpu.make_async_copy(src, dst, loads.at[k])
        copy.start()
        held.append(copy)

    owner, rank = report_ranks(route_ref)
    within = build_table(emb_ref, place_ref, owner, rank, pick_ref, table)
    pl.semaphore_wait(barrier, BANDS - 1 + REPS - 1)
    mine = rr_ref.at[rep]
    send_tiles(me, rep, table, mine, ssem, rsem)
    own = rows_at(me, TILE)
    rr_ref[rep, own, :] = table[own, :]

    finish(held)
    r512 = iota((512, 512), 0)
    c512 = iota((512, 512), 1)
    w1p_ref[...] = dot(one_where(c512 == (r512 & 127) * 4 + (r512 >> 7)), w1_ref[...]).astype(bf16)
    w1t_ref[...] = dot_nt(eye(512), w1p_ref[...]).astype(bf16)
    bcol_ref[...] = jnp.sum(jnp.where(r512 == c512, b1_ref[...], 0.0), axis=1, keepdims=True)

    done = tiles_done(me, rep, table, mine, ssem, rsem)
    done.wait_recv()
    def report_piece(half):
        return lambda k, h: rr_ref.at[((rep + k) & (REPS - 1)), pl.ds(half * 512 + h * 256, 256)]

    forward_first = ring_gather(report_piece(0), (xs, xr), 0, x_peer)
    ident = eye(128)
    group = one_where(
        ((iota((128, 128), 0) >> 4) == (iota((128, 128), 1) >> 4)) & ((iota((128, 128), 0) & 15) == 15)
    )
    turned = dot_nt(ident, rr_ref[rep]).astype(bf16)
    for b in range(8):
        expand[:, b * 128 : (b + 1) * 128] = dot(turned[:, b * 128 : (b + 1) * 128], group)
    decode_places(me, rep, expand, base_ref, east_ref, valid_ref)
    acc_ref[...] = jnp.zeros_like(acc_ref)

    def make(it, carry):
        kernels(it, scales_ref, base_ref, east_ref, valid_ref, col_ref, rk_ref, mix_ref, rowf_ref)
        return carry

    lax.fori_loop(0, 16, make, 0)
    first_half = forward_first()
    forward_second = ring_gather(report_piece(1), (xs, xr), 6, x_peer)

    for half in range(2):
        lanes = slice(half * 512, (half + 1) * 512)
        if half == 0:
            first_half()
            second_half = forward_second()
        else:
            second_half()
        for q in range(REPS):
            turned = dot_nt(ident, rr_ref[q, lanes, :]).astype(bf16)
            for s in range(4):
                emb_t[s, q * PART : (q + 1) * PART, lanes] = turned[s * PART : (s + 1) * PART, :]

        def splat(it, carry):
            s = it >> 2
            level = it & 3
            rows = [rk_ref[it, i, :, lanes] for i in range(SUB)]
            w_ref[SUB * CH : SUB * CH + 16, lanes] = mix_ref[it, :, lanes]
            for c in range(8):
                e = emb_t[s, c * 16 : (c + 1) * 16, lanes]
                for i in range(SUB):
                    w_ref[i * CH + c * 16 : i * CH + (c + 1) * 16, lanes] = e * rows[i]
            acc_ref[level] += dot_nt(w_ref[:, lanes], col_ref[it, :, lanes])
            return carry

        lax.fori_loop(0, 16, splat, 0)
    done.wait_send()

    def inverse(level, i):
        return 1.0 / (acc_ref[level, SUB * CH + i : SUB * CH + i + 1, :] + 1.0)

    for level in range(LEVELS):
        for i in range(SUB):
            feat_ref[level * CH : (level + 1) * CH, i * NLON : (i + 1) * NLON] = (
                acc_ref[level, i * CH : (i + 1) * CH, :] * inverse(level, i)
            ).astype(bf16)

    for i in range(SUB):
        cells = slice(i * NLON, (i + 1) * NLON)
        for h in range(2):
            rows = slice(h * 256, (h + 1) * 256)
            pre = dot(w1t_ref[rows, :], feat_ref[:, cells]) + bcol_ref[rows, :]
            above = dot(w2_ref[rows, :], cot_ref[i])
            square = pre * pre
            tangent = jnp.tanh(root_two_pi * (pre + cubic * square * pre))
            hid_ref[rows, cells] = (0.5 * pre * (1.0 + tangent)).astype(bf16)
            slope = 0.5 * (1.0 + tangent) + 0.5 * pre * (1.0 - tangent * tangent) * root_two_pi * (
                1.0 + 3.0 * cubic * square
            )
            pg_ref[rows, cells] = (above * slope).astype(bf16)

    back = one_where(c512 == (r512 & 3) * 128 + (r512 >> 2))
    for h in range(2):
        rows = slice(h * 256, (h + 1) * 256)
        first = dot(back, dot_nt(feat_ref[...], pg_ref[rows, :]).astype(bf16)).astype(bf16)
        second = dot_nt(hid_ref[:, 0:NLON], cot_ref[0, rows, :])
        for i in range(1, SUB):
            second = second + dot_nt(hid_ref[:, i * NLON : (i + 1) * NLON], cot_ref[i, rows, :])
        second = second.astype(bf16)
        for c in range(2):
            at = (h * 2 + c) * 1024
            g0[at : at + 512, :] = first[:, c * 128 : (c + 1) * 128]
            g0[at + 512 : at + 1024, :] = second[:, c * 128 : (c + 1) * 128]
    bias = dot_nt(jnp.ones((16, CELLS), bf16), pg_ref[...])
    bias_tile = jnp.concatenate(
        [bias[0:1, c * 128 : (c + 1) * 128] for c in range(4)] + [jnp.zeros((4, 128), f32)], axis=0
    )
    c_copies = []
    for d in (1, 2, 3, 0):
        k = ((y + d) & (YS - 1))
        c_copies.append(
            start(g0.at[rows_at((1 - core) * YS + k, 512)], in_c.at[rows_at(k, 512)], gs.at[d], gr.at[d], core_peer(1))
        )
    c_bias = bias_round(bias_tile, bc, CORES, core, core_peer, 0)

    for i in range(SUB):
        grad = dot(w1p_ref[...], pg_ref[:, i * NLON : (i + 1) * NLON])
        for level in range(LEVELS):
            sg_ref[level, i * CH : (i + 1) * CH, :] = (
                grad[level * CH : (level + 1) * CH, :] * inverse(level, i)
            ).astype(bf16)

    def spread(n):
        lanes = slice(n * 256, (n + 1) * 256)

        def one_group(s, carry):
            total = None
            for level in range(LEVELS):
                it = s * 4 + level
                along = dot(sg_ref[level], col_ref[it, :, lanes])
                for i in range(SUB):
                    term = along[i * CH : (i + 1) * CH, :] * rowf_ref[it, i : i + 1, lanes]
                    total = term if total is None else total + term
            for q in range(REPS):
                d_out[n, q, rows_at(s, PART), :] = total[q * PART : (q + 1) * PART, :].astype(bf16)
            return carry

        lax.fori_loop(0, 4, one_group, 0)
        return [
            start(
                d_out.at[n, ((rep + d) & (REPS - 1))], d_in.at[n, d - 1],
                ds.at[n * 3 + d - 1], dr.at[n * 3 + d - 1], x_peer(d),
            )
            for d in range(1, REPS)
        ]

    def to_feeds(n, copies):
        finish(copies)
        total = d_out[n, rep].astype(f32)
        for d in range(REPS - 1):
            total = total + d_in[n, d].astype(f32)
        table2[n * 256 : (n + 1) * 256, :] = jnp.transpose(total).astype(bf16)

        def send(j, carry):
            peer = n * 16 + ((j + me) & 15)

            @pl.when(peer != me)
            def _():
                pltpu.make_async_remote_copy(
                    src_ref=table2.at[rows_at(peer, TILE)],
                    dst_ref=landing.at[rows_at(me, TILE)],
                    send_sem=ssem2,
                    recv_sem=rsem2,
                    device_id=(peer, rep),
                    device_id_type=MESH,
                ).start()

            return carry

        lax.fori_loop(0, 4, lambda g, c: [send(g * 4 + k, c) for k in range(4)][0], 0)

    y_copies = []
    for d, copy in zip((1, 2, 3, 0), c_copies):
        k = ((y + d) & (YS - 1))
        copy.wait()
        g1[rows_at(k, 512), :] = (
            g0[rows_at(core * YS + k, 512), :].astype(f32) + in_c[rows_at(k, 512), :].astype(f32)
        ).astype(bf16)
        if d:
            y_copies.append(start(g1.at[rows_at(k, 512)], in_y.at[d - 1], gs.at[3 + d], gr.at[3 + d], y_peer(d)))
    finish(c_bias)
    y_bias = bias_round(bias_sum(bc, CORES), by, YS, y, y_peer, 1)
    d0 = spread(0)
    d1 = spread(1)
    d2 = spread(2)
    finish(y_copies)
    total = g1[rows_at(y, 512), :].astype(f32)
    for d in range(YS - 1):
        total = total + in_y[d].astype(f32)
    g2[...] = total.astype(bf16)
    own_tile = rows_at(group_at, TILE)
    in_g[own_tile, :] = g2[own_tile, :]
    scattered = to_group(g2, lambda j: j * TILE, in_g, group_at * TILE, vs, vr)
    finish(y_bias)
    z_bias = bias_round(bias_sum(by, YS), bz, ZS, z, z_peer, 4)
    to_feeds(0, d0)
    d3 = spread(3)
    scattered.wait()
    total = in_g[0:TILE, :].astype(f32)
    for j in range(1, ZS * REPS):
        total = total + in_g[j * TILE : (j + 1) * TILE, :].astype(f32)
    block_at = core * 2048 + y * 512
    full_ref[pl.ds(pl.multiple_of(block_at + group_at * TILE, TILE), TILE), :] = total.astype(bf16)
    gathered = to_group(
        full_ref, lambda j: block_at + group_at * TILE, full_ref, block_at + group_at * TILE, vs2, vr2
    )
    to_feeds(1, d1)
    finish(z_bias)
    x_bias = bias_round(bias_sum(bz, ZS), bx, REPS, rep, x_peer, 11)
    to_feeds(2, d2)
    gathered.wait()

    def block(k):
        return full_ref.at[rows_at(core * YS + k, 512)]

    def to_core(d):
        k = ((y + YS - d) & (YS - 1))
        return start(block(k), block(k), as_.at[3 + d], ar.at[3 + d], core_peer(1))

    blocks = [start(block(y), block(y), as_.at[d - 1], ar.at[d - 1], y_peer(d)) for d in range(1, YS)]
    crossing = [to_core(0)]
    to_feeds(3, d3)
    landing[own, :] = table2[own, :]
    finish(x_bias)
    bias_total = bias_sum(bx, REPS)
    for c in range(4):
        bout_ref[:, c * 128 : (c + 1) * 128] = bias_total[c : c + 1, :]
    for d in (1, 3, 2):
        blocks[d - 1].wait()
        crossing.append(to_core(d))
    tiles_done(me, rep, table2, landing, ssem2, rsem2).wait()
    turned = dot_nt(ident, landing[...]).astype(bf16)
    found = dot(turned, pick_ref[...])
    gradient = jnp.zeros((PART, REPORTS), f32)
    for s in range(4):
        gradient = gradient + jnp.where(within == float(s), found[s * PART : (s + 1) * PART, :], 0.0)
    eg_ref[...] = gradient
    finish(crossing)
    for c in range(4):
        grads_ref[:, c * 128 : (c + 1) * 128] = full_ref[c * 1024 : (c + 1) * 1024, :]


def sds(shape, dtype):
    return jax.ShapeDtypeStruct(shape, dtype)


def on_device(
    embeddings, route, place, scales, first_weight, first_bias, second_weight, out_cotangent
):
    dma = pltpu.SemaphoreType.DMA
    vm = pltpu.VMEM
    in_vmem = pl.BlockSpec(memory_space=pltpu.VMEM)
    anywhere = pl.BlockSpec(memory_space=pl.ANY)
    gradient, grads, bias = pl.pallas_call(
        grid_kernel,
        out_shape=[sds((PART, REPORTS), f32), sds((1024, 512), bf16), sds((1, HID), f32)],
        in_specs=[
            in_vmem, in_vmem, in_vmem, pl.BlockSpec(memory_space=pltpu.SMEM),
            anywhere, in_vmem, anywhere, anywhere,
        ],
        out_specs=[in_vmem] * 3,
        scratch_shapes=[
            vm((ROWS, 128), bf16), vm((REPS, ROWS, 128), bf16), vm((ROWS, REPORTS), bf16),
            vm((512, HID), bf16), vm((HID, 512), bf16), vm((SUB, 512, NLON), bf16),
            vm((4, CH, ROWS), bf16), vm((128, ROWS), f32),
            vm((4, 16, ROWS), f32), vm((4, 8, ROWS), f32), vm((4, 16, ROWS), f32),
            vm((16, NLON, ROWS), bf16), vm((16, SUB, 16, ROWS), bf16), vm((16, 16, ROWS), bf16),
            vm((16, 8, ROWS), f32), vm((SUB * CH + 16, ROWS), bf16),
            vm((LEVELS, SUB * CH + 16, NLON), f32),
            vm((512, CELLS), bf16), vm((512, HID), bf16), vm((HID, 512), bf16), vm((HID, 1), f32),
            vm((HID, CELLS), bf16), vm((HID, CELLS), bf16), vm((LEVELS, SUB * CH, NLON), bf16),
            vm((4, REPS, 128, 256), bf16), vm((4, REPS - 1, 128, 256), bf16),
            vm((ROWS, 128), bf16), vm((ROWS, 128), bf16),
            vm((GROWS, 128), bf16), vm((2048, 128), bf16), vm((512, 128), bf16),
            vm((2048, 128), bf16), vm((3, 512, 128), bf16), vm((512, 128), bf16),
            vm((GROWS, 128), bf16),
            vm((CORES, 8, 128), f32), vm((YS, 8, 128), f32), vm((ZS, 8, 128), f32), vm((REPS, 8, 128), f32),
            dma((3,)), dma, dma, dma, dma, dma, dma, dma, dma,
            dma((12,)), dma((12,)), dma((12,)), dma((12,)),
            dma((7,)), dma((7,)), dma((14,)), dma((14,)), dma((7,)), dma((7,)),
        ],
        compiler_params=pltpu.CompilerParams(
            collective_id=0, has_side_effects=True, vmem_limit_bytes=60 << 20
        ),
    )(
        embeddings, route.reshape(1, REPORTS), place, scales,
        first_weight, first_bias.reshape(1, HID), second_weight, out_cotangent.transpose(1, 0, 2),
    )
    return (gradient, grads[0:512].astype(f32), bias.reshape(HID), grads[512:1024].astype(f32))


def solution(mesh):
    return jax.shard_map(
        on_device,
        mesh=mesh,
        in_specs=(
            P("rep", "band"),
            P("band", None),
            P(None, "band"),
            P(),
            P(),
            P(),
            P(),
            P(None, ("band", "rep"), None),
        ),
        out_specs=(P("rep", "band"), P(), P(), P()),
        check_vma=False,
    )
```
